32 devices in a mesh: dp: 16 (over z, y, core), tensor: 2 (over x).
Axes of the slice: x: 2, y: 2, z: 4, core: 2. Of those that a mesh axis runs over, the one named last changes fastest.
Arguments:
- tokens: bfloat16 [16384, 1024], P(('dp', 'tensor')), may hold values from -6 to 6
- cotangent: bfloat16 [16384, 1024], P(('dp', 'tensor')), may hold values from -6 to 6
- positions: int32 [16384], P('dp'), may hold values from 0 to 1023, as said below
- qkv_weight: float32 [1024, 3072], P('dp', 'tensor'), may hold values from -0.25 to 0.25
- dense_weight: float32 [1024, 1024], P('dp', 'tensor'), may hold values from -0.375 to 0.375
- fc1_weight: float32 [1024, 4096], P('dp', 'tensor'), may hold values from -0.1875 to 0.1875
- fc2_weight: float32 [1024, 4096], P('dp', 'tensor'), may hold values from -0.125 to 0.125
- vectors: float32 [11264], P('dp'), may hold values from -1.8 to 1.8, as said below
- mom_qkv: float32 [1024, 3072], P('dp', 'tensor'), as said below
- mom_dense: float32 [1024, 1024], P('dp', 'tensor'), as said below
- mom_fc1: float32 [1024, 4096], P('dp', 'tensor'), as said below
- mom_fc2: float32 [1024, 4096], P('dp', 'tensor'), as said below
- first_moment: float32 [11264], P(('dp', 'tensor')), as said below
- second_moment: float32 [11264], P(('dp', 'tensor')), as said below
Outputs:
- output: bfloat16 [16384, 1024], P(('dp', 'tensor'))
- grad_tokens: float32 [16384, 1024], P(('dp', 'tensor'))
- new_mom_qkv: float32 [1024, 3072], P('dp', 'tensor')
- new_qkv: float32 [1024, 3072], P('dp', 'tensor')
- new_mom_dense: float32 [1024, 1024], P('dp', 'tensor')
- new_dense: float32 [1024, 1024], P('dp', 'tensor')
- new_mom_fc1: float32 [1024, 4096], P('dp', 'tensor')
- new_fc1: float32 [1024, 4096], P('dp', 'tensor')
- new_mom_fc2: float32 [1024, 4096], P('dp', 'tensor')
- new_fc2: float32 [1024, 4096], P('dp', 'tensor')
- new_first: float32 [11264], P(('dp', 'tensor'))
- new_second: float32 [11264], P(('dp', 'tensor'))
- new_vectors: float32 [11264], P(('dp', 'tensor'))
The draws below stay inside these ranges and needn't reach their ends.
Inputs may be any that keep to these rules, and one draw needn't show every extreme that they name: Each index of dp holds one sequence of 1024 positions made of three documents one after another, the first and the last possibly empty; a position counts the tokens before it in its own document; one document of every sequence covers the positions 256 to 768; one sequence, drawn from the seed, is a single document. `vectors`: gains lie in 0.5 to 1.5, the other entries are of order a few tenths. `mom_qkv`: finite values. `mom_dense`: finite values. `mom_fc1`: finite values. `mom_fc2`: finite values. `first_moment`: finite values. `second_moment`: positive values.
All inputs are finite; a program needn't handle non-finite values.
Results may differ from the reference program's by a relative error of at most 0.025.
Values may be sent and summed in bfloat16 or wider, within the bound.
No kernel may reach another device: no remote copies, remote signals or barrier semaphores. Data moves between devices by JAX's collectives and lax.ppermute only.
A program may use at most 128 MiB of HBM per device.

```python
import math
import jax
import jax.numpy as jnp
from jax import lax

D = 1024
HEADS = 16
HD = 64
ROT = 32
FF = 4096
SEQ = 1024
STEP = 10
TOKENS = 16384
N_DP = 16


def scaled_momentum(key, entries, row_range, column_rise, base):
    row_key, column_key = jax.random.split(key)
    columns = entries.shape[1]
    row_scale = jnp.exp(jax.random.uniform(row_key, (entries.shape[0], 1), jnp.float32, 0.0, math.log(row_range)))
    ramp = jnp.arange(columns, dtype=jnp.float32) / (columns - 1)
    column_scale = jnp.exp(ramp * math.log(column_rise) + jax.random.uniform(column_key, (columns,), jnp.float32, 0.0, math.log(4.0)))
    return entries * row_scale * column_scale[None, :] * base


def segment_scale():
    sections = [jnp.full((D,), 1.0, jnp.float32), jnp.full((D,), 1.0, jnp.float32), jnp.full((3 * D,), 0.3, jnp.float32), jnp.full((D,), 1.0, jnp.float32), jnp.full((FF,), 0.3, jnp.float32), jnp.full((D,), 1.0, jnp.float32)]
    return jnp.concatenate(sections) * math.sqrt(TOKENS)


def draw_positions(key, part):
    key = jax.random.fold_in(key, 1)
    first_key, second_key, pick_key = jax.random.split(key, 3)
    row_count = TOKENS // SEQ
    first_cut = jax.random.randint(first_key, (row_count, 1), 0, SEQ // 4)
    second_cut = jax.random.randint(second_key, (row_count, 1), 3 * SEQ // 4 + 1, SEQ + 1)
    chosen_row = jax.random.randint(pick_key, (), 0, row_count)
    row_ids = jnp.arange(row_count, dtype=jnp.int32)[:, None]
    first_cut = jnp.where(row_ids == chosen_row, 0, first_cut)
    second_cut = jnp.where(row_ids == chosen_row, SEQ + 1, second_cut)
    places = jnp.arange(SEQ, dtype=jnp.int32)[None, :]
    starts = jnp.where(places >= second_cut, second_cut, jnp.where(places >= first_cut, first_cut, 0))
    return (places - starts).reshape(TOKENS).astype(jnp.int32)


def draw_vectors(key, part):
    key = jax.random.fold_in(key, 2)
    gain_key, other_key = jax.random.split(key)
    gains = jax.random.uniform(gain_key, (D,), jnp.float32, 0.5, 1.5)
    others = 0.3 * jnp.clip(jax.random.normal(other_key, (6 * D + FF,), jnp.float32), -6.0, 6.0)
    return jnp.concatenate([gains, others])


def draw_mom_qkv(key, part):
    key = jax.random.fold_in(key, 3)
    entry_key, scale_key = jax.random.split(key)
    entries = jax.random.normal(entry_key, (D, 3 * D), jnp.float32)
    return scaled_momentum(scale_key, entries, 10.0, 3.0, 0.3 * math.sqrt(TOKENS) / 12.0)


def draw_mom_dense(key, part):
    key = jax.random.fold_in(key, 4)
    entry_key, scale_key = jax.random.split(key)
    entries = jax.random.normal(entry_key, (D, D), jnp.float32)
    return scaled_momentum(scale_key, entries, 10.0, 3.0, 0.3 * math.sqrt(TOKENS) / 12.0)


def draw_mom_fc1(key, part):
    key = jax.random.fold_in(key, 5)
    entry_key, scale_key = jax.random.split(key)
    entries = jax.random.normal(entry_key, (D, FF), jnp.float32)
    return scaled_momentum(scale_key, entries, 10.0, 3.0, 0.25 * math.sqrt(TOKENS) / 12.0)


def draw_mom_fc2(key, part):
    key = jax.random.fold_in(key, 6)
    entry_key, scale_key = jax.random.split(key)
    entries = jax.random.normal(entry_key, (D, FF), jnp.float32)
    return scaled_momentum(scale_key, entries, 10.0, 3.0, 0.6 * math.sqrt(TOKENS) / 12.0)


def draw_first_moment(key, part):
    key = jax.random.fold_in(key, 7)
    entries = jnp.clip(jax.random.normal(key, (D * 7 + FF,), jnp.float32), -6.0, 6.0)
    return 0.111 * entries * segment_scale()


def draw_second_moment(key, part):
    key = jax.random.fold_in(key, 8)
    factors = jnp.exp(jax.random.uniform(key, (D * 7 + FF,), jnp.float32, 0.0, math.log(4.0)))
    scales = segment_scale()
    return 0.0526 * scales * scales * factors


def strengthened(drawn, rng, source, target, blocks, factor):
    def block_of(dim):
        return (jnp.arange(drawn.shape[dim]) // (drawn.shape[dim] // blocks)).reshape((-1,) + (1,) * (drawn.ndim - 1 - dim))

    first = jax.random.permutation(rng, blocks)[block_of(target)]
    second = (block_of(target) + blocks // 2) % blocks
    return jnp.where((block_of(source) == first) | (block_of(source) == second), factor * drawn, drawn)


def level_of(rng, shape, cuts, smallest, top_value):
    def one(dim, parts):
        heights = jax.random.uniform(jax.random.fold_in(jax.random.fold_in(rng, 6), dim), (parts,), jnp.float32, smallest / len(cuts), top_value / len(cuts))
        return jnp.repeat(jnp.exp(heights), shape[dim] // parts).reshape((-1,) + (1,) * (len(shape) - dim - 1))

    factor_of = one(*cuts[0])
    for cut in cuts[1:]:
        factor_of = factor_of * one(*cut)
    return factor_of


def gaussian(own_key, extent, deviation, bound, pieces=(), held_as=jnp.bfloat16):
    result = deviation * jax.random.normal(own_key, extent, jnp.float32)
    if pieces:
        result = result * level_of(own_key, extent, pieces, -0.22, 0.18)
    return jnp.clip(result, -bound, bound).astype(held_as)


def gaussian_with(rng, extent, width, reach, pieces, heavy, kind=jnp.bfloat16):
    values = width * jax.random.normal(rng, extent, jnp.float32)
    if pieces:
        values = values * level_of(rng, extent, pieces, -0.22, 0.18)
    return jnp.clip(strengthened(values, jax.random.fold_in(rng, 3), *heavy), -reach, reach).astype(kind)


def setup_inputs(seed: int = 0) -> dict:
    arg_keys = jax.random.split(jax.random.key(seed), 15)
    tokens = gaussian(arg_keys[0], (TOKENS, D), 1.0, 6.0, ((0, 32),))
    cotangent = gaussian_with(arg_keys[1], (TOKENS, D), 1.0, 6.0, ((0, 32),), (0, 1, 32, 2.75))
    positions = draw_positions(jax.random.fold_in(arg_keys[14], 71), 0)
    qkv_weight = gaussian(arg_keys[3], (D, 3 * D), (D // 2) ** -0.5, 0.25, ((0, 16), (1, 2)), jnp.float32)
    dense_weight = gaussian(arg_keys[4], (D, D), (D // 4) ** -0.5, 0.375, ((0, 16), (1, 2)), jnp.float32)
    fc1_weight = gaussian(arg_keys[5], (D, FF), D ** -0.5, 0.1875, ((0, 16), (1, 2)), jnp.float32)
    fc2_weight = gaussian(arg_keys[6], (D, FF), (FF // 2) ** -0.5, 0.125, ((0, 16), (1, 2)), jnp.float32)
    vectors = draw_vectors(jax.random.fold_in(arg_keys[14], 71), 0)
    mom_qkv = draw_mom_qkv(jax.random.fold_in(arg_keys[14], 71), 0)
    mom_dense = draw_mom_dense(jax.random.fold_in(arg_keys[14], 71), 0)
    mom_fc1 = draw_mom_fc1(jax.random.fold_in(arg_keys[14], 71), 0)
    mom_fc2 = draw_mom_fc2(jax.random.fold_in(arg_keys[14], 71), 0)
    first_moment = draw_first_moment(jax.random.fold_in(arg_keys[14], 71), 0)
    second_moment = draw_second_moment(jax.random.fold_in(arg_keys[14], 71), 0)
    return dict(tokens=tokens, cotangent=cotangent, positions=positions, qkv_weight=qkv_weight, dense_weight=dense_weight, fc1_weight=fc1_weight, fc2_weight=fc2_weight, vectors=vectors, mom_qkv=mom_qkv, mom_dense=mom_dense, mom_fc1=mom_fc1, mom_fc2=mom_fc2, first_moment=first_moment, second_moment=second_moment)


@jax.custom_vjp
def low(v):
    return lax.optimization_barrier(v.astype(jnp.bfloat16)).astype(jnp.float32)

@jax.custom_vjp
def low_back(v):
    return v

def low_keep(v):
    return (low(v), None)

def low_pass(kept, grad):
    return (grad,)

def back_keep(v):
    return (v, None)

def back_low(kept, grad):
    return (low(grad),)
low.defvjp(low_keep, low_pass)
low_back.defvjp(back_keep, back_low)
highest = lax.Precision.HIGHEST
momentum_decay = 0.95
muon_rate = 0.15
weight_decay = 0.1
vector_rate = 0.4
beta_first = 0.9
beta_second = 0.95
coef_linear = 3.4445
coef_square = -4.775
coef_cubic = 2.0315

def vector_parts(vector_full):
    return (vector_full[:D], vector_full[D:2 * D], vector_full[2 * D:5 * D], vector_full[5 * D:6 * D], vector_full[6 * D:6 * D + FF], vector_full[6 * D + FF:])

def rotary_tables(positions):
    half_rot = ROT // 2
    frequency = 10000.0 ** (-2.0 * jnp.arange(half_rot, dtype=jnp.float32) / ROT)
    angles = positions.astype(jnp.float32)[..., None] * frequency
    return (jnp.cos(angles), jnp.sin(angles))

def rotate_forward(values, cosine_table, sine_table):
    half_rot = ROT // 2
    first_half = values[..., :half_rot]
    second_half = values[..., half_rot:ROT]
    return jnp.concatenate([first_half * cosine_table - second_half * sine_table, second_half * cosine_table + first_half * sine_table, values[..., ROT:]], axis=-1)

def sequence_mask(positions):
    row_ids = jnp.arange(SEQ, dtype=jnp.int32)
    earlier = row_ids[None, None, :] <= row_ids[None, :, None]
    within = row_ids[None, :, None] - row_ids[None, None, :] <= positions[:, :, None]
    return earlier & within

def group_forward(lowered, token_block, position_block):
    qkv_low, dense_low, fc1_low, fc2_low, vector_low = lowered
    ln_gain, ln_shift, qkv_bias, dense_bias, fc1_bias, fc2_bias = vector_parts(vector_low)
    row_mean = lax.optimization_barrier(jnp.mean(token_block, axis=-1, keepdims=True))
    centred = token_block - row_mean
    inv_std = lax.rsqrt(lax.optimization_barrier(jnp.mean(centred * centred, axis=-1, keepdims=True)) + 1e-05)
    normed = low(centred * inv_std * ln_gain + ln_shift)
    joined_rows = low_back(jnp.dot(normed, qkv_low, precision=highest) + qkv_bias)
    hidden = low_back(jnp.dot(normed, fc1_low, precision=highest) + fc1_bias)
    group_size = position_block.shape[0]
    joined_rows = joined_rows.reshape(group_size, SEQ, HEADS, 3, HD)
    cosine_table, sine_table = rotary_tables(position_block)
    cosine_table = cosine_table[:, :, None, :]
    sine_table = sine_table[:, :, None, :]
    queries = low(rotate_forward(joined_rows[..., 0, :], cosine_table, sine_table))
    key_rows = low(rotate_forward(joined_rows[..., 1, :], cosine_table, sine_table))
    value_rows = low(joined_rows[..., 2, :])
    allowed = sequence_mask(position_block)

    def attend_head(operands):
        head_queries, head_keys, head_values = operands
        scores = low_back(jnp.einsum('gqd,gkd->gqk', head_queries, head_keys, precision=highest) * HD ** (-0.5))
        probabilities = jax.nn.softmax(jnp.where(allowed, scores, -1e+30), axis=-1)
        return jnp.einsum('gqk,gkd->gqd', low(probabilities), head_values, precision=highest)
    attended = lax.map(jax.checkpoint(attend_head), (jnp.moveaxis(queries, 2, 0), jnp.moveaxis(key_rows, 2, 0), jnp.moveaxis(value_rows, 2, 0)))
    attended = low(low_back(attended))
    attended = jnp.moveaxis(attended, 0, 2).reshape(group_size * SEQ, D)
    activation = low(jax.nn.gelu(hidden, approximate=True))
    branch = jnp.dot(attended, dense_low.T, precision=highest) + jnp.dot(activation, fc2_low.T, precision=highest)
    return token_block + branch + dense_bias + fc2_bias

def orthogonalize(momentum):
    rounded = low(momentum)
    iterate = low(rounded / (jnp.sqrt(jnp.sum(rounded * rounded)) + 1e-07))
    for turn_index in range(5):
        gram_matrix = low(jnp.dot(iterate, iterate.T, precision=highest))
        mixing = low(coef_square * gram_matrix + coef_cubic * jnp.dot(gram_matrix, gram_matrix, precision=highest))
        iterate = low(coef_linear * iterate + jnp.dot(mixing, iterate, precision=highest))
    return iterate

def muon_update(master, momentum, gradient):
    new_momentum = momentum_decay * momentum + gradient
    ortho = orthogonalize(new_momentum)
    scale_factor = 0.2 * math.sqrt(max(master.shape))
    return (new_momentum, master * (1.0 - muon_rate * weight_decay) - muon_rate * scale_factor * ortho)

def reference(tokens, cotangent, positions, qkv_weight, dense_weight, fc1_weight, fc2_weight, vectors, mom_qkv, mom_dense, mom_fc1, mom_fc2, first_moment, second_moment):
    group_size = math.gcd(N_DP, max(1, 4096 // SEQ))
    block_count = N_DP // group_size
    token_blocks = tokens.astype(jnp.float32).reshape(block_count, group_size * SEQ, D)
    position_blocks = positions.reshape(block_count, group_size, SEQ)
    masters = (qkv_weight, dense_weight, fc1_weight, fc2_weight, vectors)

    def whole_forward(params, token_input):
        lowered = tuple((low(master) for master in params))

        def one_block(carried, scan_item):
            return (carried, jax.checkpoint(group_forward)(lowered, scan_item[0], scan_item[1]))
        _, results = lax.scan(one_block, jnp.zeros((), jnp.float32), (token_input, position_blocks))
        return results
    results, pullback = jax.vjp(whole_forward, masters, token_blocks)
    grad_masters, token_grad = pullback(cotangent.astype(jnp.float32).reshape(block_count, group_size * SEQ, D))
    output = results.reshape(TOKENS, D).astype(jnp.bfloat16)
    grad_tokens = token_grad.reshape(TOKENS, D)
    new_mom_qkv, new_qkv = muon_update(qkv_weight, mom_qkv, grad_masters[0])
    new_mom_dense, new_dense = muon_update(dense_weight, mom_dense, grad_masters[1])
    new_mom_fc1, new_fc1 = muon_update(fc1_weight, mom_fc1, grad_masters[2])
    new_mom_fc2, new_fc2 = muon_update(fc2_weight, mom_fc2, grad_masters[3])
    vector_grad = grad_masters[4]
    new_first = beta_first * first_moment + (1.0 - beta_first) * vector_grad
    new_second = beta_second * second_moment + (1.0 - beta_second) * vector_grad * vector_grad
    new_vectors = vectors - vector_rate * (new_first / (1.0 - beta_first ** STEP)) / (jnp.sqrt(new_second / (1.0 - beta_second ** STEP)) + 1e-08)
    return (output, grad_tokens, new_mom_qkv, new_qkv, new_mom_dense, new_dense, new_mom_fc1, new_fc1, new_mom_fc2, new_fc2, new_first, new_second, new_vectors)
```

```python
import math

import jax
import jax.numpy as jnp
from jax import lax
from jax.experimental import pallas as pl
from jax.experimental.pallas import tpu as pltpu
from jax.sharding import PartitionSpec as P

D = 1024
HEADS = 16
FF = 4096
STEP = 10
momentum_decay = 0.95
muon_rate = 0.15
weight_decay = 0.1
vector_rate = 0.4
beta_first = 0.9
beta_second = 0.95
HD=64; ROT=32
F32=jnp.float32; BF=jnp.bfloat16
coef_linear = 3.4445
coef_square = -4.775
coef_cubic = 2.0315

def dot_nt(x, y):
    return lax.dot_general(x, y, (((1,), (1,)), ((), ())), preferred_element_type=F32)

def dot_tn(x, y):
    return lax.dot_general(x, y, (((0,), (0,)), ((), ())), preferred_element_type=F32)

def dot_nn(x, y):
    return jnp.dot(x, y, preferred_element_type=F32)

def rope_tables(positions):
    half = ROT // 2
    frequency = 10000.0 ** (-2.0 * jnp.arange(half, dtype=F32) / ROT)
    angles = positions.astype(F32)[:, None] * frequency[None, :]
    cosine, sine = jnp.cos(angles), jnp.sin(angles)
    n = positions.shape[0]
    zeros = jnp.zeros((n, half), F32)
    ones = jnp.ones((n, HD - ROT), F32)
    keep = jnp.concatenate([cosine, cosine, ones], axis=1)
    upper = jnp.concatenate([-sine, zeros, zeros, zeros], axis=1)
    lower = jnp.concatenate([zeros, sine, zeros, zeros], axis=1)
    return tuple(jnp.concatenate([t, t], axis=1) for t in (keep, upper, lower))

ROWS = 256

def attention_kernel(lo_ref, x_ref, g_ref, keep_ref, upper_ref, lower_ref, att_ref, out_ref,
                     q_ref, k_ref, v_ref, dk_ref, dv_ref, dq_ref):
    seq = x_ref.shape[0]
    lane = lax.broadcasted_iota(jnp.int32, (1, 128), 1)
    first = lane < HD
    def rotated(block, rotate_low, rotate_high, sign):
        values = block
        keep, upper, lower = keep_ref[...], upper_ref[...], lower_ref[...]
        if not rotate_low:
            keep = jnp.where(first, 1.0, keep); upper = jnp.where(first, 0.0, upper); lower = jnp.where(first, 0.0, lower)
        if not rotate_high:
            keep = jnp.where(first, keep, 1.0); upper = jnp.where(first, upper, 0.0); lower = jnp.where(first, lower, 0.0)
        half = ROT // 2
        up = pltpu.roll(values, 128 - half, 1) * upper
        down = pltpu.roll(values, half, 1) * lower
        return values * keep + (up + down) * sign
    b0 = rotated(x_ref[:, 0:128], True, True, 1.0)
    b1 = rotated(x_ref[:, 128:256], False, True, 1.0)
    b2 = rotated(x_ref[:, 256:384], True, False, 1.0)
    scale = HD ** -0.5
    q_ref[0] = (b0[:, :HD].astype(BF) * scale).astype(BF)
    k_ref[0] = b0[:, HD:].astype(BF)
    v_ref[0] = b1[:, :HD].astype(BF)
    q_ref[1] = (b1[:, HD:].astype(BF) * scale).astype(BF)
    k_ref[1] = b2[:, :HD].astype(BF)
    v_ref[1] = b2[:, HD:].astype(BF)
    dk_ref[...] = jnp.zeros_like(dk_ref)
    dv_ref[...] = jnp.zeros_like(dv_ref)
    for head in range(2):
        for i in range(seq // ROWS):
            r0, n = i * ROWS, (i + 1) * ROWS
            rows = slice(r0, n)
            q = q_ref[head, rows, :]
            k = k_ref[head, :n, :]
            v = v_ref[head, :n, :]
            g = g_ref[rows, head * HD:(head + 1) * HD]
            s = dot_nt(q, k)
            col = lax.broadcasted_iota(jnp.int32, (ROWS, n), 1)
            row = lax.broadcasted_iota(jnp.int32, (ROWS, n), 0) + r0
            allowed = (col >= lo_ref[rows, :]) & (col <= row)
            s = jnp.where(allowed, s, -1e30)
            top = jnp.max(s, axis=1, keepdims=True)
            e = jnp.exp(s - top)
            total = jnp.sum(e, axis=1, keepdims=True)
            p = e * (1.0 / total)
            pb = p.astype(BF)
            att_ref[rows, head * HD:(head + 1) * HD] = dot_nn(pb, v).astype(BF)
            dp = dot_nt(g, v)
            delta = jnp.sum(p * dp, axis=1, keepdims=True)
            ds = (p * (dp - delta)).astype(BF)
            dq_ref[head, rows, :] = dot_nn(ds, k) * scale
            dk_ref[head, :n, :] += dot_tn(ds, q)
            dv_ref[head, :n, :] += dot_tn(pb, g)
    d0 = jnp.concatenate([dq_ref[0], dk_ref[0]], axis=1)
    d1 = jnp.concatenate([dv_ref[0], dq_ref[1]], axis=1)
    d2 = jnp.concatenate([dk_ref[1], dv_ref[1]], axis=1)
    out_ref[:, 0:128] = rotated(d0, True, True, -1.0).astype(BF)
    out_ref[:, 128:256] = rotated(d1, False, True, -1.0).astype(BF)
    out_ref[:, 256:384] = rotated(d2, True, False, -1.0).astype(BF)

def attention(positions, joined, grad_att):
    seq, width = joined.shape
    pairs = width // (6 * HD)
    keep, upper, lower = rope_tables(positions)
    lo = (jnp.arange(seq, dtype=jnp.int32) - positions)[:, None]
    whole = lambda w: pl.BlockSpec((seq, w), lambda h: (0, 0))
    part = lambda w: pl.BlockSpec((seq, w), lambda h: (0, h))
    return pl.pallas_call(
        attention_kernel,
        grid=(pairs,),
        in_specs=[whole(1), part(6 * HD), part(2 * HD), whole(128), whole(128), whole(128)],
        out_specs=[part(2 * HD), part(6 * HD)],
        out_shape=[jax.ShapeDtypeStruct((seq, pairs * 2 * HD), BF), jax.ShapeDtypeStruct((seq, width), BF)],
        scratch_shapes=[pltpu.VMEM((2, seq, HD), BF)] * 3 + [pltpu.VMEM((2, seq, HD), F32)] * 3,
        compiler_params=pltpu.CompilerParams(vmem_limit_bytes=48 * 2**20),
        name="attention_both",
    )(lo, joined, grad_att, keep, upper, lower)

def chain_kernel(gram_ref, x0_ref, out_ref, a_ref, ah_ref, al_ref, m_ref, t_ref, th_ref, tl_ref, xa_ref):
    size = gram_ref.shape[0]
    blocks = size // ROWS
    row = lax.broadcasted_iota(jnp.int32, (size, size), 0)
    col = lax.broadcasted_iota(jnp.int32, (size, size), 1)
    gram = gram_ref[...]
    trace = jnp.sum(jnp.where(row == col, gram, 0.0))
    norm = jnp.sqrt(trace) + 1e-07
    a_ref[...] = gram * (1.0 / (norm * norm))
    xa_ref[...] = x0_ref[...]
    lin = coef_linear
    def rows_of(i):
        return pl.ds(pl.multiple_of(i * ROWS, ROWS), ROWS)
    def turn(k, last):
        inv = jnp.where(k == 0, 1.0 / norm, 1.0)
        a = a_ref[...]
        ah = a.astype(BF)
        ah_ref[...] = ah
        if not last:
            al_ref[...] = (a - ah.astype(F32)).astype(BF)
        def poly(i, _):
            r = rows_of(i)
            s = dot_nn(ah_ref[r, :], ah_ref[...])
            m_ref[r, :] = (coef_square * ah_ref[r, :].astype(F32) + coef_cubic * s).astype(BF)
            return 0
        lax.fori_loop(0, blocks, poly, 0)
        def apply(i, _):
            r = rows_of(i)
            out_ref[r, :] = ((lin * xa_ref[r, :].astype(F32) + dot_nn(m_ref[r, :], xa_ref[...])) * inv).astype(BF)
            return 0
        lax.fori_loop(0, blocks, apply, 0)
        if last:
            return
        xa_ref[...] = out_ref[...]
        def left(i, _):
            r = rows_of(i)
            t = dot_nn(m_ref[r, :], ah_ref[...]) + dot_nn(m_ref[r, :], al_ref[...])
            t_ref[r, :] = t
            th = t.astype(BF)
            th_ref[r, :] = th
            tl_ref[r, :] = (t - th.astype(F32)).astype(BF)
            return 0
        lax.fori_loop(0, blocks, left, 0)
        def right(i, _):
            r = rows_of(i)
            both = dot_nn(th_ref[r, :], m_ref[...]) + dot_nn(tl_ref[r, :], m_ref[...])
            a_ref[r, :] = lin * lin * a_ref[r, :] + lin * (t_ref[r, :] + t_ref[:, r].T) + both
            return 0
        lax.fori_loop(0, blocks, right, 0)
    def body(k, _):
        turn(k, False)
        return 0
    lax.fori_loop(0, 4, body, 0)
    turn(4, True)

def chain(gram, x0):
    size, width = x0.shape
    V = lambda dt: pltpu.VMEM((size, size), dt)
    spec = pl.BlockSpec(memory_space=pltpu.VMEM)
    return pl.pallas_call(
        chain_kernel,
        out_shape=jax.ShapeDtypeStruct((size, width), BF),
        in_specs=[spec] * 2, out_specs=spec,
        scratch_shapes=[V(F32), V(BF), V(BF), V(BF), V(F32), V(BF), V(BF), pltpu.VMEM((size, width), BF)],
        compiler_params=pltpu.CompilerParams(vmem_limit_bytes=56 * 2**20),
        name="orthogonalize",
    )(gram, x0)


def other(x, axis, bit):
    n = lax.axis_size(axis)
    return lax.ppermute(x, axis, [(i, i ^ bit) for i in range(n)])


def in_order(mine, theirs, index, axis=0):
    low = jnp.where(index == 0, mine, theirs)
    high = jnp.where(index == 0, theirs, mine)
    return jnp.concatenate([low, high], axis=axis)


def sum_over_group(gram, bits):
    core = lax.axis_index("dp") & 1
    rows = gram.shape[0] // 2
    keep = lax.dynamic_slice_in_dim(gram, core * rows, rows, 0)
    give = lax.dynamic_slice_in_dim(gram, (1 - core) * rows, rows, 0)
    keep = keep + other(give, "dp", 1)
    pieces = [keep[: rows // 2], keep[rows // 2 :]]
    steps = [("dp", b) for b in bits] + [("tensor", 1)]
    for turn in range(len(steps)):
        axis, bit = steps[turn]
        pieces[0] = pieces[0] + other(pieces[0], axis, bit)
        axis, bit = steps[len(steps) - 1 - turn]
        pieces[1] = pieces[1] + other(pieces[1], axis, bit)
    half = jnp.concatenate(pieces, axis=0)
    return in_order(half, other(half, "dp", 1), core)


def per_device(
    tokens,
    cotangent,
    positions,
    qkv_weight,
    dense_weight,
    fc1_weight,
    fc2_weight,
    vectors,
    mom_qkv,
    mom_dense,
    mom_fc1,
    mom_fc2,
    first_moment,
    second_moment,
):
    tensor_index = lax.axis_index("tensor")
    n = lax.axis_size("dp")
    joined_width = 3 * D // 2
    unit_width = FF // 2
    shard_rows = qkv_weight.shape[0]
    half_rows = tokens.shape[0]
    seq = 2 * half_rows

    share = vectors.shape[0]
    vec_rows = 16
    vec_pad = jnp.pad(vectors.astype(BF), (0, vec_rows * unit_width - share)).reshape(
        vec_rows, unit_width
    )
    first_pack = jnp.concatenate(
        [
            jnp.concatenate([qkv_weight.astype(BF), dense_weight.astype(BF)], axis=1),
            vec_pad,
        ],
        axis=0,
    )
    first_full = lax.all_gather(first_pack, "dp", axis=0, tiled=False)
    second_pack = jnp.concatenate([fc1_weight.astype(BF), fc2_weight.astype(BF)], axis=0)
    second_full = lax.all_gather(second_pack, "dp", axis=0, tiled=False)
    full_qkv = first_full[:, :shard_rows, :joined_width].reshape(D, joined_width)
    full_dense = first_full[:, :shard_rows, joined_width:].reshape(D, D // 2)
    full_fc1 = second_full[:, :shard_rows].reshape(D, unit_width)
    full_fc2 = second_full[:, shard_rows:].reshape(D, unit_width)
    vector_full = first_full[:, shard_rows, :share].reshape(n * share).astype(F32)

    ln_gain = vector_full[:D]
    ln_shift = vector_full[D : 2 * D]
    qkv_bias = lax.dynamic_slice_in_dim(
        vector_full, 2 * D + tensor_index * joined_width, joined_width
    )
    dense_bias = vector_full[5 * D : 6 * D]
    fc1_bias = lax.dynamic_slice_in_dim(vector_full, 6 * D + tensor_index * unit_width, unit_width)
    fc2_bias = vector_full[6 * D + FF :]

    tokens_all = in_order(tokens, other(tokens, "tensor", 1), tensor_index)
    cotangent_all = in_order(cotangent, other(cotangent, "tensor", 1), tensor_index)

    def normalized(rows):
        values = rows.astype(F32)
        centred = values - jnp.mean(values, axis=1, keepdims=True)
        inv_std = lax.rsqrt(jnp.mean(centred * centred, axis=1, keepdims=True) + 1e-05)
        return centred * inv_std, inv_std

    normed_all = (normalized(tokens_all)[0] * ln_gain + ln_shift).astype(BF)
    joined = dot_nn(normed_all, full_qkv) + qkv_bias
    grad_attended = dot_nn(cotangent_all, full_dense).astype(BF)
    attended, grad_joined = attention(positions, joined, grad_attended)

    hidden = dot_nn(normed_all, full_fc1) + fc1_bias
    activation, gelu_pullback = jax.vjp(lambda v: jax.nn.gelu(v, approximate=True), hidden)
    activation = activation.astype(BF)
    grad_hidden = gelu_pullback(dot_nn(cotangent_all, full_fc2))[0].astype(BF)
    grad_fc2 = dot_tn(cotangent_all, activation).astype(BF)
    grad_fc1 = dot_tn(normed_all, grad_hidden).astype(BF)
    wide_share = lax.psum_scatter(
        jnp.concatenate([grad_fc1, grad_fc2], axis=1), "dp", scatter_dimension=0, tiled=True
    )

    def across(partial):
        mine = lax.dynamic_slice_in_dim(partial, tensor_index * half_rows, half_rows, 0)
        theirs = lax.dynamic_slice_in_dim(partial, (1 - tensor_index) * half_rows, half_rows, 0)
        return mine.astype(F32) + other(theirs, "tensor", 1).astype(F32)

    branch = across((dot_nt(attended, full_dense) + dot_nt(activation, full_fc2)).astype(BF))
    output = (tokens.astype(F32) + branch + dense_bias + fc2_bias).astype(BF)

    grad_normed = across((dot_nt(grad_joined, full_qkv) + dot_nt(grad_hidden, full_fc1)).astype(BF))
    unit_normed, inv_std = normalized(tokens)
    scaled_grad = grad_normed * ln_gain
    grad_tokens = cotangent.astype(F32) + inv_std * (
        scaled_grad
        - jnp.mean(scaled_grad, axis=1, keepdims=True)
        - unit_normed * jnp.mean(scaled_grad * unit_normed, axis=1, keepdims=True)
    )

    grad_qkv = dot_tn(normed_all, grad_joined).astype(BF)
    grad_dense = dot_tn(cotangent_all, attended).astype(BF)
    narrow_share = lax.psum_scatter(
        jnp.concatenate([grad_qkv, grad_dense], axis=1), "dp", scatter_dimension=0, tiled=True
    )

    row_cotangent = jnp.sum(cotangent.astype(F32), axis=0)
    qkv_bias_grad = lax.dynamic_update_slice_in_dim(
        jnp.zeros((3 * D,), F32),
        jnp.sum(grad_joined.astype(F32), axis=0),
        tensor_index * joined_width,
        0,
    )
    fc1_bias_grad = lax.dynamic_update_slice_in_dim(
        jnp.zeros((FF,), F32),
        jnp.sum(grad_hidden.astype(F32), axis=0),
        tensor_index * unit_width,
        0,
    )
    vector_grad = jnp.concatenate(
        [
            jnp.sum(grad_normed * unit_normed, axis=0),
            jnp.sum(grad_normed, axis=0),
            qkv_bias_grad,
            row_cotangent,
            fc1_bias_grad,
            row_cotangent,
        ]
    )
    vector_parts = lax.all_to_all(
        vector_grad.reshape(2 * n, share // 2), ("dp", "tensor"), 0, 0, tiled=True
    )
    vector_share = jnp.sum(vector_parts, axis=0)

    grads = (
        narrow_share[:, :joined_width],
        narrow_share[:, joined_width:],
        wide_share[:, :unit_width],
        wide_share[:, unit_width:],
    )
    moms = (mom_qkv, mom_dense, mom_fc1, mom_fc2)
    new_moms = [momentum_decay * m + g.astype(F32) for m, g in zip(moms, grads)]

    group = n // 4
    slot = unit_width // group
    blocks = []
    for moment in new_moms:
        width = moment.shape[1] // group
        block = moment.astype(BF).reshape(shard_rows, group, width).transpose(1, 0, 2)
        blocks.append(jnp.pad(block, ((0, 0), (0, 0), (0, slot - width))))
    columns = lax.all_to_all(jnp.concatenate(blocks, axis=0), "dp", 0, 0, tiled=True)
    columns = columns.reshape(D, slot)
    bits = []
    bit = 2
    while bit < group:
        bits.append(bit)
        bit *= 2
    gram = sum_over_group(dot_nt(columns, columns), bits)
    ortho = chain(gram, columns)
    pieces = lax.all_to_all(ortho.reshape(n, shard_rows, slot), "dp", 0, 0, tiled=True)
    masters = (qkv_weight, dense_weight, fc1_weight, fc2_weight)
    new_weights = []
    for index, master in enumerate(masters):
        width = master.shape[1]
        piece = pieces[index * group : (index + 1) * group, :, : width // group]
        piece = piece.transpose(1, 0, 2).reshape(shard_rows, width).astype(F32)
        scale_factor = 0.2 * math.sqrt(max(D, 2 * width))
        new_weights.append(
            master * (1.0 - muon_rate * weight_decay) - muon_rate * scale_factor * piece
        )

    vector_slot = lax.dynamic_slice_in_dim(vectors, tensor_index * (share // 2), share // 2)
    new_first = beta_first * first_moment + (1.0 - beta_first) * vector_share
    new_second = beta_second * second_moment + (1.0 - beta_second) * vector_share * vector_share
    new_vectors = vector_slot - vector_rate * (new_first / (1.0 - beta_first**STEP)) / (
        jnp.sqrt(new_second / (1.0 - beta_second**STEP)) + 1e-08
    )
    return (
        output,
        grad_tokens,
        new_moms[0],
        new_weights[0],
        new_moms[1],
        new_weights[1],
        new_moms[2],
        new_weights[2],
        new_moms[3],
        new_weights[3],
        new_first,
        new_second,
        new_vectors,
    )


def solution(mesh):
    rows = P(("dp", "tensor"), None)
    weight = P("dp", "tensor")
    vector = P(("dp", "tensor"))
    return jax.shard_map(
        per_device,
        mesh=mesh,
        in_specs=(rows, rows, P("dp")) + (weight,) * 4 + (P("dp"),) + (weight,) * 4 + (vector,) * 2,
        out_specs=(rows, rows) + (weight,) * 8 + (vector,) * 3,
        check_vma=False,
    )
```

```python
import math

import jax
import jax.numpy as jnp
from jax import lax
from jax.experimental import pallas as pl
from jax.experimental.pallas import tpu as pltpu
from jax.sharding import PartitionSpec as P

D = 1024
HEADS = 16
FF = 4096
STEP = 10
momentum_decay = 0.95
muon_rate = 0.15
weight_decay = 0.1
vector_rate = 0.4
beta_first = 0.9
beta_second = 0.95
HD=64; ROT=32
F32=jnp.float32; BF=jnp.bfloat16
coef_linear = 3.4445
coef_square = -4.775
coef_cubic = 2.0315

def dot_nt(x, y):
    return lax.dot_general(x, y, (((1,), (1,)), ((), ())), preferred_element_type=F32)

def dot_tn(x, y):
    return lax.dot_general(x, y, (((0,), (0,)), ((), ())), preferred_element_type=F32)

def dot_nn(x, y):
    return jnp.dot(x, y, preferred_element_type=F32)

def tables_kernel(position_ref, frequency_ref, keep_ref, upper_ref, lower_ref):
    half = ROT // 2
    lane = lax.broadcasted_iota(jnp.int32, (1, 2 * HD), 1) % HD
    angles = position_ref[...].astype(F32) * frequency_ref[...]
    cosine, sine = jnp.cos(angles), jnp.sin(angles)
    keep_ref[...] = jnp.where(lane < ROT, cosine, 1.0)
    upper_ref[...] = jnp.where(lane < half, -sine, 0.0)
    lower_ref[...] = jnp.where((lane >= half) & (lane < ROT), sine, 0.0)

def rope_tables(positions):
    half = ROT // 2
    frequency = 10000.0 ** (-2.0 * jnp.arange(half, dtype=F32) / ROT)
    table = jax.ShapeDtypeStruct((positions.shape[0], 2 * HD), F32)
    return pl.pallas_call(
        tables_kernel,
        out_shape=[table] * 3,
        cost_estimate=pl.CostEstimate(flops=10**9, bytes_accessed=2 * 10**7, transcendentals=0),
        name="rope_tables",
    )(positions[:, None], jnp.tile(frequency, 2 * HD // half)[None])

ROWS = 256

def attention_kernel(lo_ref, x_ref, g_ref, keep_ref, upper_ref, lower_ref, att_ref, out_ref,
           bias_ref, s_ref, top_ref, o_ref, ge_ref, q_ref, k_ref, v_ref, dk_ref, dv_ref, dq_ref):
    seq = x_ref.shape[0]
    lane = lax.broadcasted_iota(jnp.int32, (1, 128), 1)
    first = lane < HD
    half = ROT // 2
    blocks = seq // ROWS
    @pl.when(pl.program_id(0) == 0)
    def _():
        for i in range(blocks):
            r0, n = i * ROWS, (i + 1) * ROWS
            col = lax.broadcasted_iota(jnp.int32, (ROWS, n), 1)
            row = lax.broadcasted_iota(jnp.int32, (ROWS, n), 0) + r0
            allowed = (col >= lo_ref[r0:n, :]) & (col <= row)
            bias_ref[r0:n, :n] = jnp.where(allowed, 0.0, -1e30)
    def rotated(values, low, high, sign):
        keep, upper, lower = keep_ref[...], upper_ref[...], lower_ref[...]
        if not (low and high):
            off = first if high else ~first
            keep = jnp.where(off, 1.0, keep); upper = jnp.where(off, 0.0, upper); lower = jnp.where(off, 0.0, lower)
        up = pltpu.roll(values, 128 - half, 1) * upper
        down = pltpu.roll(values, half, 1) * lower
        return values * keep + (up + down) * sign
    b0 = rotated(x_ref[:, 0:128], True, True, 1.0)
    b1 = rotated(x_ref[:, 128:256], False, True, 1.0)
    b2 = rotated(x_ref[:, 256:384], True, False, 1.0)
    scale = HD ** -0.5
    r1, r2 = pltpu.roll(b1, HD, 1), pltpu.roll(b2, HD, 1)
    ones = jnp.where((lane == HD) | (lane == HD + 1), 1.0, 0.0)
    q_ref[0] = jnp.where(first, b0 * scale, 0.0).astype(BF)
    k_ref[0] = pltpu.roll(b0, HD, 1).astype(BF)
    v_ref[0] = jnp.where(first, b1, ones).astype(BF)
    q_ref[1] = jnp.where(first, r1 * scale, 0.0).astype(BF)
    k_ref[1] = b2.astype(BF)
    v_ref[1] = jnp.where(first, r2, ones).astype(BF)
    units = [(h, i) for i in range(blocks) for h in range(2)]
    def spans(i):
        return slice(i * ROWS, (i + 1) * ROWS), (i + 1) * ROWS
    for h, i in units:
        rows, n = spans(i)
        s = dot_nt(q_ref[h, rows, :], k_ref[h, :n, :]) + bias_ref[rows, :n]
        s_ref[h, rows, :n] = s
        m = s[:, :128]
        for c in range(128, n, 128):
            m = jnp.maximum(m, s[:, c:c + 128])
        top_ref[h, rows, :] = m
    for h in range(2):
        top_ref[h] = jnp.broadcast_to(jnp.max(top_ref[h], axis=1, keepdims=True), (seq, 128))
    for h, i in units:
        rows, n = spans(i)
        e = jnp.exp(s_ref[h, rows, :n] - top_ref[h, rows, :1])
        s_ref[h, rows, :n] = e
        o_ref[h, rows, :] = dot_nn(e.astype(BF), v_ref[h, :n, :])
    atts = []
    for h in range(2):
        o = o_ref[h]
        inv = 1.0 / o[:, HD:HD + 1]
        att = jnp.where(first, o * inv, 0.0)
        atts.append(att)
        gr = g_ref[...].astype(F32)
        if h == 1:
            gr = pltpu.roll(gr, HD, 1)
        gs = jnp.where(first, gr * inv, 0.0).astype(BF).astype(F32)
        delta = jnp.sum(gs * att, axis=1, keepdims=True)
        dh = delta.astype(BF).astype(F32)
        ge_ref[h] = jnp.where(lane == HD, -dh, jnp.where(lane == HD + 1, dh - delta, gs)).astype(BF)
    att_ref[...] = jnp.where(first, atts[0], pltpu.roll(atts[1], HD, 1)).astype(BF)
    dk_ref[...] = jnp.zeros_like(dk_ref)
    dv_ref[...] = jnp.zeros_like(dv_ref)
    for h, i in units:
        rows, n = spans(i)
        e = s_ref[h, rows, :n]
        ge = ge_ref[h, rows, :]
        ds = (e * dot_nt(ge, v_ref[h, :n, :])).astype(BF)
        dq_ref[h, rows, :] = dot_nn(ds, k_ref[h, :n, :]) * scale
        dk_ref[h, :n, :] += dot_tn(ds, q_ref[h, rows, :])
        dv_ref[h, :n, :] += dot_tn(e.astype(BF), ge)
    d0 = jnp.where(first, dq_ref[0], pltpu.roll(dk_ref[0], HD, 1))
    d1 = jnp.where(first, dv_ref[0], pltpu.roll(dq_ref[1], HD, 1))
    d2 = jnp.where(first, dk_ref[1], pltpu.roll(dv_ref[1], HD, 1))
    out_ref[:, 0:128] = rotated(d0, True, True, -1.0).astype(BF)
    out_ref[:, 128:256] = rotated(d1, False, True, -1.0).astype(BF)
    out_ref[:, 256:384] = rotated(d2, True, False, -1.0).astype(BF)

def attention_tables(positions):
    lo = (jnp.arange(positions.shape[0], dtype=jnp.int32) - positions)[:, None]
    return (lo, *rope_tables(positions))

def attention(tables, joined, grad_att):
    lo, keep, upper, lower = tables
    seq, width = joined.shape
    pairs = width // (6 * HD)
    whole = lambda w: pl.BlockSpec((seq, w), lambda h: (0, 0))
    part = lambda w: pl.BlockSpec((seq, w), lambda h: (0, h))
    return pl.pallas_call(
        attention_kernel,
        grid=(pairs,),
        in_specs=[whole(1), part(6 * HD), part(2 * HD), whole(128), whole(128), whole(128)],
        out_specs=[part(2 * HD), part(6 * HD)],
        out_shape=[jax.ShapeDtypeStruct((seq, pairs * 2 * HD), BF), jax.ShapeDtypeStruct((seq, width), BF)],
        scratch_shapes=[pltpu.VMEM((seq, seq), F32), pltpu.VMEM((2, seq, seq), F32)]
        + [pltpu.VMEM((2, seq, 2 * HD), dtype) for dtype in (F32, F32, BF, BF, BF, BF, F32, F32, F32)],
        compiler_params=pltpu.CompilerParams(vmem_limit_bytes=48 * 2**20),
        name="attention_both",
    )(lo, joined, grad_att, keep, upper, lower)

BAND = 128

def gram_kernel(x_ref, out_ref, twice_ref):
    size = x_ref.shape[0]
    span = out_ref.shape[1]
    twice_ref[:size, :] = x_ref[...]
    twice_ref[size:, :] = x_ref[: span - BAND, :]
    for i in range(size // BAND):
        r = i * BAND
        out_ref[r:r + BAND, :] = dot_nt(x_ref[r:r + BAND, :], twice_ref[r:r + span, :])

def gram(x):
    size, width = x.shape
    span = size // 2 + BAND
    spec = pl.BlockSpec(memory_space=pltpu.VMEM)
    return pl.pallas_call(
        gram_kernel,
        out_shape=jax.ShapeDtypeStruct((size, span), F32),
        in_specs=[spec], out_specs=spec,
        scratch_shapes=[pltpu.VMEM((size + span - BAND, width), BF)],
        compiler_params=pltpu.CompilerParams(vmem_limit_bytes=32 * 2**20),
        name="gram",
    )(x)

def chain_kernel(core_ref, mine_ref, theirs_ref, x0_ref, out_ref, a_ref, ah_ref, m_ref, u_ref, uh_ref, xa_ref):
    size = x0_ref.shape[0]
    bands = size // BAND
    row = lax.broadcasted_iota(jnp.int32, (size // 2, BAND), 0)
    col = lax.broadcasted_iota(jnp.int32, (size // 2, BAND), 1)
    diagonal = mine_ref[:, :BAND] + theirs_ref[:, :BAND]
    trace = jnp.sum(jnp.where(row % BAND == col, diagonal, 0.0))
    norm = jnp.sqrt(trace) + 1e-07
    scale = 1.0 / (norm * norm)
    def store(rs, cs, block):
        a_ref[rs, cs] = block
        ah_ref[rs, cs] = block.astype(BF)
    def unpack(half_ref, start):
        for i in range(start, start + bands // 2):
            r = (i - start) * BAND
            for o in range(bands // 2 + 1):
                j = (i + o) % bands
                block = half_ref[r:r + BAND, o * BAND:(o + 1) * BAND] * scale
                store(slice(i * BAND, (i + 1) * BAND), slice(j * BAND, (j + 1) * BAND), block)
                if 0 < o < bands // 2:
                    store(slice(j * BAND, (j + 1) * BAND), slice(i * BAND, (i + 1) * BAND), block.T)
    @pl.when(core_ref[0] == 0)
    def _():
        unpack(mine_ref, 0)
        unpack(theirs_ref, bands // 2)
    @pl.when(core_ref[0] == 1)
    def _():
        unpack(theirs_ref, 0)
        unpack(mine_ref, bands // 2)
    xa_ref[...] = x0_ref[...]
    lin = coef_linear
    def turn(k, last):
        inv = jnp.where(k == 0, 1.0 / norm, 1.0)
        for r0 in range(0, size, ROWS):
            r, c = slice(r0, r0 + ROWS), slice(r0, size)
            s = dot_nn(ah_ref[r, :], ah_ref[:, c])
            m = (coef_square * ah_ref[r, c].astype(F32) + coef_cubic * s).astype(BF)
            m_ref[r, c] = m
            if r0 + ROWS < size:
                m_ref[r0 + ROWS:, r] = m[:, ROWS:].T
        for r0 in range(0, size, 2 * ROWS):
            r = slice(r0, r0 + (2 * ROWS))
            out_ref[r, :] = ((lin * xa_ref[r, :].astype(F32) + dot_nn(m_ref[r, :], xa_ref[...])) * inv).astype(BF)
        if last:
            return
        xa_ref[...] = out_ref[...]
        for r0 in range(0, size, 2 * ROWS):
            r = slice(r0, r0 + 2 * ROWS)
            u = lin * a_ref[r, :] + dot_nn(m_ref[r, :], ah_ref[...])
            u_ref[r, :] = u
            uh_ref[r, :] = u.astype(BF)
        for r0 in range(0, size, ROWS):
            r, c = slice(r0, r0 + ROWS), slice(r0, size)
            block = lin * u_ref[r, c] + dot_nn(uh_ref[r, :], m_ref[:, c])
            store(r, c, block)
            if r0 + ROWS < size:
                store(slice(r0 + ROWS, size), r, block[:, ROWS:].T)
    def body(k, _):
        turn(k, False)
        return 0
    lax.fori_loop(0, 4, body, 0)
    turn(4, True)
def chain(core, mine, theirs, x0):
    size, width = x0.shape
    V = lambda dt: pltpu.VMEM((size, size), dt)
    spec = pl.BlockSpec(memory_space=pltpu.VMEM)
    return pl.pallas_call(
        chain_kernel,
        out_shape=jax.ShapeDtypeStruct((size, width), BF),
        in_specs=[pl.BlockSpec(memory_space=pltpu.SMEM)] + [spec] * 3, out_specs=spec,
        scratch_shapes=[V(F32), V(BF), V(BF), V(F32), V(BF), pltpu.VMEM((size, width), BF)],
        compiler_params=pltpu.CompilerParams(vmem_limit_bytes=56 * 2**20),
        name="orthogonalize",
    )(core.reshape(1), mine, theirs, x0)

def assemble(core, chips, mine, theirs, widths, rest):
    count = len(mine)
    rows = mine[0].shape[0] - rest
    width = mine[0].shape[1]
    n = 2 * count
    def kernel(core_ref, chips_ref, *refs):
        blocks, outs = refs[:n], refs[n:]
        for k in range(n):
            which = core_ref[0] if k < count else 1 - core_ref[0]
            index = chips_ref[k % count] * 2 + which
            place = pl.ds(pl.multiple_of(index * rows, rows), rows)
            start = 0
            for out, w in zip(outs, widths):
                out[place, :] = blocks[k][:rows, start:start + w]
                start += w
            outs[-1][pl.ds(pl.multiple_of(index * rest, rest), rest), :] = blocks[k][rows:, :]
    vmem, smem = pl.BlockSpec(memory_space=pltpu.VMEM), pl.BlockSpec(memory_space=pltpu.SMEM)
    shapes = [(n * rows, w) for w in widths] + [(n * rest, width)]
    return pl.pallas_call(
        kernel,
        out_shape=[jax.ShapeDtypeStruct(s, BF) for s in shapes],
        in_specs=[smem, smem] + [vmem] * n,
        out_specs=[vmem] * len(shapes),
        compiler_params=pltpu.CompilerParams(vmem_limit_bytes=48 * 2**20),
        name="assemble",
    )(core.reshape(1), chips, *mine, *theirs)


def other(x, axis, bit):
    n = lax.axis_size(axis)
    return lax.ppermute(x, axis, [(i, i ^ bit) for i in range(n)])


def in_order(mine, theirs, index, axis=0):
    low = jnp.where(index == 0, mine, theirs)
    high = jnp.where(index == 0, theirs, mine)
    return jnp.concatenate([low, high], axis=axis)


class Ring:
    def __init__(self):
        n = lax.axis_size("dp")
        self.count = n // 2
        rows = self.count // 2
        order = [2 * i for i in range(rows)] + [2 * i + 1 for i in reversed(range(rows))]
        place = [order.index(chip) for chip in range(self.count)]
        index = lax.axis_index("dp")
        self.core = index % 2
        position = lax.dynamic_index_in_dim(jnp.array(place, jnp.int32), index // 2, 0, False)
        self.chips = lax.dynamic_slice_in_dim(
            jnp.array(order + order, jnp.int32), position, self.count, 0
        )
        self.up_pairs = [
            (2 * order[i] + c, 2 * order[(i + 1) % self.count] + c)
            for i in range(self.count)
            for c in range(2)
        ]
        self.down_pairs = [(b, a) for a, b in self.up_pairs]

    def up(self, x):
        return lax.ppermute(x, "dp", self.up_pairs)

    def down(self, x):
        return lax.ppermute(x, "dp", self.down_pairs)

    def gather(self, shard, rides, positions):
        rows = shard.shape[0]
        half, cut = self.count // 2, rows // 32 * 16 or rows // 2
        mine = {0: shard}
        rising = falling = shard
        for step in range(half):
            if step == half - 1:
                rising, falling = rising[:cut], falling[cut:]
            rising, falling = self.up(rising), self.down(falling)
            if step < len(rides):
                ride = other(rides[step], "tensor", 1)
                if step == 1:
                    tables = attention_tables(positions)
                    rising, falling, tables = lax.optimization_barrier((rising, falling, tables))
                rising, falling, rides[step] = lax.optimization_barrier((rising, falling, ride))
                if step == 0:
                    rising, positions = lax.optimization_barrier((rising, positions))
            if step < half - 1:
                mine[self.count - 1 - step], mine[1 + step] = rising, falling
        mine[half] = jnp.concatenate([rising, falling], axis=0)
        mine = [mine[k] for k in range(self.count)]
        return mine, [other(block, "dp", 1) for block in mine], tables

    def split(self, values, rows):
        parts = values.reshape(values.shape[0], self.count, 2, rows)
        return tuple(
            lax.dynamic_index_in_dim(parts, c, 2, False).reshape(values.shape[0], -1)
            for c in (self.core, 1 - self.core)
        )

    def pair_sum(self, lefts, right):
        keep, give = lefts
        theirs = other(dot_tn(give, right).astype(BF), "dp", 1)
        return (dot_tn(keep, right) + theirs.astype(F32)).astype(BF)

    def scatter(self, sums, beside=(), state=()):
        rows = sums[0].shape[0] // self.count
        half, cut = self.count // 2, rows // 32 * 16 or rows // 2

        def block(step):
            start = self.chips[step % self.count] * rows
            return jnp.concatenate(
                [lax.dynamic_slice_in_dim(s, start, rows, 0) for s in sums], axis=1
            )

        def send(step, rising, falling):
            nonlocal state
            if step >= len(beside):
                return self.up(rising), self.down(falling)
            rising, falling, state = lax.optimization_barrier((rising, falling, state))
            rising, falling, state = self.up(rising), self.down(falling), beside[step](state)
            rising, falling, state = lax.optimization_barrier((rising, falling, state))
            return rising, falling

        far = block(half)
        rising, falling = send(0, far[:cut], far[cut:])
        for step in range(half - 1, 0, -1):
            low, high = block(step).astype(F32), block(-step).astype(F32)
            rising, falling = rising.astype(F32), falling.astype(F32)
            if step == half - 1:
                low = jnp.concatenate([low[:cut] + rising, low[cut:]], axis=0)
                high = jnp.concatenate([high[:cut], high[cut:] + falling], axis=0)
            else:
                low, high = low + rising, high + falling
            rising, falling = send(half - step, low.astype(BF), high.astype(BF))
        return block(0).astype(F32) + rising.astype(F32) + falling.astype(F32), state


def gelu_and_slope(v):
    root = math.sqrt(2.0 / math.pi)
    square = v * v
    tanh = jnp.tanh(root * v * (1.0 + 0.044715 * square))
    half = 0.5 * (1.0 + tanh)
    inner = root * (1.0 + 3.0 * 0.044715 * square)
    return v * half, half + 0.5 * v * (1.0 - tanh * tanh) * inner


def sum_over_group(packed, bits, tie):
    core = lax.axis_index("dp") % 2
    rows = packed.shape[0] // 2
    keep = lax.dynamic_slice_in_dim(packed, core * rows, rows, 0)
    give = lax.dynamic_slice_in_dim(packed, (1 - core) * rows, rows, 0)
    keep = keep + other(give, "dp", 1)
    pieces = [keep[: rows // 2], keep[rows // 2 :]]
    steps = [("dp", b) for b in bits] + [("tensor", 1)]
    for turn in range(len(steps)):
        if turn == len(steps) - 1:
            pieces, tie = lax.optimization_barrier((pieces, tie))
        axis, bit = steps[turn]
        first = other(pieces[0], axis, bit)
        axis, bit = steps[len(steps) - 1 - turn]
        second = other(pieces[1], axis, bit)
        pieces = [pieces[0] + first, pieces[1] + second]
    half = jnp.concatenate(pieces, axis=0)
    return half, other(half, "dp", 1), tie


def per_device(
    tokens,
    cotangent,
    positions,
    qkv_weight,
    dense_weight,
    fc1_weight,
    fc2_weight,
    vectors,
    mom_qkv,
    mom_dense,
    mom_fc1,
    mom_fc2,
    first_moment,
    second_moment,
):
    tensor_index = lax.axis_index("tensor")
    n = lax.axis_size("dp")
    ring = Ring()
    joined_width = 3 * D // 2
    unit_width = FF // 2
    shard_rows = qkv_weight.shape[0]
    half_rows = tokens.shape[0]
    seq = 2 * half_rows

    share = vectors.shape[0]
    vec_rows = 16
    vec_pad = jnp.pad(vectors.astype(BF), (0, vec_rows * unit_width - share)).reshape(
        vec_rows, unit_width
    )
    first_pack = jnp.concatenate(
        [
            jnp.concatenate([qkv_weight.astype(BF), dense_weight.astype(BF)], axis=1),
            vec_pad,
        ],
        axis=0,
    )
    second_pack = jnp.stack([fc1_weight.astype(BF), fc2_weight.astype(BF)])
    quarter = half_rows // 2
    rides = [tokens[:quarter], tokens[quarter:], cotangent[:quarter], cotangent[quarter:]]
    mine, theirs, tables = ring.gather(first_pack, rides, positions)
    second_pack, rides[1] = lax.optimization_barrier((second_pack, rides[1]))
    full_fc1, full_fc2 = lax.all_gather(second_pack, "dp", axis=1, tiled=True)
    tokens_theirs = jnp.concatenate(rides[:2], axis=0)
    cotangent_theirs = jnp.concatenate(rides[2:], axis=0)
    full_qkv, full_dense, full_rest = assemble(
        ring.core, ring.chips, mine, theirs, (joined_width, D // 2), vec_rows
    )
    vector_full = full_rest.reshape(n, vec_rows, unit_width)[:, 0, :share].reshape(-1).astype(F32)

    ln_gain = vector_full[:D]
    ln_shift = vector_full[D : 2 * D]
    qkv_bias = lax.dynamic_slice_in_dim(
        vector_full, 2 * D + tensor_index * joined_width, joined_width
    )
    dense_bias = vector_full[5 * D : 6 * D]
    fc1_bias = lax.dynamic_slice_in_dim(vector_full, 6 * D + tensor_index * unit_width, unit_width)
    fc2_bias = vector_full[6 * D + FF :]

    tokens_all = in_order(tokens, tokens_theirs, tensor_index)
    cotangent_all = in_order(cotangent, cotangent_theirs, tensor_index)

    def normalized(rows):
        values = rows.astype(F32)
        centred = values - jnp.mean(values, axis=1, keepdims=True)
        inv_std = lax.rsqrt(jnp.mean(centred * centred, axis=1, keepdims=True) + 1e-05)
        return centred * inv_std, inv_std

    normed_all = (normalized(tokens_all)[0] * ln_gain + ln_shift).astype(BF)
    joined = dot_nn(normed_all, full_qkv) + qkv_bias
    grad_attended = dot_nn(cotangent_all, full_dense).astype(BF)
    attended, grad_joined = attention(tables, joined, grad_attended)

    normed_parts = ring.split(normed_all, shard_rows)
    cotangent_parts = ring.split(cotangent_all, shard_rows)
    narrow_sums = [
        ring.pair_sum(normed_parts, grad_joined),
        ring.pair_sum(cotangent_parts, attended),
    ]

    def forward(state):
        normed_all, full_fc1 = state
        hidden = dot_nn(normed_all, full_fc1) + fc1_bias
        return tuple(v.astype(BF) for v in gelu_and_slope(hidden))

    def backward(state):
        activation, slope, cotangent_all, full_fc2 = state
        grad_act = dot_nn(cotangent_all, full_fc2)
        return activation, (grad_act * slope.astype(F32)).astype(BF)

    def give(state):
        activation, grad_hidden = state
        return state + (
            dot_tn(normed_parts[1], grad_hidden).astype(BF),
            dot_tn(cotangent_parts[1], activation).astype(BF),
        )

    def keep(state):
        activation, grad_hidden, *given = state
        mine = (dot_tn(normed_parts[0], grad_hidden), dot_tn(cotangent_parts[0], activation))
        sums = [
            (m + other(g, "dp", 1).astype(F32)).astype(BF) for m, g in zip(mine, given)
        ]
        return activation, grad_hidden, sums

    narrow_share, (activation, grad_hidden, wide_sums) = ring.scatter(
        narrow_sums,
        (forward, lambda state: backward((*state, cotangent_all, full_fc2)), give, keep),
        (normed_all, full_fc1),
    )
    wide_sums, narrow_share, attended, grad_joined = lax.optimization_barrier(
        (wide_sums, narrow_share, attended, grad_joined)
    )

    def across(partial):
        mine = lax.dynamic_slice_in_dim(partial, tensor_index * half_rows, half_rows, 0)
        theirs = lax.dynamic_slice_in_dim(partial, (1 - tensor_index) * half_rows, half_rows, 0)
        return mine, theirs

    branch_mine, branch_theirs = across(
        (dot_nt(attended, full_dense) + dot_nt(activation, full_fc2)).astype(BF)
    )
    normed_mine, normed_theirs = across(
        (dot_nt(grad_joined, full_qkv) + dot_nt(grad_hidden, full_fc1)).astype(BF)
    )
    def ride(step):
        def exchange(state):
            return (*state[:step], other(state[step], "tensor", 1), *state[step + 1 :])

        return exchange

    wide_share, state = ring.scatter(
        wide_sums,
        (lambda state: state, ride(0), ride(1), ride(2)),
        (branch_theirs[:quarter], branch_theirs[quarter:], normed_theirs[:quarter]),
    )
    branch_theirs = jnp.concatenate(state[:2], axis=0)
    normed_theirs = jnp.concatenate([state[2], other(normed_theirs[quarter:], "tensor", 1)], axis=0)
    branch = branch_mine.astype(F32) + branch_theirs.astype(F32)
    output = (tokens.astype(F32) + branch + dense_bias + fc2_bias).astype(BF)
    grads = (
        narrow_share[:, :joined_width],
        narrow_share[:, joined_width:],
        wide_share[:, :unit_width],
        wide_share[:, unit_width:],
    )
    moms = (mom_qkv, mom_dense, mom_fc1, mom_fc2)
    new_moms = [momentum_decay * m + g for m, g in zip(moms, grads)]

    group = n // 4
    slot = unit_width // group
    blocks = []
    for moment in new_moms:
        width = moment.shape[1] // group
        block = moment.astype(BF).reshape(shard_rows, group, width).transpose(1, 0, 2)
        blocks.append(jnp.pad(block, ((0, 0), (0, 0), (0, slot - width))))
    columns = lax.all_to_all(jnp.concatenate(blocks, axis=0), "dp", 0, 0, tiled=True)
    columns = columns.reshape(D, slot)
    grad_normed = normed_mine.astype(F32) + normed_theirs.astype(F32)
    unit_normed, inv_std = normalized(tokens)
    scaled_grad = grad_normed * ln_gain
    grad_tokens = cotangent.astype(F32) + inv_std * (
        scaled_grad
        - jnp.mean(scaled_grad, axis=1, keepdims=True)
        - unit_normed * jnp.mean(scaled_grad * unit_normed, axis=1, keepdims=True)
    )

    row_cotangent = jnp.sum(cotangent.astype(F32), axis=0)
    qkv_bias_grad = lax.dynamic_update_slice_in_dim(
        jnp.zeros((3 * D,), F32),
        jnp.sum(grad_joined.astype(F32), axis=0),
        tensor_index * joined_width,
        0,
    )
    fc1_bias_grad = lax.dynamic_update_slice_in_dim(
        jnp.zeros((FF,), F32),
        jnp.sum(grad_hidden.astype(F32), axis=0),
        tensor_index * unit_width,
        0,
    )
    vector_grad = jnp.concatenate(
        [
            jnp.sum(grad_normed * unit_normed, axis=0),
            jnp.sum(grad_normed, axis=0),
            qkv_bias_grad,
            row_cotangent,
            fc1_bias_grad,
            row_cotangent,
        ]
    )
    bits = []
    bit = 2
    while bit < group:
        bits.append(bit)
        bit *= 2
    columns, vector_grad = lax.optimization_barrier((columns, vector_grad))
    vector_parts = lax.all_to_all(
        vector_grad.reshape(2 * n, share // 2), ("dp", "tensor"), 0, 0, tiled=True
    )
    mine, theirs, vector_parts = sum_over_group(gram(columns), bits, vector_parts)
    ortho = chain(ring.core, mine, theirs, columns)
    pieces = lax.all_to_all(ortho.reshape(n, shard_rows, slot), "dp", 0, 0, tiled=True)
    vector_share = jnp.sum(vector_parts, axis=0)

    masters = (qkv_weight, dense_weight, fc1_weight, fc2_weight)
    new_weights = []
    for index, master in enumerate(masters):
        width = master.shape[1]
        piece = pieces[index * group : (index + 1) * group, :, : width // group]
        piece = piece.transpose(1, 0, 2).reshape(shard_rows, width).astype(F32)
        scale_factor = 0.2 * math.sqrt(max(D, 2 * width))
        new_weights.append(
            master * (1.0 - muon_rate * weight_decay) - muon_rate * scale_factor * piece
        )

    vector_slot = lax.dynamic_slice_in_dim(vectors, tensor_index * (share // 2), share // 2)
    new_first = beta_first * first_moment + (1.0 - beta_first) * vector_share
    new_second = beta_second * second_moment + (1.0 - beta_second) * vector_share * vector_share
    new_vectors = vector_slot - vector_rate * (new_first / (1.0 - beta_first**STEP)) / (
        jnp.sqrt(new_second / (1.0 - beta_second**STEP)) + 1e-08
    )
    return (
        output,
        grad_tokens,
        new_moms[0],
        new_weights[0],
        new_moms[1],
        new_weights[1],
        new_moms[2],
        new_weights[2],
        new_moms[3],
        new_weights[3],
        new_first,
        new_second,
        new_vectors,
    )


def solution(mesh):
    rows = P(("dp", "tensor"), None)
    weight = P("dp", "tensor")
    vector = P(("dp", "tensor"))
    return jax.shard_map(
        per_device,
        mesh=mesh,
        in_specs=(rows, rows, P("dp")) + (weight,) * 4 + (P("dp"),) + (weight,) * 4 + (vector,) * 2,
        out_specs=(rows, rows) + (weight,) * 8 + (vector,) * 3,
        check_vma=False,
    )
```

```python
import math

import jax
import jax.numpy as jnp
from jax import lax
from jax.experimental import pallas as pl
from jax.experimental.pallas import tpu as pltpu
from jax.sharding import PartitionSpec as P

D = 1024
HEADS = 16
FF = 4096
STEP = 10
momentum_decay = 0.95
muon_rate = 0.15
weight_decay = 0.1
vector_rate = 0.4
beta_first = 0.9
beta_second = 0.95
HD=64; ROT=32
F32=jnp.float32; BF=jnp.bfloat16
coef_linear = 3.4445
coef_square = -4.775
coef_cubic = 2.0315

def dot_nt(x, y):
    return lax.dot_general(x, y, (((1,), (1,)), ((), ())), preferred_element_type=F32)

def dot_tn(x, y):
    return lax.dot_general(x, y, (((0,), (0,)), ((), ())), preferred_element_type=F32)

def dot_nn(x, y):
    return jnp.dot(x, y, preferred_element_type=F32)

def tables_kernel(position_ref, frequency_ref, keep_ref, upper_ref, lower_ref):
    half = ROT // 2
    lane = lax.broadcasted_iota(jnp.int32, (1, 2 * HD), 1) % HD
    angles = position_ref[...].astype(F32) * frequency_ref[...]
    cosine, sine = jnp.cos(angles), jnp.sin(angles)
    keep_ref[...] = jnp.where(lane < ROT, cosine, 1.0)
    upper_ref[...] = jnp.where(lane < half, -sine, 0.0)
    lower_ref[...] = jnp.where((lane >= half) & (lane < ROT), sine, 0.0)

def rope_tables(positions):
    half = ROT // 2
    frequency = 10000.0 ** (-2.0 * jnp.arange(half, dtype=F32) / ROT)
    table = jax.ShapeDtypeStruct((positions.shape[0], 2 * HD), F32)
    return pl.pallas_call(
        tables_kernel,
        out_shape=[table] * 3,
        cost_estimate=pl.CostEstimate(flops=10**9, bytes_accessed=2 * 10**7, transcendentals=0),
        name="rope_tables",
    )(positions[:, None], jnp.tile(frequency, 2 * HD // half)[None])

ROWS = 256

def attention_kernel(lo_ref, x_ref, b_ref, g_ref, keep_ref, upper_ref, lower_ref, *refs):
    (att_ref, out_ref, sum_ref, bias_ref, s_ref, top_ref, o_ref, ge_ref, q_ref, k_ref, v_ref,
     dk_ref, dv_ref, dq_ref) = refs[-14:]
    seq = x_ref.shape[0]
    width = 2 * HD
    lane = lax.broadcasted_iota(jnp.int32, (1, width), 1)
    first = lane < HD
    mine = (first, ~first)
    half = ROT // 2
    blocks = seq // ROWS
    @pl.when(pl.program_id(0) == 0)
    def _():
        for i in range(blocks):
            r0, n = i * ROWS, (i + 1) * ROWS
            col = lax.broadcasted_iota(jnp.int32, (ROWS, n), 1)
            row = lax.broadcasted_iota(jnp.int32, (ROWS, n), 0) + r0
            allowed = (col >= lo_ref[r0:n, :]) & (col <= row)
            bias_ref[r0:n, :n] = jnp.where(allowed, 0.0, -1e30)
    def rotated(values, sign):
        up = pltpu.roll(values, width - half, 1) * upper_ref[...]
        down = pltpu.roll(values, half, 1) * lower_ref[...]
        return values * keep_ref[...] + (up + down) * sign
    scale = HD ** -0.5
    def swapped(row):
        return pltpu.roll(jnp.broadcast_to(row, (8, width)), HD, 1)[:1]
    b0, b1, b2 = (b_ref[0, :, c * width:(c + 1) * width] for c in range(3))
    q = rotated(x_ref[:, :width] + jnp.where(first, b0, b1), 1.0) * scale
    bias_k = jnp.where(first, swapped(b0), swapped(b2))
    k_ref[...] = rotated(x_ref[:, width:2 * width] + bias_k, 1.0).astype(BF)
    v = x_ref[:, 2 * width:] + jnp.where(first, b1, b2)
    for h in range(2):
        q_ref[h] = jnp.where(mine[h], q, 0.0).astype(BF)
        spare = lane - (1 - h) * HD
        v_ref[h] = jnp.where(mine[h], v, jnp.where((spare == 0) | (spare == 1), 1.0, 0.0)).astype(BF)
    units = [(h, i) for i in range(blocks) for h in range(2)]
    def spans(i):
        return slice(i * ROWS, (i + 1) * ROWS), (i + 1) * ROWS
    for h, i in units:
        rows, n = spans(i)
        s = dot_nt(q_ref[h, rows, :], k_ref[:n, :]) + bias_ref[rows, :n]
        s_ref[h, rows, :n] = s
        m = s[:, :width]
        for c in range(width, n, width):
            m = jnp.maximum(m, s[:, c:c + width])
        top_ref[h, rows, :] = m
    for h in range(2):
        top_ref[h] = jnp.broadcast_to(jnp.max(top_ref[h], axis=1, keepdims=True), (seq, width))
    for h, i in units:
        rows, n = spans(i)
        e = jnp.exp(s_ref[h, rows, :n] - top_ref[h, rows, :1])
        s_ref[h, rows, :n] = e
        o_ref[h, rows, :] = dot_nn(e.astype(BF), v_ref[h, :n, :])
    atts = []
    g = g_ref[...].astype(F32)
    for h in range(2):
        o = o_ref[h]
        at = (1 - h) * HD
        inv = 1.0 / o[:, at:at + 1]
        att = jnp.where(mine[h], o * inv, 0.0)
        atts.append(att)
        gs = jnp.where(mine[h], g * inv, 0.0).astype(BF).astype(F32)
        delta = jnp.sum(gs * att, axis=1, keepdims=True)
        dh = delta.astype(BF).astype(F32)
        ge_ref[h] = jnp.where(lane == at, -dh, jnp.where(lane == at + 1, dh - delta, gs)).astype(BF)
    att_ref[...] = jnp.where(first, atts[0], atts[1]).astype(BF)
    dk_ref[...] = jnp.zeros_like(dk_ref)
    dv_ref[...] = jnp.zeros_like(dv_ref)
    for h, i in units:
        rows, n = spans(i)
        e = s_ref[h, rows, :n]
        ge = ge_ref[h, rows, :]
        ds = (e * dot_nt(ge, v_ref[h, :n, :])).astype(BF)
        dq = dot_nn(ds, k_ref[:n, :]) * scale
        dq_ref[rows, :] = dq if h == 0 else jnp.where(first, dq_ref[rows, :], dq)
        dk_ref[:n, :] += dot_tn(ds, q_ref[h, rows, :])
        dv_ref[h, :n, :] += dot_tn(e.astype(BF), ge)
    sums = []
    values = (rotated(dq_ref[...], -1.0), rotated(dk_ref[...], -1.0), jnp.where(first, dv_ref[0], dv_ref[1]))
    for c, value in enumerate(values):
        low = value.astype(BF)
        out_ref[:, c * width:(c + 1) * width] = low
        sums.append(jnp.sum(low.astype(F32), axis=0, keepdims=True))
    sq, sk, sv = sums
    sum_ref[0, :, :width] = jnp.where(first, sq, swapped(sk))
    sum_ref[0, :, width:2 * width] = jnp.where(first, sv, sq)
    sum_ref[0, :, 2 * width:] = jnp.where(first, swapped(sk), sv)


def attention_tables(positions):
    lo = (jnp.arange(positions.shape[0], dtype=jnp.int32) - positions)[:, None]
    return (lo, *rope_tables(positions))

def attention(tables, joined, bias, grad_att, start, count, before=()):
    lo, keep, upper, lower = tables
    seq, width = joined.shape
    pairs = width // (6 * HD)
    whole = lambda w: pl.BlockSpec((seq, w), lambda h: (0, 0))
    part = lambda w: pl.BlockSpec((seq, w), lambda h: (0, h + start))
    line = pl.BlockSpec((1, 1, 6 * HD), lambda h: (h + start, 0, 0))
    one = lambda dtype: pltpu.VMEM((seq, 2 * HD), dtype)
    two = lambda dtype: pltpu.VMEM((2, seq, 2 * HD), dtype)
    tables = [whole(2 * HD)] * 3
    return pl.pallas_call(
        attention_kernel,
        grid=(count,),
        in_specs=[whole(1), part(6 * HD), line, part(2 * HD)] + tables
        + [pl.BlockSpec(memory_space=pl.ANY)] * len(before),
        out_specs=[part(2 * HD), part(6 * HD), line],
        out_shape=[
            jax.ShapeDtypeStruct((seq, pairs * 2 * HD), BF),
            jax.ShapeDtypeStruct((seq, width), BF),
            jax.ShapeDtypeStruct((pairs, 1, 6 * HD), F32),
        ],
        input_output_aliases={7 + i: i for i in range(len(before))},
        scratch_shapes=[pltpu.VMEM((seq, seq), F32), pltpu.VMEM((2, seq, seq), F32)]
        + [two(F32), two(F32), two(BF), two(BF), one(BF), two(BF), one(F32), two(F32), one(F32)],
        compiler_params=pltpu.CompilerParams(vmem_limit_bytes=48 * 2**20),
        cost_estimate=pl.CostEstimate(flops=10**10, bytes_accessed=4 * 10**7, transcendentals=0),
        name="attention_both",
    )(lo, joined, bias.reshape(pairs, 1, 6 * HD), grad_att, keep, upper, lower, *before)

def permute(x):
    y = x.reshape(*x.shape[:-1], -1, 2, 3, HD)
    return jnp.swapaxes(y, -3, -2).reshape(x.shape)
def unpermute(x):
    y = x.reshape(*x.shape[:-1], -1, 3, 2, HD)
    return jnp.swapaxes(y, -3, -2).reshape(x.shape)

BAND = 128

def gram_kernel(core_ref, x_ref, keep_ref, give_ref, twice_ref):
    size = x_ref.shape[0]
    span = keep_ref.shape[1]
    twice_ref[:size, :] = x_ref[...]
    twice_ref[size:, :] = x_ref[: span - BAND, :]
    def half(out_ref, start):
        for r in range(0, size // 2, BAND):
            band = twice_ref[pl.ds(start + r, BAND), :]
            out_ref[r:r + BAND, :] = dot_nt(band, twice_ref[pl.ds(start + r, span), :])
    start = pl.multiple_of(core_ref[0] * (size // 2), size // 2)
    half(give_ref, pl.multiple_of(size // 2 - start, size // 2))
    half(keep_ref, start)

def gram(core, x):
    size, width = x.shape
    span = size // 2 + BAND
    half = jax.ShapeDtypeStruct((size // 2, span), F32)
    spec = pl.BlockSpec(memory_space=pltpu.VMEM)
    return pl.pallas_call(
        gram_kernel,
        out_shape=[half, half],
        in_specs=[pl.BlockSpec(memory_space=pltpu.SMEM), spec],
        out_specs=[spec, spec],
        scratch_shapes=[pltpu.VMEM((size + span - BAND, width), BF)],
        compiler_params=pltpu.CompilerParams(vmem_limit_bytes=32 * 2**20),
        name="gram",
    )(core.reshape(1), x)

def chain_kernel(core_ref, mine_ref, theirs_ref, x0_ref, out_ref, a_ref, ah_ref, m_ref, u_ref, uh_ref, xa_ref):
    size = x0_ref.shape[0]
    bands = size // BAND
    row = lax.broadcasted_iota(jnp.int32, (size // 2, BAND), 0)
    col = lax.broadcasted_iota(jnp.int32, (size // 2, BAND), 1)
    diagonal = mine_ref[:, :BAND] + theirs_ref[:, :BAND]
    trace = jnp.sum(jnp.where(row % BAND == col, diagonal, 0.0))
    norm = jnp.sqrt(trace) + 1e-07
    scale = 1.0 / (norm * norm)
    def store(rs, cs, block):
        a_ref[rs, cs] = block
        ah_ref[rs, cs] = block.astype(BF)
    def unpack(half_ref, start):
        for i in range(start, start + bands // 2):
            r = (i - start) * BAND
            for o in range(bands // 2 + 1):
                j = (i + o) % bands
                block = half_ref[r:r + BAND, o * BAND:(o + 1) * BAND] * scale
                store(slice(i * BAND, (i + 1) * BAND), slice(j * BAND, (j + 1) * BAND), block)
                if 0 < o < bands // 2:
                    store(slice(j * BAND, (j + 1) * BAND), slice(i * BAND, (i + 1) * BAND), block.T)
    @pl.when(core_ref[0] == 0)
    def _():
        unpack(mine_ref, 0)
        unpack(theirs_ref, bands // 2)
    @pl.when(core_ref[0] == 1)
    def _():
        unpack(theirs_ref, 0)
        unpack(mine_ref, bands // 2)
    xa_ref[...] = x0_ref[...]
    lin = coef_linear
    def turn(k, last):
        inv = jnp.where(k == 0, 1.0 / norm, 1.0)
        for r0 in range(0, size, ROWS):
            r, c = slice(r0, r0 + ROWS), slice(r0, size)
            s = dot_nn(ah_ref[r, :], ah_ref[:, c])
            m = (coef_square * ah_ref[r, c].astype(F32) + coef_cubic * s).astype(BF)
            m_ref[r, c] = m
            if r0 + ROWS < size:
                m_ref[r0 + ROWS:, r] = m[:, ROWS:].T
        for r0 in range(0, size, 2 * ROWS):
            r = slice(r0, r0 + (2 * ROWS))
            out_ref[r, :] = ((lin * xa_ref[r, :].astype(F32) + dot_nn(m_ref[r, :], xa_ref[...])) * inv).astype(BF)
        if last:
            return
        xa_ref[...] = out_ref[...]
        for r0 in range(0, size, 2 * ROWS):
            r = slice(r0, r0 + 2 * ROWS)
            u = lin * a_ref[r, :] + dot_nn(m_ref[r, :], ah_ref[...])
            u_ref[r, :] = u
            uh_ref[r, :] = u.astype(BF)
        for r0 in range(0, size, ROWS):
            r, c = slice(r0, r0 + ROWS), slice(r0, size)
            block = lin * u_ref[r, c] + dot_nn(uh_ref[r, :], m_ref[:, c])
            store(r, c, block)
            if r0 + ROWS < size:
                store(slice(r0 + ROWS, size), r, block[:, ROWS:].T)
    def body(k, _):
        turn(k, False)
        return 0
    lax.fori_loop(0, 4, body, 0)
    turn(4, True)
def chain(core, mine, theirs, x0):
    size, width = x0.shape
    V = lambda dt: pltpu.VMEM((size, size), dt)
    spec = pl.BlockSpec(memory_space=pltpu.VMEM)
    return pl.pallas_call(
        chain_kernel,
        out_shape=jax.ShapeDtypeStruct((size, width), BF),
        in_specs=[pl.BlockSpec(memory_space=pltpu.SMEM)] + [spec] * 3, out_specs=spec,
        scratch_shapes=[V(F32), V(BF), V(BF), V(F32), V(BF), pltpu.VMEM((size, width), BF)],
        compiler_params=pltpu.CompilerParams(vmem_limit_bytes=56 * 2**20),
        name="orthogonalize",
    )(core.reshape(1), mine, theirs, x0)

def assemble(core, position, mine, theirs, widths):
    count = len(mine)
    rows = mine[0].shape[0]
    n = 2 * count
    def kernel(core_ref, position_ref, *refs):
        blocks, outs = refs[:n], refs[n:]
        for k in range(n):
            which = core_ref[0] if k < count else 1 - core_ref[0]
            place = position_ref[0] + k % count
            place = jnp.where(place < count, place, place - count)
            chip = jnp.where(place < count // 2, 2 * place, 2 * (count - 1 - place) + 1)
            span = pl.ds(pl.multiple_of((chip * 2 + which) * rows, rows), rows)
            start = 0
            for out, w in zip(outs, widths):
                out[span, :] = blocks[k][:, start:start + w]
                start += w
    vmem, smem = pl.BlockSpec(memory_space=pltpu.VMEM), pl.BlockSpec(memory_space=pltpu.SMEM)
    return pl.pallas_call(
        kernel,
        out_shape=[jax.ShapeDtypeStruct((n * rows, w), BF) for w in widths],
        in_specs=[smem, smem] + [vmem] * n,
        out_specs=[vmem] * len(widths),
        compiler_params=pltpu.CompilerParams(vmem_limit_bytes=48 * 2**20),
        name="assemble",
    )(core.reshape(1), position.reshape(1), *mine, *theirs)

def whole_call(kernel, name, out_shape, *args, scalars=0, scratch=(), limit=48):
    vmem, smem = pl.BlockSpec(memory_space=pltpu.VMEM), pl.BlockSpec(memory_space=pltpu.SMEM)
    args = [a.reshape(1) if i < scalars else a for i, a in enumerate(args)]
    return pl.pallas_call(
        kernel,
        out_shape=out_shape,
        in_specs=[smem] * scalars + [vmem] * (len(args) - scalars),
        out_specs=[vmem] * len(out_shape),
        scratch_shapes=list(scratch),
        compiler_params=pltpu.CompilerParams(vmem_limit_bytes=limit * 2**20),
        name=name,
    )(*args)

def momentum(decay, narrow, wide, moms, group):
    rows = moms[0].shape[0]
    widths = [m.shape[1] for m in moms]
    slot = max(widths) // group
    def kernel(*refs):
        narrow_refs, wide_refs, mom_refs, new_refs, out_ref = refs[:3], refs[3:6], refs[6:10], refs[10:14], refs[14]
        def total(parts, c, w):
            return sum(p[:, c:c + w].astype(F32) for p in parts)
        first = lax.broadcasted_iota(jnp.int32, (1, 2 * HD), 1) < HD
        for c in range(0, widths[0], 6 * HD):
            q, k, v = (total(narrow_refs, c + i * 2 * HD, 2 * HD) for i in range(3))
            k = pltpu.roll(k, HD, 1)
            parts = (jnp.where(first, q, k), jnp.where(first, v, q), jnp.where(first, k, v))
            for i, part in enumerate(parts):
                s = slice(c + i * 2 * HD, c + (i + 1) * 2 * HD)
                new_refs[0][:, s] = decay * mom_refs[0][:, s] + part
        new_refs[1][...] = decay * mom_refs[1][...] + total(narrow_refs, widths[0], widths[1])
        new_refs[2][...] = decay * mom_refs[2][...] + total(wide_refs, 0, widths[2])
        new_refs[3][...] = decay * mom_refs[3][...] + total(wide_refs, widths[2], widths[3])
        for m, new in enumerate(new_refs):
            w = widths[m] // group
            for j in range(group):
                block = new[:, j * w:(j + 1) * w].astype(BF)
                if w < slot:
                    block = jnp.concatenate([block, jnp.zeros((rows, slot - w), BF)], axis=1)
                out_ref[m * group + j] = block
    shapes = [jax.ShapeDtypeStruct(m.shape, F32) for m in moms]
    shapes.append(jax.ShapeDtypeStruct((4 * group, rows, slot), BF))
    return whole_call(kernel, "momentum", shapes, *narrow, *wide, *moms)

def update(pieces, masters, keep, rates, group):
    def kernel(piece_ref, *refs):
        for m in range(4):
            master, new = refs[m], refs[4 + m]
            w = master.shape[1] // group
            for j in range(group):
                s = slice(j * w, (j + 1) * w)
                new[:, s] = master[:, s] * keep - rates[m] * piece_ref[m * group + j, :, :w].astype(F32)
    shapes = [jax.ShapeDtypeStruct(m.shape, F32) for m in masters]
    return whole_call(kernel, "update", shapes, pieces, *masters)

def gelu_and_slope(v):
    root = math.sqrt(2.0 / math.pi)
    square = v * v
    half = 0.5 * jnp.tanh(v * (root + (root * 0.044715) * square)) + 0.5
    value = v * half
    return value, half + value * (1.0 - half) * (2.0 * root + (6.0 * root * 0.044715) * square)


def other(x, axis, bit):
    n = lax.axis_size(axis)
    return lax.ppermute(x, axis, [(i, i ^ bit) for i in range(n)])


def in_order(mine, theirs, index, axis=0):
    low = jnp.where(index == 0, mine, theirs)
    high = jnp.where(index == 0, theirs, mine)
    return jnp.concatenate([low, high], axis=axis)


class Ring:
    def __init__(self):
        n = lax.axis_size("dp")
        self.count = n // 2
        rows = self.count // 2
        order = [2 * i for i in range(rows)] + [2 * i + 1 for i in reversed(range(rows))]
        index = lax.axis_index("dp")
        self.core = index % 2
        chip = index // 2
        self.position = jnp.where(chip % 2 == 0, chip // 2, self.count - 1 - chip // 2)
        self.up_pairs = [
            (2 * order[i] + c, 2 * order[(i + 1) % self.count] + c)
            for i in range(self.count)
            for c in range(2)
        ]
        self.down_pairs = [(b, a) for a, b in self.up_pairs]

    def chip(self, step):
        place = (self.position + step % self.count) % self.count
        return jnp.where(place < self.count // 2, 2 * place, 2 * (self.count - 1 - place) + 1)

    def up(self, x):
        return lax.ppermute(x, "dp", self.up_pairs)

    def down(self, x):
        return lax.ppermute(x, "dp", self.down_pairs)

    def gather(self, shard, rides, positions):
        rows = shard.shape[0]
        half, cut = self.count // 2, rows // 32 * 16 or rows // 2
        mine = {0: shard}
        rising = falling = shard
        for step in range(half):
            if step == half - 1:
                rising, falling = rising[:cut], falling[cut:]
            rising, falling = self.up(rising), self.down(falling)
            if step < len(rides):
                ride = other(rides[step], "tensor", 1)
                if step == 1:
                    tables = attention_tables(positions)
                    rising, falling, tables = lax.optimization_barrier((rising, falling, tables))
                rising, falling, rides[step] = lax.optimization_barrier((rising, falling, ride))
                if step == 0:
                    rising, positions = lax.optimization_barrier((rising, positions))
            if step < half - 1:
                mine[self.count - 1 - step], mine[1 + step] = rising, falling
        mine[half] = jnp.concatenate([rising, falling], axis=0)
        mine = [mine[k] for k in range(self.count)]
        return mine, [other(block, "dp", 1) for block in mine], tables

    def split(self, values, rows):
        parts = values.reshape(values.shape[0], self.count, 2, rows)
        return tuple(
            lax.dynamic_index_in_dim(parts, c, 2, False).reshape(values.shape[0], -1)
            for c in (self.core, 1 - self.core)
        )

    def pair_sum(self, lefts, right):
        keep, give = lefts
        theirs = other(dot_tn(give, right).astype(BF), "dp", 1)
        return (dot_tn(keep, right) + theirs.astype(F32)).astype(BF)

    def sweep(self, send, work, state):
        going, state = lax.optimization_barrier(([chain.outgoing() for chain in send], state))
        coming = [(self.up(rising), self.down(falling)) for rising, falling in going]
        coming, state = lax.optimization_barrier((coming, work(state)))
        for chain, received in zip(send, coming):
            chain.received = received
        return state


class Chain:
    def __init__(self, ring, sums):
        self.ring, self.sums, self.received = ring, sums, None
        self.rows = sums[0].shape[0] // ring.count
        self.cut = self.rows // 32 * 16 or self.rows // 2
        self.left = ring.count // 2

    def block(self, step):
        start = self.ring.chip(step) * self.rows
        parts = [lax.dynamic_slice_in_dim(s, start, self.rows, 0) for s in self.sums]
        return jnp.concatenate(parts, axis=1)

    def outgoing(self):
        step, cut = self.left, self.cut
        self.left -= 1
        if self.received is None:
            far = self.block(step)
            return far[:cut], far[cut:]
        low, high = self.block(step).astype(F32), self.block(-step).astype(F32)
        rising, falling = (r.astype(F32) for r in self.received)
        if rising.shape[0] < self.rows:
            low = jnp.concatenate([low[:cut] + rising, low[cut:]], axis=0)
            high = jnp.concatenate([high[:cut], high[cut:] + falling], axis=0)
        else:
            low, high = low + rising, high + falling
        return low.astype(BF), high.astype(BF)

    def parts(self):
        return (self.block(0), *self.received)


def sum_over_group(core, columns, bits, tie):
    keep, give = gram(core, columns)
    rows = keep.shape[0]
    keep = keep + other(give, "dp", 1)
    pieces = [keep[: rows // 2], keep[rows // 2 :]]
    steps = [("dp", b) for b in bits] + [("tensor", 1)]
    for turn in range(len(steps)):
        if turn == len(steps) - 1:
            pieces, tie = lax.optimization_barrier((pieces, tie))
        axis, bit = steps[turn]
        first = other(pieces[0], axis, bit)
        axis, bit = steps[len(steps) - 1 - turn]
        second = other(pieces[1], axis, bit)
        pieces = [pieces[0] + first, pieces[1] + second]
    half = jnp.concatenate(pieces, axis=0)
    return half, other(half, "dp", 1), tie


def per_device(
    tokens,
    cotangent,
    positions,
    qkv_weight,
    dense_weight,
    fc1_weight,
    fc2_weight,
    vectors,
    mom_qkv,
    mom_dense,
    mom_fc1,
    mom_fc2,
    first_moment,
    second_moment,
):
    tensor_index = lax.axis_index("tensor")
    n = lax.axis_size("dp")
    ring = Ring()
    joined_width = 3 * D // 2
    unit_width = FF // 2
    shard_rows = qkv_weight.shape[0]
    half_rows = tokens.shape[0]
    seq = 2 * half_rows

    share = vectors.shape[0]
    lines = share // shard_rows
    spare = 128 - lines
    vec_pad = jnp.pad(vectors.astype(BF).reshape(shard_rows, lines), ((0, 0), (0, spare)))
    first_pack = jnp.concatenate(
        [fc1_weight.astype(BF), fc2_weight.astype(BF), dense_weight.astype(BF), vec_pad], axis=1
    )
    second_pack = permute(qkv_weight.astype(BF))
    quarter = half_rows // 2
    quarter = half_rows // 2
    rides = [tokens[:quarter], tokens[quarter:], cotangent[:quarter], cotangent[quarter:]]
    mine, theirs, tables = ring.gather(first_pack, rides, positions)
    second_pack, rides[2] = lax.optimization_barrier((second_pack, rides[2]))
    full_qkv = lax.all_gather(second_pack, "dp", axis=0, tiled=True)
    tokens_theirs = jnp.concatenate(rides[:2], axis=0)
    cotangent_theirs = jnp.concatenate(rides[2:], axis=0)
    widths = (unit_width, unit_width, D // 2, lines + spare)
    full_fc1, full_fc2, full_dense, lines_full = assemble(
        ring.core, ring.position, mine, theirs, widths
    )
    vector_full = lines_full[:, :lines].reshape(-1).astype(F32)

    ln_gain = vector_full[:D]
    ln_shift = vector_full[D : 2 * D]
    qkv_bias = lax.dynamic_slice_in_dim(
        vector_full, 2 * D + tensor_index * joined_width, joined_width
    )
    dense_bias = vector_full[5 * D : 6 * D]
    fc1_bias = lax.dynamic_slice_in_dim(vector_full, 6 * D + tensor_index * unit_width, unit_width)
    fc2_bias = vector_full[6 * D + FF :]

    tokens_all = in_order(tokens, tokens_theirs, tensor_index)
    cotangent_all = in_order(cotangent, cotangent_theirs, tensor_index)

    def normalized(rows):
        values = rows.astype(F32)
        centred = values - jnp.mean(values, axis=1, keepdims=True)
        inv_std = lax.rsqrt(jnp.mean(centred * centred, axis=1, keepdims=True) + 1e-05)
        return centred * inv_std, inv_std

    normed_all = (normalized(tokens_all)[0] * ln_gain + ln_shift).astype(BF)
    normed_parts = ring.split(normed_all, shard_rows)
    cotangent_parts = ring.split(cotangent_all, shard_rows)
    hidden = dot_nn(normed_all, full_fc1) + fc1_bias
    activation, slope = (v.astype(BF) for v in gelu_and_slope(hidden))
    grad_act = dot_nn(cotangent_all, full_fc2)
    grad_hidden = (grad_act * slope.astype(F32)).astype(BF)
    wide_sums = [
        ring.pair_sum(normed_parts, grad_hidden),
        ring.pair_sum(cotangent_parts, activation),
    ]

    def project(state):
        normed_all, cotangent_all, full_qkv, full_dense = state
        return dot_nn(normed_all, full_qkv), dot_nn(cotangent_all, full_dense).astype(BF)

    pairs = joined_width // (6 * HD)

    def attend_some(state):
        joined, grad_attended = state
        return joined, grad_attended, *attention(tables, joined, qkv_bias, grad_attended, 0, pairs // 2)

    def attend_rest(state):
        joined, grad_attended, *before = state
        return attention(
            tables, joined, qkv_bias, grad_attended, pairs // 2, pairs - pairs // 2, before
        )

    def sum_narrow(state):
        attended, grad_joined, qkv_bias_sum = state
        sums = [
            ring.pair_sum(normed_parts, grad_joined),
            ring.pair_sum(cotangent_parts, attended),
        ]
        return attended, grad_joined, qkv_bias_sum, sums

    def sum_normed(state):
        attended, activation, grad_joined, grad_hidden = state
        partial = (dot_nt(grad_joined, full_qkv) + dot_nt(grad_hidden, full_fc1)).astype(BF)
        return attended, activation, across(partial)

    def sum_branch(state):
        attended, activation, normed = state
        partial = (dot_nt(attended, full_dense) + dot_nt(activation, full_fc2)).astype(BF)
        return across(partial), normed

    def across(partial):
        mine = lax.dynamic_slice_in_dim(partial, tensor_index * half_rows, half_rows, 0)
        theirs = lax.dynamic_slice_in_dim(partial, (1 - tensor_index) * half_rows, half_rows, 0)
        return mine, theirs

    def run(chain, works, state):
        for step in range(ring.count // 2):
            work = works[step] if step < len(works) else lambda state: state
            state = ring.sweep([chain], work, state)
        return state

    wide = Chain(ring, wide_sums)
    works = (project, attend_some, attend_rest, sum_narrow)
    state = run(wide, works, (normed_all, cotangent_all, full_qkv, full_dense))
    attended, grad_joined, qkv_bias_sum, narrow_sums = state
    narrow = Chain(ring, narrow_sums)
    state = (attended, activation, grad_joined, grad_hidden)
    branch, normed = run(narrow, (lambda state: state, sum_normed, sum_branch), state)
    branch_mine, branch_theirs = branch
    normed_mine, normed_theirs = normed[0], other(normed[1], "tensor", 1)
    moms = (mom_qkv, mom_dense, mom_fc1, mom_fc2)
    group = n // 4
    slot = unit_width // group
    *new_moms, blocks = momentum(momentum_decay, narrow.parts(), wide.parts(), moms, group)
    columns = lax.all_to_all(blocks, "dp", 0, 0, tiled=True)
    columns = columns.reshape(D, slot)
    grad_normed = normed_mine.astype(F32) + normed_theirs.astype(F32)
    unit_normed, inv_std = normalized(tokens)
    scaled_grad = grad_normed * ln_gain
    grad_tokens = cotangent.astype(F32) + inv_std * (
        scaled_grad
        - jnp.mean(scaled_grad, axis=1, keepdims=True)
        - unit_normed * jnp.mean(scaled_grad * unit_normed, axis=1, keepdims=True)
    )

    row_cotangent = jnp.sum(cotangent.astype(F32), axis=0)
    qkv_bias_grad = lax.dynamic_update_slice_in_dim(
        jnp.zeros((3 * D,), F32),
        qkv_bias_sum.reshape(-1),
        tensor_index * joined_width,
        0,
    )
    fc1_bias_grad = lax.dynamic_update_slice_in_dim(
        jnp.zeros((FF,), F32),
        jnp.sum(grad_hidden.astype(F32), axis=0),
        tensor_index * unit_width,
        0,
    )
    vector_grad = jnp.concatenate(
        [
            jnp.sum(grad_normed * unit_normed, axis=0),
            jnp.sum(grad_normed, axis=0),
            qkv_bias_grad,
            row_cotangent,
            fc1_bias_grad,
            row_cotangent,
        ]
    )
    bits = []
    bit = 2
    while bit < group:
        bits.append(bit)
        bit *= 2
    columns, vector_grad = lax.optimization_barrier((columns, vector_grad))
    vector_parts = lax.all_to_all(
        vector_grad.reshape(2 * n, share // 2), ("dp", "tensor"), 0, 0, tiled=True
    )
    mine, theirs, vector_parts = sum_over_group(ring.core, columns, bits, vector_parts)
    branch_theirs, mine = lax.optimization_barrier((branch_theirs, mine))
    ortho = chain(ring.core, mine, theirs, columns)
    ortho, branch_theirs = lax.optimization_barrier((ortho, other(branch_theirs, "tensor", 1)))
    branch = branch_mine.astype(F32) + branch_theirs.astype(F32)
    output = (tokens.astype(F32) + branch + dense_bias + fc2_bias).astype(BF)
    pieces = lax.all_to_all(ortho.reshape(n, shard_rows, slot), "dp", 0, 0, tiled=True)
    vector_share = jnp.sum(vector_parts, axis=0)

    masters = (qkv_weight, dense_weight, fc1_weight, fc2_weight)
    rates = [muon_rate * 0.2 * math.sqrt(max(D, 2 * m.shape[1])) for m in masters]
    new_weights = update(pieces, masters, 1.0 - muon_rate * weight_decay, rates, group)

    vector_slot = lax.dynamic_slice_in_dim(vectors, tensor_index * (share // 2), share // 2)
    new_first = beta_first * first_moment + (1.0 - beta_first) * vector_share
    new_second = beta_second * second_moment + (1.0 - beta_second) * vector_share * vector_share
    new_vectors = vector_slot - vector_rate * (new_first / (1.0 - beta_first**STEP)) / (
        jnp.sqrt(new_second / (1.0 - beta_second**STEP)) + 1e-08
    )
    return (
        output,
        grad_tokens,
        new_moms[0],
        new_weights[0],
        new_moms[1],
        new_weights[1],
        new_moms[2],
        new_weights[2],
        new_moms[3],
        new_weights[3],
        new_first,
        new_second,
        new_vectors,
    )


def solution(mesh):
    rows = P(("dp", "tensor"), None)
    weight = P("dp", "tensor")
    vector = P(("dp", "tensor"))
    return jax.shard_map(
        per_device,
        mesh=mesh,
        in_specs=(rows, rows, P("dp")) + (weight,) * 4 + (P("dp"),) + (weight,) * 4 + (vector,) * 2,
        out_specs=(rows, rows) + (weight,) * 8 + (vector,) * 3,
        check_vma=False,
    )
```

```python
import math

import jax
import jax.numpy as jnp
from jax import lax
from jax.experimental import pallas as pl
from jax.experimental.pallas import tpu as pltpu
from jax.sharding import PartitionSpec as P

D = 1024
HEADS = 16
FF = 4096
STEP = 10
momentum_decay = 0.95
muon_rate = 0.15
weight_decay = 0.1
vector_rate = 0.4
beta_first = 0.9
beta_second = 0.95
HD=64; ROT=32
F32=jnp.float32; BF=jnp.bfloat16
coef_linear = 3.4445
coef_square = -4.775
coef_cubic = 2.0315

def dot_nt(x, y):
    return lax.dot_general(x, y, (((1,), (1,)), ((), ())), preferred_element_type=F32)

def dot_tn(x, y):
    return lax.dot_general(x, y, (((0,), (0,)), ((), ())), preferred_element_type=F32)

def dot_nn(x, y):
    return jnp.dot(x, y, preferred_element_type=F32)

def tables_kernel(position_ref, frequency_ref, keep_ref, upper_ref, lower_ref):
    half = ROT // 2
    lane = lax.broadcasted_iota(jnp.int32, (1, 2 * HD), 1) % HD
    angles = position_ref[...].astype(F32) * frequency_ref[...]
    cosine, sine = jnp.cos(angles), jnp.sin(angles)
    keep_ref[...] = jnp.where(lane < ROT, cosine, 1.0)
    upper_ref[...] = jnp.where(lane < half, -sine, 0.0)
    lower_ref[...] = jnp.where((lane >= half) & (lane < ROT), sine, 0.0)

def rope_tables(positions):
    half = ROT // 2
    frequency = 10000.0 ** (-2.0 * jnp.arange(half, dtype=F32) / ROT)
    table = jax.ShapeDtypeStruct((positions.shape[0], 2 * HD), F32)
    return pl.pallas_call(
        tables_kernel,
        out_shape=[table] * 3,
        cost_estimate=pl.CostEstimate(flops=10**9, bytes_accessed=2 * 10**7, transcendentals=0),
        name="rope_tables",
    )(positions[:, None], jnp.tile(frequency, 2 * HD // half)[None])

ROWS = 256

def attention_kernel(lo_ref, x_ref, b_ref, g_ref, keep_ref, upper_ref, lower_ref, *refs):
    (att_ref, out_ref, sum_ref, bias_ref, s_ref, e_ref, top_ref, o_ref, ge_ref, q_ref, k_ref, v_ref,
     dk_ref, dv_ref, dq_ref) = refs[-15:]
    seq = x_ref.shape[0]
    width = 2 * HD
    lane = lax.broadcasted_iota(jnp.int32, (1, width), 1)
    first = lane < HD
    mine = (first, ~first)
    half = ROT // 2
    blocks = seq // ROWS
    @pl.when(pl.program_id(0) == 0)
    def _():
        for i in range(blocks):
            r0, n = i * ROWS, (i + 1) * ROWS
            col = lax.broadcasted_iota(jnp.int32, (ROWS, n), 1)
            row = lax.broadcasted_iota(jnp.int32, (ROWS, n), 0) + r0
            allowed = (col >= lo_ref[r0:n, :]) & (col <= row)
            bias_ref[r0:n, :n] = jnp.where(allowed, 0.0, -1e30)
    def rotated(values, sign):
        up = pltpu.roll(values, width - half, 1) * upper_ref[...]
        down = pltpu.roll(values, half, 1) * lower_ref[...]
        return values * keep_ref[...] + (up + down) * sign
    scale = HD ** -0.5
    def swapped(row):
        return pltpu.roll(jnp.broadcast_to(row, (8, width)), HD, 1)[:1]
    b0, b1, b2 = (b_ref[0, :, c * width:(c + 1) * width] for c in range(3))
    q = rotated(x_ref[:, :width] + jnp.where(first, b0, b1), 1.0) * scale
    bias_k = jnp.where(first, swapped(b0), swapped(b2))
    k_ref[...] = rotated(x_ref[:, width:2 * width] + bias_k, 1.0).astype(BF)
    v = x_ref[:, 2 * width:] + jnp.where(first, b1, b2)
    for h in range(2):
        q_ref[h] = jnp.where(mine[h], q, 0.0).astype(BF)
        spare = lane - (1 - h) * HD
        v_ref[h] = jnp.where(mine[h], v, jnp.where((spare == 0) | (spare == 1), 1.0, 0.0)).astype(BF)
    units = [(h, i) for i in range(blocks) for h in range(2)]
    def spans(i):
        return slice(i * ROWS, (i + 1) * ROWS), (i + 1) * ROWS
    for h, i in units:
        rows, n = spans(i)
        s = dot_nt(q_ref[h, rows, :], k_ref[:n, :]) + bias_ref[rows, :n]
        s_ref[h, rows, :n] = s
        m = s[:, :width]
        for c in range(width, n, width):
            m = jnp.maximum(m, s[:, c:c + width])
        top_ref[h, rows, :] = m
    for h in range(2):
        top_ref[h] = jnp.broadcast_to(jnp.max(top_ref[h], axis=1, keepdims=True), (seq, width))
    for h, i in units:
        rows, n = spans(i)
        e = jnp.exp(s_ref[h, rows, :n] - top_ref[h, rows, :1])
        low = e.astype(BF)
        e_ref[h, rows, :n] = low
        o_ref[h, rows, :] = dot_nn(low, v_ref[h, :n, :])
    atts = []
    g = g_ref[...].astype(F32)
    for h in range(2):
        o = o_ref[h]
        at = (1 - h) * HD
        inv = 1.0 / o[:, at:at + 1]
        att = jnp.where(mine[h], o * inv, 0.0)
        atts.append(att)
        gs = jnp.where(mine[h], g * inv, 0.0).astype(BF).astype(F32)
        delta = jnp.sum(gs * att, axis=1, keepdims=True)
        dh = delta.astype(BF).astype(F32)
        ge_ref[h] = jnp.where(lane == at, -dh, jnp.where(lane == at + 1, dh - delta, gs)).astype(BF)
    att_ref[...] = jnp.where(first, atts[0], atts[1]).astype(BF)
    dk_ref[...] = jnp.zeros_like(dk_ref)
    dv_ref[...] = jnp.zeros_like(dv_ref)
    for h, i in units:
        rows, n = spans(i)
        e = e_ref[h, rows, :n]
        ge = ge_ref[h, rows, :]
        ds = (e.astype(F32) * dot_nt(ge, v_ref[h, :n, :])).astype(BF)
        dq = dot_nn(ds, k_ref[:n, :]) * scale
        dq_ref[rows, :] = dq if h == 0 else jnp.where(first, dq_ref[rows, :], dq)
        dk_ref[:, :n] += dot_nn(q_ref[h, rows, :].T, ds)
        dv_ref[h, :, :n] += dot_nn(ge.T, e)
    sums = []
    values = (rotated(dq_ref[...], -1.0), rotated(dk_ref[...].T, -1.0), jnp.where(first, dv_ref[0].T, dv_ref[1].T))
    for c, value in enumerate(values):
        low = value.astype(BF)
        out_ref[:, c * width:(c + 1) * width] = low
        sums.append(jnp.sum(low.astype(F32), axis=0, keepdims=True))
    sq, sk, sv = sums
    sum_ref[0, :, :width] = jnp.where(first, sq, swapped(sk))
    sum_ref[0, :, width:2 * width] = jnp.where(first, sv, sq)
    sum_ref[0, :, 2 * width:] = jnp.where(first, swapped(sk), sv)


def attention_tables(positions):
    lo = (jnp.arange(positions.shape[0], dtype=jnp.int32) - positions)[:, None]
    return (lo, *rope_tables(positions))

def attention(tables, joined, bias, grad_att, start, count, before=()):
    lo, keep, upper, lower = tables
    seq, width = joined.shape
    pairs = width // (6 * HD)
    whole = lambda w: pl.BlockSpec((seq, w), lambda h: (0, 0))
    part = lambda w: pl.BlockSpec((seq, w), lambda h: (0, h + start))
    line = pl.BlockSpec((1, 1, 6 * HD), lambda h: (h + start, 0, 0))
    one = lambda dtype: pltpu.VMEM((seq, 2 * HD), dtype)
    two = lambda dtype: pltpu.VMEM((2, seq, 2 * HD), dtype)
    tables = [whole(2 * HD)] * 3
    return pl.pallas_call(
        attention_kernel,
        grid=(count,),
        in_specs=[whole(1), part(6 * HD), line, part(2 * HD)] + tables
        + [pl.BlockSpec(memory_space=pl.ANY)] * len(before),
        out_specs=[part(2 * HD), part(6 * HD), line],
        out_shape=[
            jax.ShapeDtypeStruct((seq, pairs * 2 * HD), BF),
            jax.ShapeDtypeStruct((seq, width), BF),
            jax.ShapeDtypeStruct((pairs, 1, 6 * HD), F32),
        ],
        input_output_aliases={7 + i: i for i in range(len(before))},
        scratch_shapes=[pltpu.VMEM((seq, seq), F32)]
        + [pltpu.VMEM((2, seq, seq), dtype) for dtype in (F32, BF)]
        + [two(F32), two(F32), two(BF), two(BF), one(BF), two(BF)]
        + [pltpu.VMEM((2 * HD, seq), F32), pltpu.VMEM((2, 2 * HD, seq), F32), one(F32)],
        compiler_params=pltpu.CompilerParams(vmem_limit_bytes=48 * 2**20),
        cost_estimate=pl.CostEstimate(flops=10**10, bytes_accessed=4 * 10**7, transcendentals=0),
        name="attention_both",
    )(lo, joined, bias.reshape(pairs, 1, 6 * HD), grad_att, keep, upper, lower, *before)

BAND = 128

def extra_bands(start, bands):
    return [i for i in range(start, start + bands // 2) if i % 2 == (2 * i >= bands)]

def gram_kernel(core_ref, x_ref, keep_ref, give_ref, twice_ref):
    size, width = x_ref.shape
    bands = size // BAND
    span = size // 2
    twice_ref[:size, :] = x_ref[...]
    twice_ref[size:, :] = x_ref[:span, :]
    def half(out_ref, start):
        for i in range(start, start + bands // 2):
            r = (i - start) * BAND
            band = twice_ref[i * BAND:(i + 1) * BAND, :]
            out_ref[r:r + BAND, :] = dot_nt(band, twice_ref[i * BAND:i * BAND + span, :])
        for e, i in enumerate(extra_bands(start, bands)):
            block = dot_nt(twice_ref[i * BAND:(i + 1) * BAND, :], twice_ref[i * BAND + span:(i + 1) * BAND + span, :])
            cut = BAND // (bands // 2)
            for c in range(bands // 2):
                r = span + e * cut
                out_ref[r:r + cut, c * BAND:(c + 1) * BAND] = block[c * cut:(c + 1) * cut, :]
    @pl.when(core_ref[0] == 0)
    def _():
        half(give_ref, bands // 2)
        half(keep_ref, 0)
    @pl.when(core_ref[0] == 1)
    def _():
        half(give_ref, 0)
        half(keep_ref, bands // 2)

def gram(core, x):
    size, width = x.shape
    span = size // 2
    half = jax.ShapeDtypeStruct((span + BAND // 2, span), F32)
    spec = pl.BlockSpec(memory_space=pltpu.VMEM)
    return pl.pallas_call(
        gram_kernel,
        out_shape=[half, half],
        in_specs=[pl.BlockSpec(memory_space=pltpu.SMEM), spec],
        out_specs=[spec, spec],
        scratch_shapes=[pltpu.VMEM((size + span, width), BF)],
        compiler_params=pltpu.CompilerParams(vmem_limit_bytes=32 * 2**20),
        name="gram",
    )(core.reshape(1), x)

def chain_kernel(core_ref, mine_ref, theirs_ref, x0_ref, out_ref, a_ref, ah_ref, m_ref, u_ref, uh_ref, xa_ref):
    size = x0_ref.shape[0]
    bands = size // BAND
    row = lax.broadcasted_iota(jnp.int32, (size // 2, BAND), 0)
    col = lax.broadcasted_iota(jnp.int32, (size // 2, BAND), 1)
    diagonal = mine_ref[:size // 2, :BAND] + theirs_ref[:size // 2, :BAND]
    trace = jnp.sum(jnp.where(row % BAND == col, diagonal, 0.0))
    norm = jnp.sqrt(trace) + 1e-07
    scale = 1.0 / (norm * norm)
    def store(rs, cs, block):
        a_ref[rs, cs] = block
        ah_ref[rs, cs] = block.astype(BF)
    def place(i, j, block):
        store(slice(i * BAND, (i + 1) * BAND), slice(j * BAND, (j + 1) * BAND), block)
        if i != j:
            store(slice(j * BAND, (j + 1) * BAND), slice(i * BAND, (i + 1) * BAND), block.T)
    def unpack(half_ref, start):
        for i in range(start, start + bands // 2):
            r = (i - start) * BAND
            for o in range(bands // 2):
                block = half_ref[r:r + BAND, o * BAND:(o + 1) * BAND] * scale
                place(i, (i + o) % bands, block)
        cut = BAND // (bands // 2)
        for e, i in enumerate(extra_bands(start, bands)):
            rows = slice(size // 2 + e * cut, size // 2 + (e + 1) * cut)
            parts = [half_ref[rows, c * BAND:(c + 1) * BAND] for c in range(bands // 2)]
            place(i, (i + bands // 2) % bands, jnp.concatenate(parts, axis=0) * scale)
    @pl.when(core_ref[0] == 0)
    def _():
        unpack(mine_ref, 0)
        unpack(theirs_ref, bands // 2)
    @pl.when(core_ref[0] == 1)
    def _():
        unpack(theirs_ref, 0)
        unpack(mine_ref, bands // 2)
    xa_ref[...] = x0_ref[...]
    lin = coef_linear
    def turn(k, last):
        inv = jnp.where(k == 0, 1.0 / norm, 1.0)
        for r0 in range(0, size, ROWS):
            r, c = slice(r0, r0 + ROWS), slice(r0, size)
            s = dot_nn(ah_ref[r, :], ah_ref[:, c])
            m = (coef_square * ah_ref[r, c].astype(F32) + coef_cubic * s).astype(BF)
            m_ref[r, c] = m
            if r0 + ROWS < size:
                m_ref[r0 + ROWS:, r] = m[:, ROWS:].T
        for r0 in range(0, size, 2 * ROWS):
            r = slice(r0, r0 + (2 * ROWS))
            out_ref[r, :] = ((lin * xa_ref[r, :].astype(F32) + dot_nn(m_ref[r, :], xa_ref[...])) * inv).astype(BF)
        if last:
            return
        xa_ref[...] = out_ref[...]
        for r0 in range(0, size, 2 * ROWS):
            r = slice(r0, r0 + 2 * ROWS)
            u = lin * a_ref[r, :] + dot_nn(m_ref[r, :], ah_ref[...])
            u_ref[r, :] = u
            uh_ref[r, :] = u.astype(BF)
        for r0 in range(0, size, ROWS):
            r, c = slice(r0, r0 + ROWS), slice(r0, size)
            block = lin * u_ref[r, c] + dot_nn(uh_ref[r, :], m_ref[:, c])
            store(r, c, block)
            if r0 + ROWS < size:
                store(slice(r0 + ROWS, size), r, block[:, ROWS:].T)
    def body(k, _):
        turn(k, False)
        return 0
    lax.fori_loop(0, 4, body, 0)
    turn(4, True)
def chain(core, mine, theirs, x0):
    size, width = x0.shape
    V = lambda dt: pltpu.VMEM((size, size), dt)
    spec = pl.BlockSpec(memory_space=pltpu.VMEM)
    return pl.pallas_call(
        chain_kernel,
        out_shape=jax.ShapeDtypeStruct((size, width), BF),
        in_specs=[pl.BlockSpec(memory_space=pltpu.SMEM)] + [spec] * 3, out_specs=spec,
        scratch_shapes=[V(F32), V(BF), V(BF), V(F32), V(BF), pltpu.VMEM((size, width), BF)],
        compiler_params=pltpu.CompilerParams(vmem_limit_bytes=56 * 2**20),
        name="orthogonalize",
    )(core.reshape(1), mine, theirs, x0)

def assemble(core, position, count, rows, mine, theirs, widths):
    pieces = mine + theirs
    n = len(pieces)
    def kernel(core_ref, position_ref, *refs):
        values, outs = refs[:n], refs[n:]
        for k, (step, offset, piece) in enumerate(pieces):
            which = core_ref[0] if k < len(mine) else 1 - core_ref[0]
            place = position_ref[0] + step
            place = jnp.where(place < count, place, place - count)
            chip = jnp.where(place < count // 2, 2 * place, 2 * (count - 1 - place) + 1)
            size = piece.shape[0]
            tile = math.gcd(rows, size)
            span = pl.ds(pl.multiple_of((chip * 2 + which) * rows + offset, tile), size)
            start = 0
            for out, w in zip(outs, widths):
                out[span, :] = values[k][:, start:start + w]
                start += w
    vmem, smem = pl.BlockSpec(memory_space=pltpu.VMEM), pl.BlockSpec(memory_space=pltpu.SMEM)
    return pl.pallas_call(
        kernel,
        out_shape=[jax.ShapeDtypeStruct((2 * count * rows, w), BF) for w in widths],
        in_specs=[smem, smem] + [vmem] * n,
        out_specs=[vmem] * len(widths),
        compiler_params=pltpu.CompilerParams(vmem_limit_bytes=48 * 2**20),
        name="assemble",
    )(core.reshape(1), position.reshape(1), *(piece[2] for piece in pieces))

def whole_call(kernel, name, out_shape, *args, scalars=0, scratch=(), limit=48):
    vmem, smem = pl.BlockSpec(memory_space=pltpu.VMEM), pl.BlockSpec(memory_space=pltpu.SMEM)
    args = [a.reshape(1) if i < scalars else a for i, a in enumerate(args)]
    return pl.pallas_call(
        kernel,
        out_shape=out_shape,
        in_specs=[smem] * scalars + [vmem] * (len(args) - scalars),
        out_specs=[vmem] * len(out_shape),
        scratch_shapes=list(scratch),
        compiler_params=pltpu.CompilerParams(vmem_limit_bytes=limit * 2**20),
        name=name,
    )(*args)

def momentum(decay, narrow, wide, moms, group):
    rows = moms[0].shape[0]
    widths = [m.shape[1] for m in moms]
    slot = max(widths) // group
    def kernel(*refs):
        narrow_refs, wide_refs, mom_refs, new_refs, out_ref = refs[:3], refs[3:6], refs[6:10], refs[10:14], refs[14]
        def total(parts, c, w):
            return sum(p[:, c:c + w].astype(F32) for p in parts)
        first = lax.broadcasted_iota(jnp.int32, (1, 2 * HD), 1) < HD
        for c in range(0, widths[0], 6 * HD):
            q, k, v = (total(narrow_refs, c + i * 2 * HD, 2 * HD) for i in range(3))
            k = pltpu.roll(k, HD, 1)
            parts = (jnp.where(first, q, k), jnp.where(first, v, q), jnp.where(first, k, v))
            for i, part in enumerate(parts):
                s = slice(c + i * 2 * HD, c + (i + 1) * 2 * HD)
                new_refs[0][:, s] = decay * mom_refs[0][:, s] + part
        new_refs[1][...] = decay * mom_refs[1][...] + total(narrow_refs, widths[0], widths[1])
        new_refs[2][...] = decay * mom_refs[2][...] + total(wide_refs, 0, widths[2])
        new_refs[3][...] = decay * mom_refs[3][...] + total(wide_refs, widths[2], widths[3])
        for m, new in enumerate(new_refs):
            w = widths[m] // group
            for j in range(group):
                block = new[:, j * w:(j + 1) * w].astype(BF)
                if w < slot:
                    block = jnp.concatenate([block, jnp.zeros((rows, slot - w), BF)], axis=1)
                out_ref[m * group + j] = block
    shapes = [jax.ShapeDtypeStruct(m.shape, F32) for m in moms]
    shapes.append(jax.ShapeDtypeStruct((4 * group, rows, slot), BF))
    return whole_call(kernel, "momentum", shapes, *narrow, *wide, *moms)

def update(pieces, masters, keep, rates, group):
    def kernel(piece_ref, *refs):
        for m in range(4):
            master, new = refs[m], refs[4 + m]
            w = master.shape[1] // group
            for j in range(group):
                s = slice(j * w, (j + 1) * w)
                new[:, s] = master[:, s] * keep - rates[m] * piece_ref[m * group + j, :, :w].astype(F32)
    shapes = [jax.ShapeDtypeStruct(m.shape, F32) for m in masters]
    return whole_call(kernel, "update", shapes, pieces, *masters)

def gelu_and_slope(v):
    root = math.sqrt(2.0 / math.pi)
    square = v * v
    half = 0.5 * jnp.tanh(v * (root + (root * 0.044715) * square)) + 0.5
    value = v * half
    return value, half + value * (1.0 - half) * (2.0 * root + (6.0 * root * 0.044715) * square)

def pack(fc1, fc2, dense, vectors, qkv):
    rows = fc1.shape[0]
    widths = [x.shape[1] for x in (fc1, fc2, dense)]
    lanes = 2 * HD
    def kernel(fc1_ref, fc2_ref, dense_ref, vectors_ref, qkv_ref, ring_ref, pair_ref):
        start = 0
        for x in (fc1_ref, fc2_ref, dense_ref):
            ring_ref[:, start:start + x.shape[1]] = x[...].astype(BF)
            start += x.shape[1]
        spare = jnp.zeros((rows - vectors_ref.shape[0], lanes), F32)
        ring_ref[:, start:] = jnp.concatenate([vectors_ref[...], spare], axis=0).astype(BF)
        first = lax.broadcasted_iota(jnp.int32, (1, lanes), 1) < HD
        for c in range(0, qkv_ref.shape[1], 3 * lanes):
            a, b, d = (qkv_ref[:, c + i * lanes:c + (i + 1) * lanes] for i in range(3))
            k = jnp.where(first, pltpu.roll(a, HD, 1), pltpu.roll(d, HD, 1))
            for i, part in enumerate((jnp.where(first, a, b), k, jnp.where(first, b, d))):
                pair_ref[:, c + i * lanes:c + (i + 1) * lanes] = part.astype(BF)
    lines = -(-vectors.shape[0] // (8 * lanes)) * 8
    vectors = jnp.pad(vectors, (0, lines * lanes - vectors.shape[0])).reshape(lines, lanes)
    shapes = [(rows, sum(widths) + lanes), qkv.shape]
    return whole_call(
        kernel, "pack", [jax.ShapeDtypeStruct(s, BF) for s in shapes], fc1, fc2, dense, vectors, qkv
    )


def other(x, axis, bit):
    n = lax.axis_size(axis)
    return lax.ppermute(x, axis, [(i, i ^ bit) for i in range(n)])


def in_order(mine, theirs, index, axis=0):
    low = jnp.where(index == 0, mine, theirs)
    high = jnp.where(index == 0, theirs, mine)
    return jnp.concatenate([low, high], axis=axis)


class Ring:
    def __init__(self):
        n = lax.axis_size("dp")
        self.count = n // 2
        rows = self.count // 2
        order = [2 * i for i in range(rows)] + [2 * i + 1 for i in reversed(range(rows))]
        index = lax.axis_index("dp")
        self.core = index % 2
        chip = index // 2
        self.position = jnp.where(chip % 2 == 0, chip // 2, self.count - 1 - chip // 2)
        self.up_pairs = [
            (2 * order[i] + c, 2 * order[(i + 1) % self.count] + c)
            for i in range(self.count)
            for c in range(2)
        ]
        self.down_pairs = [(b, a) for a, b in self.up_pairs]

    def chip(self, step):
        place = (self.position + step % self.count) % self.count
        return jnp.where(place < self.count // 2, 2 * place, 2 * (self.count - 1 - place) + 1)

    def up(self, x):
        return lax.ppermute(x, "dp", self.up_pairs)

    def down(self, x):
        return lax.ppermute(x, "dp", self.down_pairs)

    def gather(self, shard, rides, positions):
        rows = shard.shape[0]
        half, cut = self.count // 2, rows // 32 * 16 or rows // 2
        mine = {0: shard}
        rising = falling = shard
        ride = other(rides[0], "tensor", 1)
        for step in range(half):
            if step == half - 1:
                rising, falling = rising[:cut], falling[cut:]
            rising, falling = self.up(rising), self.down(falling)
            if step == 0:
                rising, positions = lax.optimization_barrier((rising, positions))
                tables = attention_tables(positions)
            elif step <= len(rides):
                if step == 1:
                    rising, falling, tables = lax.optimization_barrier((rising, falling, tables))
                else:
                    ride = other(rides[step - 1], "tensor", 1)
                rising, falling, rides[step - 1] = lax.optimization_barrier((rising, falling, ride))
            if step < half - 1:
                mine[self.count - 1 - step], mine[1 + step] = rising, falling
        mine[half] = jnp.concatenate([rising, falling], axis=0)
        mine = [(k, 0, mine[k]) for k in range(self.count)]
        return mine, [(k, row, other(block, "dp", 1)) for k, row, block in mine], tables

    def split(self, values, rows):
        parts = values.reshape(values.shape[0], self.count, 2, rows)
        return tuple(
            lax.dynamic_index_in_dim(parts, c, 2, False).reshape(values.shape[0], -1)
            for c in (self.core, 1 - self.core)
        )

    def pair_sum(self, lefts, right):
        keep, give = lefts
        theirs = other(dot_tn(give, right).astype(BF), "dp", 1)
        return (dot_tn(keep, right) + theirs.astype(F32)).astype(BF)

    def sweep(self, chain, work, state, last=False):
        (rising, falling), state = lax.optimization_barrier((chain.outgoing(), state))
        chain.received = self.up(rising), self.down(falling)
        state = work(state)
        if not last:
            chain.received, state = lax.optimization_barrier((chain.received, state))
        return state


class Chain:
    def __init__(self, ring, sums):
        self.ring, self.sums, self.received = ring, sums, None
        self.rows = sums[0].shape[0] // ring.count
        self.cut = self.rows // 32 * 16 or self.rows // 2
        self.left = ring.count // 2

    def block(self, step):
        start = self.ring.chip(step) * self.rows
        parts = [lax.dynamic_slice_in_dim(s, start, self.rows, 0) for s in self.sums]
        return jnp.concatenate(parts, axis=1)

    def outgoing(self):
        step, cut = self.left, self.cut
        self.left -= 1
        if self.received is None:
            far = self.block(step)
            return far[:cut], far[cut:]
        low, high = self.block(step).astype(F32), self.block(-step).astype(F32)
        rising, falling = (r.astype(F32) for r in self.received)
        if rising.shape[0] < self.rows:
            low = jnp.concatenate([low[:cut] + rising, low[cut:]], axis=0)
            high = jnp.concatenate([high[:cut], high[cut:] + falling], axis=0)
        else:
            low, high = low + rising, high + falling
        return low.astype(BF), high.astype(BF)

    def parts(self):
        return (self.block(0), *self.received)


def sum_over_group(core, columns, bits, tie):
    keep, give = gram(core, columns)
    rows = keep.shape[0]
    keep = keep + other(give, "dp", 1)
    pieces = [keep[: rows // 2], keep[rows // 2 :]]
    steps = [("dp", b) for b in bits] + [("tensor", 1)]
    for turn in range(len(steps)):
        if turn == len(steps) - 1:
            pieces, tie = lax.optimization_barrier((pieces, tie))
        axis, bit = steps[turn]
        first = other(pieces[0], axis, bit)
        axis, bit = steps[len(steps) - 1 - turn]
        second = other(pieces[1], axis, bit)
        pieces = [pieces[0] + first, pieces[1] + second]
    half = jnp.concatenate(pieces, axis=0)
    return half, other(half, "dp", 1), tie


def per_device(
    tokens,
    cotangent,
    positions,
    qkv_weight,
    dense_weight,
    fc1_weight,
    fc2_weight,
    vectors,
    mom_qkv,
    mom_dense,
    mom_fc1,
    mom_fc2,
    first_moment,
    second_moment,
):
    tensor_index = lax.axis_index("tensor")
    n = lax.axis_size("dp")
    ring = Ring()
    joined_width = 3 * D // 2
    unit_width = FF // 2
    shard_rows = qkv_weight.shape[0]
    half_rows = tokens.shape[0]
    seq = 2 * half_rows

    share = vectors.shape[0]
    first_pack, second_pack = pack(fc1_weight, fc2_weight, dense_weight, vectors, qkv_weight)
    lanes = 2 * HD
    quarter = half_rows // 2
    rides = [tokens, cotangent[:quarter], cotangent[quarter:]]
    mine, theirs, tables = ring.gather(first_pack, rides, positions)
    second_pack, rides[1] = lax.optimization_barrier((second_pack, rides[1]))
    tokens_theirs, cotangent_theirs = rides[0], jnp.concatenate(rides[1:], axis=0)
    full_qkv = lax.all_gather(second_pack, "dp", axis=0, tiled=True)
    widths = (unit_width, unit_width, D // 2, lanes)
    full_fc1, full_fc2, full_dense, lines_full = assemble(
        ring.core, ring.position, ring.count, shard_rows, mine, theirs, widths
    )
    lines_full = lines_full.reshape(n, shard_rows, lanes)[:, : -(-share // lanes)]
    vector_full = lines_full.reshape(n, -1)[:, :share].reshape(-1).astype(F32)

    ln_gain = vector_full[:D]
    ln_shift = vector_full[D : 2 * D]
    qkv_bias = lax.dynamic_slice_in_dim(
        vector_full, 2 * D + tensor_index * joined_width, joined_width
    )
    dense_bias = vector_full[5 * D : 6 * D]
    fc1_bias = lax.dynamic_slice_in_dim(vector_full, 6 * D + tensor_index * unit_width, unit_width)
    fc2_bias = vector_full[6 * D + FF :]

    tokens_all = in_order(tokens, tokens_theirs, tensor_index)
    cotangent_all = in_order(cotangent, cotangent_theirs, tensor_index)

    def normalized(rows):
        values = rows.astype(F32)
        centred = values - jnp.mean(values, axis=1, keepdims=True)
        inv_std = lax.rsqrt(jnp.mean(centred * centred, axis=1, keepdims=True) + 1e-05)
        return centred * inv_std, inv_std

    normed_all = (normalized(tokens_all)[0] * ln_gain + ln_shift).astype(BF)
    normed_parts = ring.split(normed_all, shard_rows)
    cotangent_parts = ring.split(cotangent_all, shard_rows)
    hidden = dot_nn(normed_all, full_fc1) + fc1_bias
    activation, slope = (v.astype(BF) for v in gelu_and_slope(hidden))
    grad_act = dot_nn(cotangent_all, full_fc2)
    grad_hidden = (grad_act * slope.astype(F32)).astype(BF)
    wide_sums = [
        ring.pair_sum(normed_parts, grad_hidden),
        ring.pair_sum(cotangent_parts, activation),
    ]

    def project(state):
        normed_all, cotangent_all, full_qkv, full_dense = state
        return dot_nn(normed_all, full_qkv), dot_nn(cotangent_all, full_dense).astype(BF)

    pairs = joined_width // (6 * HD)

    def attend_some(state):
        joined, grad_attended = state
        return joined, grad_attended, *attention(tables, joined, qkv_bias, grad_attended, 0, pairs // 2)

    def attend_rest(state):
        joined, grad_attended, *before = state
        return attention(
            tables, joined, qkv_bias, grad_attended, pairs // 2, pairs - pairs // 2, before
        )

    def sum_narrow(state):
        attended, grad_joined, qkv_bias_sum = state
        sums = [
            ring.pair_sum(normed_parts, grad_joined),
            ring.pair_sum(cotangent_parts, attended),
        ]
        return attended, grad_joined, qkv_bias_sum, sums

    def start_normed(state):
        attended, activation, grad_joined, grad_hidden = state
        return attended, activation, dot_nt(grad_joined, full_qkv), grad_hidden

    def sum_normed(state):
        attended, activation, partial, grad_hidden = state
        partial = (partial + dot_nt(grad_hidden, full_fc1)).astype(BF)
        return attended, activation, across(partial)

    def sum_branch(state):
        attended, activation, normed = state
        partial = (dot_nt(attended, full_dense) + dot_nt(activation, full_fc2)).astype(BF)
        return across(partial), normed

    def across(partial):
        mine = lax.dynamic_slice_in_dim(partial, tensor_index * half_rows, half_rows, 0)
        theirs = lax.dynamic_slice_in_dim(partial, (1 - tensor_index) * half_rows, half_rows, 0)
        return mine, theirs

    def run(chain, works, state):
        for step in range(ring.count // 2):
            work = works[step] if step < len(works) else lambda state: state
            state = ring.sweep(chain, work, state, step == ring.count // 2 - 1)
        return state

    wide = Chain(ring, wide_sums)
    works = (project, attend_some, attend_rest, sum_narrow)
    state = run(wide, works, (normed_all, cotangent_all, full_qkv, full_dense))
    attended, grad_joined, qkv_bias_sum, narrow_sums = state
    narrow = Chain(ring, narrow_sums)
    state = (attended, activation, grad_joined, grad_hidden)
    branch, normed = run(
        narrow, (lambda state: state, start_normed, sum_normed, sum_branch), state
    )
    branch_mine, branch_theirs = branch
    normed_mine, normed_theirs = normed[0], other(normed[1], "tensor", 1)
    moms = (mom_qkv, mom_dense, mom_fc1, mom_fc2)
    group = n // 4
    slot = unit_width // group
    *new_moms, blocks = momentum(momentum_decay, narrow.parts(), wide.parts(), moms, group)
    columns = lax.all_to_all(blocks, "dp", 0, 0, tiled=True)
    columns = columns.reshape(D, slot)
    grad_normed = normed_mine.astype(F32) + normed_theirs.astype(F32)
    unit_normed, inv_std = normalized(tokens)
    scaled_grad = grad_normed * ln_gain
    grad_tokens = cotangent.astype(F32) + inv_std * (
        scaled_grad
        - jnp.mean(scaled_grad, axis=1, keepdims=True)
        - unit_normed * jnp.mean(scaled_grad * unit_normed, axis=1, keepdims=True)
    )

    row_cotangent = jnp.sum(cotangent.astype(F32), axis=0)
    qkv_bias_grad = lax.dynamic_update_slice_in_dim(
        jnp.zeros((3 * D,), F32),
        qkv_bias_sum.reshape(-1),
        tensor_index * joined_width,
        0,
    )
    fc1_bias_grad = lax.dynamic_update_slice_in_dim(
        jnp.zeros((FF,), F32),
        jnp.sum(grad_hidden.astype(F32), axis=0),
        tensor_index * unit_width,
        0,
    )
    vector_grad = jnp.concatenate(
        [
            jnp.sum(grad_normed * unit_normed, axis=0),
            jnp.sum(grad_normed, axis=0),
            qkv_bias_grad,
            row_cotangent,
            fc1_bias_grad,
            row_cotangent,
        ]
    )
    bits = []
    bit = 2
    while bit < group:
        bits.append(bit)
        bit *= 2
    columns, vector_grad = lax.optimization_barrier((columns, vector_grad))
    vector_parts = lax.all_to_all(
        vector_grad.reshape(2 * n, share // 2), ("dp", "tensor"), 0, 0, tiled=True
    )
    mine, theirs, vector_parts = sum_over_group(ring.core, columns, bits, vector_parts)
    branch_theirs, mine = lax.optimization_barrier((branch_theirs, mine))
    ortho = chain(ring.core, mine, theirs, columns)
    ortho, branch_theirs = lax.optimization_barrier((ortho, other(branch_theirs, "tensor", 1)))
    branch = branch_mine.astype(F32) + branch_theirs.astype(F32)
    output = (tokens.astype(F32) + branch + dense_bias + fc2_bias).astype(BF)
    pieces = lax.all_to_all(ortho.reshape(n, shard_rows, slot), "dp", 0, 0, tiled=True)
    vector_share = jnp.sum(vector_parts, axis=0)

    masters = (qkv_weight, dense_weight, fc1_weight, fc2_weight)
    rates = [muon_rate * 0.2 * math.sqrt(max(D, 2 * m.shape[1])) for m in masters]
    new_weights = update(pieces, masters, 1.0 - muon_rate * weight_decay, rates, group)

    vector_slot = lax.dynamic_slice_in_dim(vectors, tensor_index * (share // 2), share // 2)
    new_first = beta_first * first_moment + (1.0 - beta_first) * vector_share
    new_second = beta_second * second_moment + (1.0 - beta_second) * vector_share * vector_share
    new_vectors = vector_slot - vector_rate * (new_first / (1.0 - beta_first**STEP)) / (
        jnp.sqrt(new_second / (1.0 - beta_second**STEP)) + 1e-08
    )
    return (
        output,
        grad_tokens,
        new_moms[0],
        new_weights[0],
        new_moms[1],
        new_weights[1],
        new_moms[2],
        new_weights[2],
        new_moms[3],
        new_weights[3],
        new_first,
        new_second,
        new_vectors,
    )


def solution(mesh):
    rows = P(("dp", "tensor"), None)
    weight = P("dp", "tensor")
    vector = P(("dp", "tensor"))
    return jax.shard_map(
        per_device,
        mesh=mesh,
        in_specs=(rows, rows, P("dp")) + (weight,) * 4 + (P("dp"),) + (weight,) * 4 + (vector,) * 2,
        out_specs=(rows, rows) + (weight,) * 8 + (vector,) * 3,
        check_vma=False,
    )
```

```python
import math

import jax
import jax.numpy as jnp
from jax import lax
from jax.experimental import pallas as pl
from jax.experimental.pallas import tpu as pltpu
from jax.sharding import PartitionSpec as P

D = 1024
HEADS = 16
FF = 4096
STEP = 10
momentum_decay = 0.95
muon_rate = 0.15
weight_decay = 0.1
vector_rate = 0.4
beta_first = 0.9
beta_second = 0.95
HD=64; ROT=32
F32=jnp.float32; BF=jnp.bfloat16
coef_linear = 3.4445
coef_square = -4.775
coef_cubic = 2.0315

def dot_nt(x, y):
    return lax.dot_general(x, y, (((1,), (1,)), ((), ())), preferred_element_type=F32)

def dot_tn(x, y):
    return lax.dot_general(x, y, (((0,), (0,)), ((), ())), preferred_element_type=F32)

def dot_nn(x, y):
    return jnp.dot(x, y, preferred_element_type=F32)

def tables_kernel(position_ref, frequency_ref, keep_ref, upper_ref, lower_ref):
    half = ROT // 2
    lane = lax.broadcasted_iota(jnp.int32, (1, 2 * HD), 1) % HD
    angles = position_ref[...].astype(F32) * frequency_ref[...]
    cosine, sine = jnp.cos(angles), jnp.sin(angles)
    keep_ref[...] = jnp.where(lane < ROT, cosine, 1.0)
    upper_ref[...] = jnp.where(lane < half, -sine, 0.0)
    lower_ref[...] = jnp.where((lane >= half) & (lane < ROT), sine, 0.0)

def rope_tables(positions):
    half = ROT // 2
    frequency = 10000.0 ** (-2.0 * jnp.arange(half, dtype=F32) / ROT)
    table = jax.ShapeDtypeStruct((positions.shape[0], 2 * HD), F32)
    return pl.pallas_call(
        tables_kernel,
        out_shape=[table] * 3,
        cost_estimate=pl.CostEstimate(flops=10**9, bytes_accessed=2 * 10**7, transcendentals=0),
        name="rope_tables",
    )(positions[:, None], jnp.tile(frequency, 2 * HD // half)[None])

ROWS = 256

def attention_kernel(lo_ref, x_ref, b_ref, g_ref, keep_ref, upper_ref, lower_ref, *refs):
    (att_ref, out_ref, sum_ref, bias_ref, s_ref, e_ref, top_ref, o_ref, ge_ref, q_ref, k_ref, v_ref,
     dk_ref, dv_ref, dq_ref) = refs[-15:]
    seq = x_ref.shape[0]
    width = 2 * HD
    lane = lax.broadcasted_iota(jnp.int32, (1, width), 1)
    first = lane < HD
    mine = (first, ~first)
    half = ROT // 2
    blocks = seq // ROWS
    @pl.when(pl.program_id(0) == 0)
    def _():
        for i in range(blocks):
            r0, n = i * ROWS, (i + 1) * ROWS
            col = lax.broadcasted_iota(jnp.int32, (ROWS, n), 1)
            row = lax.broadcasted_iota(jnp.int32, (ROWS, n), 0) + r0
            allowed = (col >= lo_ref[r0:n, :]) & (col <= row)
            bias_ref[r0:n, :n] = jnp.where(allowed, 0.0, -1e30)
    def rotated(values, sign):
        up = pltpu.roll(values, width - half, 1) * upper_ref[...]
        down = pltpu.roll(values, half, 1) * lower_ref[...]
        return values * keep_ref[...] + (up + down) * sign
    scale = HD ** -0.5
    def swapped(row):
        return pltpu.roll(jnp.broadcast_to(row, (8, width)), HD, 1)[:1]
    b0, b1, b2 = (b_ref[0, :, c * width:(c + 1) * width] for c in range(3))
    q = rotated(x_ref[:, :width] + jnp.where(first, b0, b1), 1.0) * scale
    bias_k = jnp.where(first, swapped(b0), swapped(b2))
    k_ref[...] = rotated(x_ref[:, width:2 * width] + bias_k, 1.0).astype(BF)
    v_ref[:, :width] = (x_ref[:, 2 * width:] + jnp.where(first, b1, b2)).astype(BF)
    v_ref[:, width:] = jnp.broadcast_to(jnp.where(lane < 2, 1.0, 0.0), (seq, width)).astype(BF)
    for i in range(blocks):
        for h in range(2):
            q_ref[i, h * ROWS:(h + 1) * ROWS, :] = jnp.where(
                mine[h], q[i * ROWS:(i + 1) * ROWS], 0.0
            ).astype(BF)
    for i in range(blocks):
        n = (i + 1) * ROWS
        both = dot_nt(q_ref[i], k_ref[:n, :])
        bias = bias_ref[i * ROWS:n, :n]
        for h in range(2):
            r = slice(h * ROWS, (h + 1) * ROWS)
            s = both[r] + bias
            s_ref[i, r, :n] = s
            m = s[:, :width]
            for c in range(width, n, width):
                m = jnp.maximum(m, s[:, c:c + width])
            top_ref[i, r, :] = m
    for i in range(blocks):
        top = jnp.max(top_ref[i], axis=1, keepdims=True)
        top_ref[i] = jnp.broadcast_to(top, (2 * ROWS, width))
    for i in range(blocks):
        n = (i + 1) * ROWS
        e = jnp.exp(s_ref[i, :, :n] - top_ref[i, :, :1]).astype(BF)
        e_ref[i, :, :n] = e
        o_ref[i] = dot_nn(e, v_ref[:n, :])
    for i in range(blocks):
        rows = slice(i * ROWS, (i + 1) * ROWS)
        g = g_ref[rows, :].astype(F32)
        atts = []
        for h in range(2):
            r = slice(h * ROWS, (h + 1) * ROWS)
            inv = 1.0 / o_ref[i, r, width:width + 1]
            att = jnp.where(mine[h], o_ref[i, r, :width] * inv, 0.0)
            atts.append(att)
            gs = jnp.where(mine[h], g * inv, 0.0).astype(BF)
            delta = jnp.sum(gs.astype(F32) * att, axis=1, keepdims=True)
            dh = delta.astype(BF).astype(F32)
            ge_ref[i, r, :width] = gs
            ge_ref[i, r, width:] = jnp.where(lane == 0, -dh, jnp.where(lane == 1, dh - delta, 0.0)).astype(BF)
        att_ref[rows, :] = jnp.where(first, atts[0], atts[1]).astype(BF)
    dk_ref[...] = jnp.zeros_like(dk_ref)
    dv_ref[...] = jnp.zeros_like(dv_ref)
    for i in range(blocks):
        n = (i + 1) * ROWS
        e = e_ref[i, :, :n]
        ds = (e.astype(F32) * dot_nt(ge_ref[i], v_ref[:n, :])).astype(BF)
        dq = dot_nn(ds, k_ref[:n, :]) * scale
        dq_ref[i * ROWS:n, :] = jnp.where(first, dq[:ROWS], dq[ROWS:])
        dk_ref[:, :n] += dot_nn(q_ref[i].T, ds)
        dv_ref[:, :n] += dot_nn(ge_ref[i, :, :width].T, e)
    sums = []
    values = (rotated(dq_ref[...], -1.0), rotated(dk_ref[...].T, -1.0), dv_ref[...].T)
    for c, value in enumerate(values):
        low = value.astype(BF)
        out_ref[:, c * width:(c + 1) * width] = low
        sums.append(jnp.sum(low.astype(F32), axis=0, keepdims=True))
    sq, sk, sv = sums
    sum_ref[0, :, :width] = jnp.where(first, sq, swapped(sk))
    sum_ref[0, :, width:2 * width] = jnp.where(first, sv, sq)
    sum_ref[0, :, 2 * width:] = jnp.where(first, swapped(sk), sv)

def attention_tables(positions):
    lo = (jnp.arange(positions.shape[0], dtype=jnp.int32) - positions)[:, None]
    return (lo, *rope_tables(positions))

def attention(tables, joined, bias, grad_att, start, count, before=()):
    lo, keep, upper, lower = tables
    seq, width = joined.shape
    pairs = width // (6 * HD)
    whole = lambda w: pl.BlockSpec((seq, w), lambda h: (0, 0))
    part = lambda w: pl.BlockSpec((seq, w), lambda h: (0, h + start))
    line = pl.BlockSpec((1, 1, 6 * HD), lambda h: (h + start, 0, 0))
    double = lambda w, dtype: pltpu.VMEM((seq // ROWS, 2 * ROWS, w), dtype)
    tables = [whole(2 * HD)] * 3
    return pl.pallas_call(
        attention_kernel,
        grid=(count,),
        in_specs=[whole(1), part(6 * HD), line, part(2 * HD)] + tables
        + [pl.BlockSpec(memory_space=pl.ANY)] * len(before),
        out_specs=[part(2 * HD), part(6 * HD), line],
        out_shape=[
            jax.ShapeDtypeStruct((seq, pairs * 2 * HD), BF),
            jax.ShapeDtypeStruct((seq, width), BF),
            jax.ShapeDtypeStruct((pairs, 1, 6 * HD), F32),
        ],
        input_output_aliases={7 + i: i for i in range(len(before))},
        scratch_shapes=[
            pltpu.VMEM((seq, seq), F32),
            double(seq, F32),
            double(seq, BF),
            double(2 * HD, F32),
            double(4 * HD, F32),
            double(4 * HD, BF),
            double(2 * HD, BF),
            pltpu.VMEM((seq, 2 * HD), BF),
            pltpu.VMEM((seq, 4 * HD), BF),
            pltpu.VMEM((2 * HD, seq), F32),
            pltpu.VMEM((2 * HD, seq), F32),
            pltpu.VMEM((seq, 2 * HD), F32),
        ],
        compiler_params=pltpu.CompilerParams(vmem_limit_bytes=40 * 2**20),
        cost_estimate=pl.CostEstimate(flops=10**10, bytes_accessed=4 * 10**7, transcendentals=0),
        name="attention_both",
    )(lo, joined, bias.reshape(pairs, 1, 6 * HD), grad_att, keep, upper, lower, *before)

BAND = 128

def extra_bands(start, bands):
    return [i for i in range(start, start + bands // 2) if i % 2 == (2 * i >= bands)]

def gram_kernel(core_ref, x_ref, keep_ref, give_ref, twice_ref):
    size, width = x_ref.shape
    bands = size // BAND
    span = size // 2
    twice_ref[:size, :] = x_ref[...]
    twice_ref[size:, :] = x_ref[:span, :]
    def half(out_ref, start):
        for i in range(start, start + bands // 2):
            r = (i - start) * BAND
            band = twice_ref[i * BAND:(i + 1) * BAND, :]
            out_ref[r:r + BAND, :] = dot_nt(band, twice_ref[i * BAND:i * BAND + span, :])
        for e, i in enumerate(extra_bands(start, bands)):
            block = dot_nt(twice_ref[i * BAND:(i + 1) * BAND, :], twice_ref[i * BAND + span:(i + 1) * BAND + span, :])
            cut = BAND // (bands // 2)
            for c in range(bands // 2):
                r = span + e * cut
                out_ref[r:r + cut, c * BAND:(c + 1) * BAND] = block[c * cut:(c + 1) * cut, :]
    @pl.when(core_ref[0] == 0)
    def _():
        half(give_ref, bands // 2)
        half(keep_ref, 0)
    @pl.when(core_ref[0] == 1)
    def _():
        half(give_ref, 0)
        half(keep_ref, bands // 2)

def gram(core, x):
    size, width = x.shape
    span = size // 2
    half = jax.ShapeDtypeStruct((span + BAND // 2, span), F32)
    spec = pl.BlockSpec(memory_space=pltpu.VMEM)
    return pl.pallas_call(
        gram_kernel,
        out_shape=[half, half],
        in_specs=[pl.BlockSpec(memory_space=pltpu.SMEM), spec],
        out_specs=[spec, spec],
        scratch_shapes=[pltpu.VMEM((size + span, width), BF)],
        compiler_params=pltpu.CompilerParams(vmem_limit_bytes=12 * 2**20),
        name="gram",
    )(core.reshape(1), x)

def chain_kernel(core_ref, mine_ref, theirs_ref, x0_ref, out_ref, a_ref, ah_ref, m_ref, u_ref, uh_ref, xa_ref):
    size = x0_ref.shape[0]
    bands = size // BAND
    row = lax.broadcasted_iota(jnp.int32, (size // 2, BAND), 0)
    col = lax.broadcasted_iota(jnp.int32, (size // 2, BAND), 1)
    diagonal = mine_ref[:size // 2, :BAND] + theirs_ref[:size // 2, :BAND]
    trace = jnp.sum(jnp.where(row % BAND == col, diagonal, 0.0))
    norm = jnp.sqrt(trace) + 1e-07
    scale = 1.0 / (norm * norm)
    def store(rs, cs, block):
        a_ref[rs, cs] = block
        ah_ref[rs, cs] = block.astype(BF)
    def place(i, j, block):
        store(slice(i * BAND, (i + 1) * BAND), slice(j * BAND, (j + 1) * BAND), block)
        if i != j:
            store(slice(j * BAND, (j + 1) * BAND), slice(i * BAND, (i + 1) * BAND), block.T)
    def unpack(half_ref, start):
        for i in range(start, start + bands // 2):
            r = (i - start) * BAND
            for o in range(bands // 2):
                block = half_ref[r:r + BAND, o * BAND:(o + 1) * BAND] * scale
                place(i, (i + o) % bands, block)
        cut = BAND // (bands // 2)
        for e, i in enumerate(extra_bands(start, bands)):
            rows = slice(size // 2 + e * cut, size // 2 + (e + 1) * cut)
            parts = [half_ref[rows, c * BAND:(c + 1) * BAND] for c in range(bands // 2)]
            place(i, (i + bands // 2) % bands, jnp.concatenate(parts, axis=0) * scale)
    @pl.when(core_ref[0] == 0)
    def _():
        unpack(mine_ref, 0)
        unpack(theirs_ref, bands // 2)
    @pl.when(core_ref[0] == 1)
    def _():
        unpack(theirs_ref, 0)
        unpack(mine_ref, bands // 2)
    xa_ref[...] = x0_ref[...]
    lin = coef_linear
    def turn(k, last):
        inv = jnp.where(k == 0, 1.0 / norm, 1.0)
        for r0 in range(0, size, ROWS):
            r, c = slice(r0, r0 + ROWS), slice(r0, size)
            s = dot_nn(ah_ref[r, :], ah_ref[:, c])
            m = (coef_square * ah_ref[r, c].astype(F32) + coef_cubic * s).astype(BF)
            m_ref[r, c] = m
            if r0 + ROWS < size:
                m_ref[r0 + ROWS:, r] = m[:, ROWS:].T
        for r0 in range(0, size, 2 * ROWS):
            r = slice(r0, r0 + (2 * ROWS))
            out_ref[r, :] = ((lin * xa_ref[r, :].astype(F32) + dot_nn(m_ref[r, :], xa_ref[...])) * inv).astype(BF)
        if last:
            return
        xa_ref[...] = out_ref[...]
        for r0 in range(0, size, 2 * ROWS):
            r = slice(r0, r0 + 2 * ROWS)
            u = lin * a_ref[r, :] + dot_nn(m_ref[r, :], ah_ref[...])
            u_ref[r, :] = u
            uh_ref[r, :] = u.astype(BF)
        for r0 in range(0, size, ROWS):
            r, c = slice(r0, r0 + ROWS), slice(r0, size)
            block = lin * u_ref[r, c] + dot_nn(uh_ref[r, :], m_ref[:, c])
            store(r, c, block)
            if r0 + ROWS < size:
                store(slice(r0 + ROWS, size), r, block[:, ROWS:].T)
    def body(k, _):
        turn(k, False)
        return 0
    lax.fori_loop(0, 4, body, 0)
    turn(4, True)
def chain(core, mine, theirs, x0):
    size, width = x0.shape
    V = lambda dt: pltpu.VMEM((size, size), dt)
    spec = pl.BlockSpec(memory_space=pltpu.VMEM)
    return pl.pallas_call(
        chain_kernel,
        out_shape=jax.ShapeDtypeStruct((size, width), BF),
        in_specs=[pl.BlockSpec(memory_space=pltpu.SMEM)] + [spec] * 3, out_specs=spec,
        scratch_shapes=[V(F32), V(BF), V(BF), V(F32), V(BF), pltpu.VMEM((size, width), BF)],
        compiler_params=pltpu.CompilerParams(vmem_limit_bytes=34 * 2**20),
        name="orthogonalize",
    )(core.reshape(1), mine, theirs, x0)

def assemble(core, position, count, rows, mine, theirs, widths):
    pieces = mine + theirs
    n = len(pieces)
    def kernel(core_ref, position_ref, *refs):
        values, outs = refs[:n], refs[n:]
        for k, (step, offset, piece) in enumerate(pieces):
            which = core_ref[0] if k < len(mine) else 1 - core_ref[0]
            place = position_ref[0] + step
            place = jnp.where(place < count, place, place - count)
            chip = jnp.where(place < count // 2, 2 * place, 2 * (count - 1 - place) + 1)
            size = piece.shape[0]
            tile = math.gcd(rows, size)
            span = pl.ds(pl.multiple_of((chip * 2 + which) * rows + offset, tile), size)
            start = 0
            for out, w in zip(outs, widths):
                out[span, :] = values[k][:, start:start + w]
                start += w
    vmem, smem = pl.BlockSpec(memory_space=pltpu.VMEM), pl.BlockSpec(memory_space=pltpu.SMEM)
    return pl.pallas_call(
        kernel,
        out_shape=[jax.ShapeDtypeStruct((2 * count * rows, w), BF) for w in widths],
        in_specs=[smem, smem] + [vmem] * n,
        out_specs=[vmem] * len(widths),
        compiler_params=pltpu.CompilerParams(vmem_limit_bytes=48 * 2**20),
        name="assemble",
    )(core.reshape(1), position.reshape(1), *(piece[2] for piece in pieces))

def whole_call(kernel, name, out_shape, *args, scalars=0, scratch=(), limit=12):
    vmem, smem = pl.BlockSpec(memory_space=pltpu.VMEM), pl.BlockSpec(memory_space=pltpu.SMEM)
    args = [a.reshape(1) if i < scalars else a for i, a in enumerate(args)]
    return pl.pallas_call(
        kernel,
        out_shape=out_shape,
        in_specs=[smem] * scalars + [vmem] * (len(args) - scalars),
        out_specs=[vmem] * len(out_shape),
        scratch_shapes=list(scratch),
        compiler_params=pltpu.CompilerParams(vmem_limit_bytes=limit * 2**20),
        name=name,
    )(*args)

def momentum(decay, narrow, wide, moms, group):
    rows = moms[0].shape[0]
    widths = [m.shape[1] for m in moms]
    slot = max(widths) // group
    def kernel(*refs):
        narrow_refs, wide_refs, mom_refs, new_refs, out_ref = refs[:3], refs[3:6], refs[6:10], refs[10:14], refs[14]
        def total(parts, c, w):
            return sum(p[:, c:c + w].astype(F32) for p in parts)
        first = lax.broadcasted_iota(jnp.int32, (1, 2 * HD), 1) < HD
        for c in range(0, widths[0], 6 * HD):
            q, k, v = (total(narrow_refs, c + i * 2 * HD, 2 * HD) for i in range(3))
            k = pltpu.roll(k, HD, 1)
            parts = (jnp.where(first, q, k), jnp.where(first, v, q), jnp.where(first, k, v))
            for i, part in enumerate(parts):
                s = slice(c + i * 2 * HD, c + (i + 1) * 2 * HD)
                new_refs[0][:, s] = decay * mom_refs[0][:, s] + part
        new_refs[1][...] = decay * mom_refs[1][...] + total(narrow_refs, widths[0], widths[1])
        new_refs[2][...] = decay * mom_refs[2][...] + total(wide_refs, 0, widths[2])
        new_refs[3][...] = decay * mom_refs[3][...] + total(wide_refs, widths[2], widths[3])
        for m, new in enumerate(new_refs):
            w = widths[m] // group
            for j in range(group):
                block = new[:, j * w:(j + 1) * w].astype(BF)
                if w < slot:
                    block = jnp.concatenate([block, jnp.zeros((rows, slot - w), BF)], axis=1)
                out_ref[m * group + j] = block
    shapes = [jax.ShapeDtypeStruct(m.shape, F32) for m in moms]
    shapes.append(jax.ShapeDtypeStruct((4 * group, rows, slot), BF))
    return whole_call(kernel, "momentum", shapes, *narrow, *wide, *moms)

def update(pieces, masters, keep, rates, group):
    def kernel(piece_ref, *refs):
        for m in range(4):
            master, new = refs[m], refs[4 + m]
            w = master.shape[1] // group
            for j in range(group):
                s = slice(j * w, (j + 1) * w)
                new[:, s] = master[:, s] * keep - rates[m] * piece_ref[m * group + j, :, :w].astype(F32)
    shapes = [jax.ShapeDtypeStruct(m.shape, F32) for m in masters]
    return whole_call(kernel, "update", shapes, pieces, *masters)

def gelu_and_slope(v):
    root = math.sqrt(2.0 / math.pi)
    square = v * v
    half = 0.5 * jnp.tanh(v * (root + (root * 0.044715) * square)) + 0.5
    value = v * half
    return value, half + value * (1.0 - half) * (2.0 * root + (6.0 * root * 0.044715) * square)

def pack(fc1, fc2, dense, vectors, qkv):
    rows = fc1.shape[0]
    widths = [x.shape[1] for x in (fc1, fc2, dense)]
    lanes = 2 * HD
    def kernel(fc1_ref, fc2_ref, dense_ref, vectors_ref, qkv_ref, ring_ref, pair_ref):
        start = 0
        for x in (fc1_ref, fc2_ref, dense_ref):
            ring_ref[:, start:start + x.shape[1]] = x[...].astype(BF)
            start += x.shape[1]
        spare = jnp.zeros((rows - vectors_ref.shape[0], lanes), F32)
        ring_ref[:, start:] = jnp.concatenate([vectors_ref[...], spare], axis=0).astype(BF)
        first = lax.broadcasted_iota(jnp.int32, (1, lanes), 1) < HD
        for c in range(0, qkv_ref.shape[1], 3 * lanes):
            a, b, d = (qkv_ref[:, c + i * lanes:c + (i + 1) * lanes] for i in range(3))
            k = jnp.where(first, pltpu.roll(a, HD, 1), pltpu.roll(d, HD, 1))
            for i, part in enumerate((jnp.where(first, a, b), k, jnp.where(first, b, d))):
                pair_ref[:, c + i * lanes:c + (i + 1) * lanes] = part.astype(BF)
    lines = -(-vectors.shape[0] // (8 * lanes)) * 8
    vectors = jnp.pad(vectors, (0, lines * lanes - vectors.shape[0])).reshape(lines, lanes)
    shapes = [(rows, sum(widths) + lanes), qkv.shape]
    args = (fc1, fc2, dense, vectors, qkv)
    block = lambda shape: pl.BlockSpec(shape, lambda i: (0, 0))
    return pl.pallas_call(
        kernel,
        grid=(1,),
        out_shape=[jax.ShapeDtypeStruct(s, BF) for s in shapes],
        in_specs=[block(a.shape) for a in args],
        out_specs=[block(s) for s in shapes],
        compiler_params=pltpu.CompilerParams(vmem_limit_bytes=12 * 2**20),
        name="pack",
    )(*args)


def other(x, axis, bit):
    n = lax.axis_size(axis)
    return lax.ppermute(x, axis, [(i, i ^ bit) for i in range(n)])


def in_order(mine, theirs, index, axis=0):
    low = jnp.where(index == 0, mine, theirs)
    high = jnp.where(index == 0, theirs, mine)
    return jnp.concatenate([low, high], axis=axis)


class Ring:
    def __init__(self):
        n = lax.axis_size("dp")
        self.count = n // 2
        rows = self.count // 2
        order = [2 * i for i in range(rows)] + [2 * i + 1 for i in reversed(range(rows))]
        index = lax.axis_index("dp")
        self.core = index % 2
        chip = index // 2
        self.position = jnp.where(chip % 2 == 0, chip // 2, self.count - 1 - chip // 2)
        self.up_pairs = [
            (2 * order[i] + c, 2 * order[(i + 1) % self.count] + c)
            for i in range(self.count)
            for c in range(2)
        ]
        self.down_pairs = [(b, a) for a, b in self.up_pairs]

    def chip(self, step):
        place = (self.position + step % self.count) % self.count
        return jnp.where(place < self.count // 2, 2 * place, 2 * (self.count - 1 - place) + 1)

    def up(self, x):
        return lax.ppermute(x, "dp", self.up_pairs)

    def down(self, x):
        return lax.ppermute(x, "dp", self.down_pairs)

    def gather(self, shard, rides, positions):
        rows = shard.shape[0]
        half, cut = self.count // 2, rows // 32 * 16 or rows // 2
        mine = {0: shard}
        rising = falling = shard
        ride = other(rides[0], "tensor", 1)
        for step in range(half):
            if step == half - 1:
                rising, falling = rising[:cut], falling[cut:]
            rising, falling = self.up(rising), self.down(falling)
            if step == 0:
                rising, positions = lax.optimization_barrier((rising, positions))
                tables = attention_tables(positions)
            elif step <= len(rides):
                if step == 1:
                    rising, falling, tables = lax.optimization_barrier((rising, falling, tables))
                else:
                    ride = other(rides[step - 1], "tensor", 1)
                rising, falling, rides[step - 1] = lax.optimization_barrier((rising, falling, ride))
            if step < half - 1:
                mine[self.count - 1 - step], mine[1 + step] = rising, falling
        mine[half] = jnp.concatenate([rising, falling], axis=0)
        mine = [(k, 0, mine[k]) for k in range(self.count)]
        return mine, [(k, row, other(block, "dp", 1)) for k, row, block in mine], tables

    def split(self, values, rows):
        parts = values.reshape(values.shape[0], self.count, 2, rows)
        return tuple(
            lax.dynamic_index_in_dim(parts, c, 2, False).reshape(values.shape[0], -1)
            for c in (self.core, 1 - self.core)
        )

    def pair_sum(self, lefts, right):
        keep, give = lefts
        theirs = other(dot_tn(give, right).astype(BF), "dp", 1)
        return (dot_tn(keep, right) + theirs.astype(F32)).astype(BF)

    def sweep(self, chain, work, state, last=False):
        (rising, falling), state = lax.optimization_barrier((chain.outgoing(), state))
        chain.received = self.up(rising), self.down(falling)
        state = work(state)
        if not last:
            chain.received, state = lax.optimization_barrier((chain.received, state))
        return state


class Chain:
    def __init__(self, ring, sums):
        self.ring, self.sums, self.received = ring, sums, None
        self.rows = sums[0].shape[0] // ring.count
        self.cut = self.rows // 32 * 16 or self.rows // 2
        self.left = ring.count // 2

    def block(self, step):
        start = self.ring.chip(step) * self.rows
        parts = [lax.dynamic_slice_in_dim(s, start, self.rows, 0) for s in self.sums]
        return jnp.concatenate(parts, axis=1)

    def outgoing(self):
        step, cut = self.left, self.cut
        self.left -= 1
        if self.received is None:
            far = self.block(step)
            return far[:cut], far[cut:]
        low, high = self.block(step).astype(F32), self.block(-step).astype(F32)
        rising, falling = (r.astype(F32) for r in self.received)
        if rising.shape[0] < self.rows:
            low = jnp.concatenate([low[:cut] + rising, low[cut:]], axis=0)
            high = jnp.concatenate([high[:cut], high[cut:] + falling], axis=0)
        else:
            low, high = low + rising, high + falling
        return low.astype(BF), high.astype(BF)

    def parts(self):
        return (self.block(0), *self.received)


def sum_over_group(core, columns, bits, tie):
    keep, give = gram(core, columns)
    rows = keep.shape[0]
    keep = keep + other(give, "dp", 1)
    pieces = [keep[: rows // 2], keep[rows // 2 :]]
    steps = [("dp", b) for b in bits] + [("tensor", 1)]
    for turn in range(len(steps)):
        if turn == len(steps) - 1:
            pieces, tie = lax.optimization_barrier((pieces, tie))
        axis, bit = steps[turn]
        first = other(pieces[0], axis, bit)
        axis, bit = steps[len(steps) - 1 - turn]
        second = other(pieces[1], axis, bit)
        pieces = [pieces[0] + first, pieces[1] + second]
    half = jnp.concatenate(pieces, axis=0)
    return half, other(half, "dp", 1), tie


def per_device(
    tokens,
    cotangent,
    positions,
    qkv_weight,
    dense_weight,
    fc1_weight,
    fc2_weight,
    vectors,
    mom_qkv,
    mom_dense,
    mom_fc1,
    mom_fc2,
    first_moment,
    second_moment,
):
    tensor_index = lax.axis_index("tensor")
    n = lax.axis_size("dp")
    ring = Ring()
    joined_width = 3 * D // 2
    unit_width = FF // 2
    shard_rows = qkv_weight.shape[0]
    half_rows = tokens.shape[0]
    seq = 2 * half_rows

    share = vectors.shape[0]
    first_pack, second_pack = pack(fc1_weight, fc2_weight, dense_weight, vectors, qkv_weight)
    lanes = 2 * HD
    quarter = half_rows // 2
    rides = [tokens, cotangent[:quarter], cotangent[quarter:]]
    mine, theirs, tables = ring.gather(first_pack, rides, positions)
    second_pack, rides[1] = lax.optimization_barrier((second_pack, rides[1]))
    tokens_theirs, cotangent_theirs = rides[0], jnp.concatenate(rides[1:], axis=0)
    full_qkv = lax.all_gather(second_pack, "dp", axis=0, tiled=True)
    widths = (unit_width, unit_width, D // 2, lanes)
    full_fc1, full_fc2, full_dense, lines_full = assemble(
        ring.core, ring.position, ring.count, shard_rows, mine, theirs, widths
    )
    lines_full = lines_full.reshape(n, shard_rows, lanes)[:, : -(-share // lanes)]
    vector_full = lines_full.reshape(n, -1)[:, :share].reshape(-1).astype(F32)

    ln_gain = vector_full[:D]
    ln_shift = vector_full[D : 2 * D]
    qkv_bias = lax.dynamic_slice_in_dim(
        vector_full, 2 * D + tensor_index * joined_width, joined_width
    )
    dense_bias = vector_full[5 * D : 6 * D]
    fc1_bias = lax.dynamic_slice_in_dim(vector_full, 6 * D + tensor_index * unit_width, unit_width)
    fc2_bias = vector_full[6 * D + FF :]

    tokens_all = in_order(tokens, tokens_theirs, tensor_index)
    cotangent_all = in_order(cotangent, cotangent_theirs, tensor_index)

    def normalized(rows):
        values = rows.astype(F32)
        centred = values - jnp.mean(values, axis=1, keepdims=True)
        inv_std = lax.rsqrt(jnp.mean(centred * centred, axis=1, keepdims=True) + 1e-05)
        return centred * inv_std, inv_std

    normed_all = (normalized(tokens_all)[0] * ln_gain + ln_shift).astype(BF)
    normed_parts = ring.split(normed_all, shard_rows)
    cotangent_parts = ring.split(cotangent_all, shard_rows)
    hidden = dot_nn(normed_all, full_fc1) + fc1_bias
    activation, slope = (v.astype(BF) for v in gelu_and_slope(hidden))
    grad_act = dot_nn(cotangent_all, full_fc2)
    grad_hidden = (grad_act * slope.astype(F32)).astype(BF)
    wide_sums = [
        ring.pair_sum(normed_parts, grad_hidden),
        ring.pair_sum(cotangent_parts, activation),
    ]

    def project(state):
        full_qkv, full_dense = state
        return dot_nn(normed_all, full_qkv), dot_nn(cotangent_all, full_dense).astype(BF)

    pairs = joined_width // (6 * HD)

    def attend_some(state):
        joined, grad_attended = state
        return joined, grad_attended, *attention(tables, joined, qkv_bias, grad_attended, 0, pairs // 2)

    def attend_rest(state):
        joined, grad_attended, *before = state
        return attention(
            tables, joined, qkv_bias, grad_attended, pairs // 2, pairs - pairs // 2, before
        )

    def sum_narrow(state):
        attended, grad_joined, qkv_bias_sum = state
        sums = [
            ring.pair_sum(normed_parts, grad_joined),
            ring.pair_sum(cotangent_parts, attended),
        ]
        return attended, grad_joined, qkv_bias_sum, sums

    def start_normed(state):
        attended, activation, grad_joined, grad_hidden = state
        return attended, activation, dot_nt(grad_joined, full_qkv), grad_hidden

    def sum_normed(state):
        attended, activation, partial, grad_hidden = state
        partial = (partial + dot_nt(grad_hidden, full_fc1)).astype(BF)
        return attended, activation, across(partial)

    def sum_branch(state):
        attended, activation, normed = state
        partial = (dot_nt(attended, full_dense) + dot_nt(activation, full_fc2)).astype(BF)
        return across(partial), normed

    def across(partial):
        mine = lax.dynamic_slice_in_dim(partial, tensor_index * half_rows, half_rows, 0)
        theirs = lax.dynamic_slice_in_dim(partial, (1 - tensor_index) * half_rows, half_rows, 0)
        return mine, theirs

    def run(chain, works, state):
        for step in range(ring.count // 2):
            work = works[step] if step < len(works) else lambda state: state
            state = ring.sweep(chain, work, state, step == ring.count // 2 - 1)
        return state

    wide = Chain(ring, wide_sums)
    works = (project, attend_some, attend_rest, sum_narrow)
    state = run(wide, works, (full_qkv, full_dense))
    attended, grad_joined, qkv_bias_sum, narrow_sums = state
    narrow = Chain(ring, narrow_sums)
    state = (attended, activation, grad_joined, grad_hidden)
    branch, normed = run(
        narrow, (lambda state: state, start_normed, sum_normed, sum_branch), state
    )
    branch_mine, branch_theirs = branch
    normed_mine, normed_theirs = normed[0], other(normed[1], "tensor", 1)
    moms = (mom_qkv, mom_dense, mom_fc1, mom_fc2)
    group = n // 4
    slot = unit_width // group
    *new_moms, blocks = momentum(momentum_decay, narrow.parts(), wide.parts(), moms, group)
    columns = lax.all_to_all(blocks, "dp", 0, 0, tiled=True)
    columns = columns.reshape(D, slot)
    grad_normed = normed_mine.astype(F32) + normed_theirs.astype(F32)
    unit_normed, inv_std = normalized(tokens)
    scaled_grad = grad_normed * ln_gain
    grad_tokens = cotangent.astype(F32) + inv_std * (
        scaled_grad
        - jnp.mean(scaled_grad, axis=1, keepdims=True)
        - unit_normed * jnp.mean(scaled_grad * unit_normed, axis=1, keepdims=True)
    )

    row_cotangent = jnp.sum(cotangent.astype(F32), axis=0)
    qkv_bias_grad = lax.dynamic_update_slice_in_dim(
        jnp.zeros((3 * D,), F32),
        qkv_bias_sum.reshape(-1),
        tensor_index * joined_width,
        0,
    )
    fc1_bias_grad = lax.dynamic_update_slice_in_dim(
        jnp.zeros((FF,), F32),
        jnp.sum(grad_hidden.astype(F32), axis=0),
        tensor_index * unit_width,
        0,
    )
    vector_grad = jnp.concatenate(
        [
            jnp.sum(grad_normed * unit_normed, axis=0),
            jnp.sum(grad_normed, axis=0),
            qkv_bias_grad,
            row_cotangent,
            fc1_bias_grad,
            row_cotangent,
        ]
    )
    bits = []
    bit = 2
    while bit < group:
        bits.append(bit)
        bit *= 2
    columns, vector_grad = lax.optimization_barrier((columns, vector_grad))
    vector_parts = lax.all_to_all(
        vector_grad.reshape(2 * n, share // 2), ("dp", "tensor"), 0, 0, tiled=True
    )
    mine, theirs, vector_parts = sum_over_group(ring.core, columns, bits, vector_parts)
    branch_theirs, mine = lax.optimization_barrier((branch_theirs, mine))
    ortho = chain(ring.core, mine, theirs, columns)
    ortho, branch_theirs = lax.optimization_barrier((ortho, other(branch_theirs, "tensor", 1)))
    branch = branch_mine.astype(F32) + branch_theirs.astype(F32)
    output = (tokens.astype(F32) + branch + dense_bias + fc2_bias).astype(BF)
    pieces = lax.all_to_all(ortho.reshape(n, shard_rows, slot), "dp", 0, 0, tiled=True)
    vector_share = jnp.sum(vector_parts, axis=0)

    masters = (qkv_weight, dense_weight, fc1_weight, fc2_weight)
    rates = [muon_rate * 0.2 * math.sqrt(max(D, 2 * m.shape[1])) for m in masters]
    new_weights = update(pieces, masters, 1.0 - muon_rate * weight_decay, rates, group)

    vector_slot = lax.dynamic_slice_in_dim(vectors, tensor_index * (share // 2), share // 2)
    new_first = beta_first * first_moment + (1.0 - beta_first) * vector_share
    new_second = beta_second * second_moment + (1.0 - beta_second) * vector_share * vector_share
    new_vectors = vector_slot - vector_rate * (new_first / (1.0 - beta_first**STEP)) / (
        jnp.sqrt(new_second / (1.0 - beta_second**STEP)) + 1e-08
    )
    return (
        output,
        grad_tokens,
        new_moms[0],
        new_weights[0],
        new_moms[1],
        new_weights[1],
        new_moms[2],
        new_weights[2],
        new_moms[3],
        new_weights[3],
        new_first,
        new_second,
        new_vectors,
    )


def solution(mesh):
    rows = P(("dp", "tensor"), None)
    weight = P("dp", "tensor")
    vector = P(("dp", "tensor"))
    return jax.shard_map(
        per_device,
        mesh=mesh,
        in_specs=(rows, rows, P("dp")) + (weight,) * 4 + (P("dp"),) + (weight,) * 4 + (vector,) * 2,
        out_specs=(rows, rows) + (weight,) * 8 + (vector,) * 3,
        check_vma=False,
    )
```

```python
import math

import jax
import jax.numpy as jnp
from jax import lax
from jax.experimental import pallas as pl
from jax.experimental.pallas import tpu as pltpu
from jax.sharding import PartitionSpec as P

D = 1024
HEADS = 16
FF = 4096
STEP = 10
momentum_decay = 0.95
muon_rate = 0.15
weight_decay = 0.1
vector_rate = 0.4
beta_first = 0.9
beta_second = 0.95
HD=64; ROT=32
F32=jnp.float32; BF=jnp.bfloat16
coef_linear = 3.4445
coef_square = -4.775
coef_cubic = 2.0315

def dot_nt(x, y):
    return lax.dot_general(x, y, (((1,), (1,)), ((), ())), preferred_element_type=F32)

def dot_tn(x, y):
    return lax.dot_general(x, y, (((0,), (0,)), ((), ())), preferred_element_type=F32)

def dot_nn(x, y):
    return jnp.dot(x, y, preferred_element_type=F32)

def tables_kernel(position_ref, frequency_ref, keep_ref, upper_ref, lower_ref):
    half = ROT // 2
    lane = lax.broadcasted_iota(jnp.int32, (1, 2 * HD), 1) % HD
    angles = position_ref[...].astype(F32) * frequency_ref[...]
    cosine, sine = jnp.cos(angles), jnp.sin(angles)
    keep_ref[...] = jnp.where(lane < ROT, cosine, 1.0)
    upper_ref[...] = jnp.where(lane < half, -sine, 0.0)
    lower_ref[...] = jnp.where((lane >= half) & (lane < ROT), sine, 0.0)

def rope_tables(positions):
    half = ROT // 2
    frequency = 10000.0 ** (-2.0 * jnp.arange(half, dtype=F32) / ROT)
    table = jax.ShapeDtypeStruct((positions.shape[0], 2 * HD), F32)
    return pl.pallas_call(
        tables_kernel,
        out_shape=[table] * 3,
        cost_estimate=pl.CostEstimate(flops=10**9, bytes_accessed=2 * 10**7, transcendentals=0),
        name="rope_tables",
    )(positions[:, None], jnp.tile(frequency, 2 * HD // half)[None])

ROWS = 256

def attention_kernel(lo_ref, x_ref, b_ref, g_ref, keep_ref, upper_ref, lower_ref, *refs):
    (att_ref, out_ref, sum_ref, bias_ref, s_ref, e_ref, top_ref, o_ref, ge_ref, q_ref, k_ref, v_ref,
     dk_ref, dv_ref, dq_ref) = refs[-15:]
    seq = x_ref.shape[0]
    width = 2 * HD
    lane = lax.broadcasted_iota(jnp.int32, (1, width), 1)
    first = lane < HD
    mine = (first, ~first)
    half = ROT // 2
    blocks = seq // ROWS
    @pl.when(pl.program_id(0) == 0)
    def _():
        for i in range(blocks):
            r0, n = i * ROWS, (i + 1) * ROWS
            col = lax.broadcasted_iota(jnp.int32, (ROWS, n), 1)
            row = lax.broadcasted_iota(jnp.int32, (ROWS, n), 0) + r0
            allowed = (col >= lo_ref[r0:n, :]) & (col <= row)
            bias_ref[r0:n, :n] = jnp.where(allowed, 0.0, -1e30)
    def rotated(values, sign):
        up = pltpu.roll(values, width - half, 1) * upper_ref[...]
        down = pltpu.roll(values, half, 1) * lower_ref[...]
        return values * keep_ref[...] + (up + down) * sign
    scale = HD ** -0.5
    def swapped(row):
        return pltpu.roll(jnp.broadcast_to(row, (8, width)), HD, 1)[:1]
    b0, b1, b2 = (b_ref[0, :, c * width:(c + 1) * width] for c in range(3))
    q = rotated(x_ref[:, :width] + jnp.where(first, b0, b1), 1.0) * scale
    bias_k = jnp.where(first, swapped(b0), swapped(b2))
    k_ref[...] = rotated(x_ref[:, width:2 * width] + bias_k, 1.0).astype(BF)
    v_ref[:, :width] = (x_ref[:, 2 * width:] + jnp.where(first, b1, b2)).astype(BF)
    v_ref[:, width:] = jnp.broadcast_to(jnp.where(lane < 2, 1.0, 0.0), (seq, width)).astype(BF)
    for i in range(blocks):
        for h in range(2):
            q_ref[i, h * ROWS:(h + 1) * ROWS, :] = jnp.where(
                mine[h], q[i * ROWS:(i + 1) * ROWS], 0.0
            ).astype(BF)
    for i in range(blocks):
        n = (i + 1) * ROWS
        both = dot_nt(q_ref[i], k_ref[:n, :])
        bias = bias_ref[i * ROWS:n, :n]
        for h in range(2):
            r = slice(h * ROWS, (h + 1) * ROWS)
            s = both[r] + bias
            s_ref[i, r, :n] = s
            m = s[:, :width]
            for c in range(width, n, width):
                m = jnp.maximum(m, s[:, c:c + width])
            top_ref[i, r, :] = m
    for i in range(blocks):
        top = jnp.max(top_ref[i], axis=1, keepdims=True)
        top_ref[i] = jnp.broadcast_to(top, (2 * ROWS, width))
    for i in range(blocks):
        n = (i + 1) * ROWS
        e = jnp.exp(s_ref[i, :, :n] - top_ref[i, :, :1]).astype(BF)
        e_ref[i, :, :n] = e
        o_ref[i] = dot_nn(e, v_ref[:n, :])
    for i in range(blocks):
        rows = slice(i * ROWS, (i + 1) * ROWS)
        g = g_ref[rows, :].astype(F32)
        atts = []
        for h in range(2):
            r = slice(h * ROWS, (h + 1) * ROWS)
            inv = 1.0 / o_ref[i, r, width:width + 1]
            att = jnp.where(mine[h], o_ref[i, r, :width] * inv, 0.0)
            atts.append(att)
            gs = jnp.where(mine[h], g * inv, 0.0).astype(BF)
            delta = jnp.sum(gs.astype(F32) * att, axis=1, keepdims=True)
            dh = delta.astype(BF).astype(F32)
            ge_ref[i, r, :width] = gs
            ge_ref[i, r, width:] = jnp.where(lane == 0, -dh, jnp.where(lane == 1, dh - delta, 0.0)).astype(BF)
        att_ref[rows, :] = jnp.where(first, atts[0], atts[1]).astype(BF)
    dk_ref[...] = jnp.zeros_like(dk_ref)
    dv_ref[...] = jnp.zeros_like(dv_ref)
    for i in range(blocks):
        n = (i + 1) * ROWS
        e = e_ref[i, :, :n]
        ds = (e.astype(F32) * dot_nt(ge_ref[i], v_ref[:n, :])).astype(BF)
        dq = dot_nn(ds, k_ref[:n, :]) * scale
        dq_ref[i * ROWS:n, :] = jnp.where(first, dq[:ROWS], dq[ROWS:])
        dk_ref[:, :n] += dot_nn(q_ref[i].T, ds)
        dv_ref[:, :n] += dot_nn(ge_ref[i, :, :width].T, e)
    sums = []
    values = (rotated(dq_ref[...], -1.0), rotated(dk_ref[...].T, -1.0), dv_ref[...].T)
    for c, value in enumerate(values):
        low = value.astype(BF)
        out_ref[:, c * width:(c + 1) * width] = low
        sums.append(jnp.sum(low.astype(F32), axis=0, keepdims=True))
    sq, sk, sv = sums
    sum_ref[0, :, :width] = jnp.where(first, sq, swapped(sk))
    sum_ref[0, :, width:2 * width] = jnp.where(first, sv, sq)
    sum_ref[0, :, 2 * width:] = jnp.where(first, swapped(sk), sv)

def attention_tables(positions):
    lo = (jnp.arange(positions.shape[0], dtype=jnp.int32) - positions)[:, None]
    return (lo, *rope_tables(positions))

def attention(tables, joined, bias, grad_att, start, count, before=()):
    lo, keep, upper, lower = tables
    seq, width = joined.shape
    pairs = width // (6 * HD)
    whole = lambda w: pl.BlockSpec((seq, w), lambda h: (0, 0))
    part = lambda w: pl.BlockSpec((seq, w), lambda h: (0, h + start))
    line = pl.BlockSpec((1, 1, 6 * HD), lambda h: (h + start, 0, 0))
    double = lambda w, dtype: pltpu.VMEM((seq // ROWS, 2 * ROWS, w), dtype)
    tables = [whole(2 * HD)] * 3
    return pl.pallas_call(
        attention_kernel,
        grid=(count,),
        in_specs=[whole(1), part(6 * HD), line, part(2 * HD)] + tables
        + [pl.BlockSpec(memory_space=pl.ANY)] * len(before),
        out_specs=[part(2 * HD), part(6 * HD), line],
        out_shape=[
            jax.ShapeDtypeStruct((seq, pairs * 2 * HD), BF),
            jax.ShapeDtypeStruct((seq, width), BF),
            jax.ShapeDtypeStruct((pairs, 1, 6 * HD), F32),
        ],
        input_output_aliases={7 + i: i for i in range(len(before))},
        scratch_shapes=[
            pltpu.VMEM((seq, seq), F32),
            double(seq, F32),
            double(seq, BF),
            double(2 * HD, F32),
            double(4 * HD, F32),
            double(4 * HD, BF),
            double(2 * HD, BF),
            pltpu.VMEM((seq, 2 * HD), BF),
            pltpu.VMEM((seq, 4 * HD), BF),
            pltpu.VMEM((2 * HD, seq), F32),
            pltpu.VMEM((2 * HD, seq), F32),
            pltpu.VMEM((seq, 2 * HD), F32),
        ],
        compiler_params=pltpu.CompilerParams(vmem_limit_bytes=37 * 2**20),
        cost_estimate=pl.CostEstimate(flops=10**10, bytes_accessed=4 * 10**7, transcendentals=0),
        name="attention_both",
    )(lo, joined, bias.reshape(pairs, 1, 6 * HD), grad_att, keep, upper, lower, *before)

BAND = 128

def extra_bands(start, bands):
    return [i for i in range(start, start + bands // 2) if i % 2 == (2 * i >= bands)]

def gram_kernel(core_ref, x_ref, keep_ref, give_ref, twice_ref):
    size, width = x_ref.shape
    bands = size // BAND
    span = size // 2
    twice_ref[:size, :] = x_ref[...]
    twice_ref[size:, :] = x_ref[:span, :]
    def half(out_ref, start):
        for i in range(start, start + bands // 2):
            r = (i - start) * BAND
            band = twice_ref[i * BAND:(i + 1) * BAND, :]
            out_ref[r:r + BAND, :] = dot_nt(band, twice_ref[i * BAND:i * BAND + span, :])
        for e, i in enumerate(extra_bands(start, bands)):
            block = dot_nt(twice_ref[i * BAND:(i + 1) * BAND, :], twice_ref[i * BAND + span:(i + 1) * BAND + span, :])
            cut = BAND // (bands // 2)
            for c in range(bands // 2):
                r = span + e * cut
                out_ref[r:r + cut, c * BAND:(c + 1) * BAND] = block[c * cut:(c + 1) * cut, :]
    @pl.when(core_ref[0] == 0)
    def _():
        half(give_ref, bands // 2)
        half(keep_ref, 0)
    @pl.when(core_ref[0] == 1)
    def _():
        half(give_ref, 0)
        half(keep_ref, bands // 2)

def gram(core, x):
    size, width = x.shape
    span = size // 2
    half = jax.ShapeDtypeStruct((span + BAND // 2, span), F32)
    spec = pl.BlockSpec(memory_space=pltpu.VMEM)
    return pl.pallas_call(
        gram_kernel,
        out_shape=[half, half],
        in_specs=[pl.BlockSpec(memory_space=pltpu.SMEM), spec],
        out_specs=[spec, spec],
        scratch_shapes=[pltpu.VMEM((size + span, width), BF)],
        compiler_params=pltpu.CompilerParams(vmem_limit_bytes=12 * 2**20),
        name="gram",
    )(core.reshape(1), x)

def chain_kernel(core_ref, mine_ref, theirs_ref, x0_ref, out_ref, a_ref, ah_ref, m_ref, u_ref, uh_ref, xa_ref):
    size = x0_ref.shape[0]
    bands = size // BAND
    row = lax.broadcasted_iota(jnp.int32, (size // 2, BAND), 0)
    col = lax.broadcasted_iota(jnp.int32, (size // 2, BAND), 1)
    diagonal = mine_ref[:size // 2, :BAND] + theirs_ref[:size // 2, :BAND]
    trace = jnp.sum(jnp.where(row % BAND == col, diagonal, 0.0))
    norm = jnp.sqrt(trace) + 1e-07
    scale = 1.0 / (norm * norm)
    def store(rs, cs, block):
        a_ref[rs, cs] = block
        ah_ref[rs, cs] = block.astype(BF)
    def place(i, j, block):
        store(slice(i * BAND, (i + 1) * BAND), slice(j * BAND, (j + 1) * BAND), block)
        if i != j:
            store(slice(j * BAND, (j + 1) * BAND), slice(i * BAND, (i + 1) * BAND), block.T)
    def unpack(half_ref, start):
        for i in range(start, start + bands // 2):
            r = (i - start) * BAND
            for o in range(bands // 2):
                block = half_ref[r:r + BAND, o * BAND:(o + 1) * BAND] * scale
                place(i, (i + o) % bands, block)
        cut = BAND // (bands // 2)
        for e, i in enumerate(extra_bands(start, bands)):
            rows = slice(size // 2 + e * cut, size // 2 + (e + 1) * cut)
            parts = [half_ref[rows, c * BAND:(c + 1) * BAND] for c in range(bands // 2)]
            place(i, (i + bands // 2) % bands, jnp.concatenate(parts, axis=0) * scale)
    @pl.when(core_ref[0] == 0)
    def _():
        unpack(mine_ref, 0)
        unpack(theirs_ref, bands // 2)
    @pl.when(core_ref[0] == 1)
    def _():
        unpack(theirs_ref, 0)
        unpack(mine_ref, bands // 2)
    xa_ref[...] = x0_ref[...]
    lin = coef_linear
    def turn(k, last):
        inv = jnp.where(k == 0, 1.0 / norm, 1.0)
        for r0 in range(0, size, ROWS):
            r, c = slice(r0, r0 + ROWS), slice(r0, size)
            s = dot_nn(ah_ref[r, :], ah_ref[:, c])
            m = (coef_square * ah_ref[r, c].astype(F32) + coef_cubic * s).astype(BF)
            m_ref[r, c] = m
            if r0 + ROWS < size:
                m_ref[r0 + ROWS:, r] = m[:, ROWS:].T
        for r0 in range(0, size, 2 * ROWS):
            r = slice(r0, r0 + (2 * ROWS))
            out_ref[r, :] = ((lin * xa_ref[r, :].astype(F32) + dot_nn(m_ref[r, :], xa_ref[...])) * inv).astype(BF)
        if last:
            return
        xa_ref[...] = out_ref[...]
        for r0 in range(0, size, 2 * ROWS):
            r = slice(r0, r0 + 2 * ROWS)
            u = lin * a_ref[r, :] + dot_nn(m_ref[r, :], ah_ref[...])
            u_ref[r, :] = u
            uh_ref[r, :] = u.astype(BF)
        for r0 in range(0, size, ROWS):
            r, c = slice(r0, r0 + ROWS), slice(r0, size)
            block = lin * u_ref[r, c] + dot_nn(uh_ref[r, :], m_ref[:, c])
            store(r, c, block)
            if r0 + ROWS < size:
                store(slice(r0 + ROWS, size), r, block[:, ROWS:].T)
    def body(k, _):
        turn(k, False)
        return 0
    lax.fori_loop(0, 4, body, 0)
    turn(4, True)
def chain(core, mine, theirs, x0):
    size, width = x0.shape
    V = lambda dt: pltpu.VMEM((size, size), dt)
    spec = pl.BlockSpec(memory_space=pltpu.VMEM)
    return pl.pallas_call(
        chain_kernel,
        out_shape=jax.ShapeDtypeStruct((size, width), BF),
        in_specs=[pl.BlockSpec(memory_space=pltpu.SMEM)] + [spec] * 3, out_specs=spec,
        scratch_shapes=[V(F32), V(BF), V(BF), V(F32), V(BF), pltpu.VMEM((size, width), BF)],
        compiler_params=pltpu.CompilerParams(vmem_limit_bytes=34 * 2**20),
        name="orthogonalize",
    )(core.reshape(1), mine, theirs, x0)

def assemble(core, position, count, rows, mine, theirs, widths):
    pieces = mine + theirs
    n = len(pieces)
    def kernel(core_ref, position_ref, *refs):
        values, outs = refs[:n], refs[n:]
        for k, (step, offset, piece) in enumerate(pieces):
            which = core_ref[0] if k < len(mine) else 1 - core_ref[0]
            place = position_ref[0] + step
            place = jnp.where(place < count, place, place - count)
            chip = jnp.where(place < count // 2, 2 * place, 2 * (count - 1 - place) + 1)
            size = piece.shape[0]
            tile = math.gcd(rows, size)
            span = pl.ds(pl.multiple_of((chip * 2 + which) * rows + offset, tile), size)
            start = 0
            for out, w in zip(outs, widths):
                out[span, :] = values[k][:, start:start + w]
                start += w
    vmem, smem = pl.BlockSpec(memory_space=pltpu.VMEM), pl.BlockSpec(memory_space=pltpu.SMEM)
    return pl.pallas_call(
        kernel,
        out_shape=[jax.ShapeDtypeStruct((2 * count * rows, w), BF) for w in widths],
        in_specs=[smem, smem] + [vmem] * n,
        out_specs=[vmem] * len(widths),
        compiler_params=pltpu.CompilerParams(vmem_limit_bytes=48 * 2**20),
        name="assemble",
    )(core.reshape(1), position.reshape(1), *(piece[2] for piece in pieces))

def whole_call(kernel, name, out_shape, *args, scalars=0, scratch=(), limit=12):
    vmem, smem = pl.BlockSpec(memory_space=pltpu.VMEM), pl.BlockSpec(memory_space=pltpu.SMEM)
    args = [a.reshape(1) if i < scalars else a for i, a in enumerate(args)]
    return pl.pallas_call(
        kernel,
        out_shape=out_shape,
        in_specs=[smem] * scalars + [vmem] * (len(args) - scalars),
        out_specs=[vmem] * len(out_shape),
        scratch_shapes=list(scratch),
        compiler_params=pltpu.CompilerParams(vmem_limit_bytes=limit * 2**20),
        name=name,
    )(*args)

def momentum(decay, narrow, wide, moms, group):
    rows = moms[0].shape[0]
    widths = [m.shape[1] for m in moms]
    slot = max(widths) // group
    def kernel(*refs):
        narrow_refs, wide_refs, mom_refs, new_refs, out_ref = refs[:3], refs[3:6], refs[6:10], refs[10:14], refs[14]
        def total(parts, c, w):
            return sum(p[:, c:c + w].astype(F32) for p in parts)
        first = lax.broadcasted_iota(jnp.int32, (1, 2 * HD), 1) < HD
        for c in range(0, widths[0], 6 * HD):
            q, k, v = (total(narrow_refs, c + i * 2 * HD, 2 * HD) for i in range(3))
            k = pltpu.roll(k, HD, 1)
            parts = (jnp.where(first, q, k), jnp.where(first, v, q), jnp.where(first, k, v))
            for i, part in enumerate(parts):
                s = slice(c + i * 2 * HD, c + (i + 1) * 2 * HD)
                new_refs[0][:, s] = decay * mom_refs[0][:, s] + part
        new_refs[1][...] = decay * mom_refs[1][...] + total(narrow_refs, widths[0], widths[1])
        new_refs[2][...] = decay * mom_refs[2][...] + total(wide_refs, 0, widths[2])
        new_refs[3][...] = decay * mom_refs[3][...] + total(wide_refs, widths[2], widths[3])
        for m, new in enumerate(new_refs):
            w = widths[m] // group
            for j in range(group):
                block = new[:, j * w:(j + 1) * w].astype(BF)
                if w < slot:
                    block = jnp.concatenate([block, jnp.zeros((rows, slot - w), BF)], axis=1)
                out_ref[m * group + j] = block
    shapes = [jax.ShapeDtypeStruct(m.shape, F32) for m in moms]
    shapes.append(jax.ShapeDtypeStruct((4 * group, rows, slot), BF))
    return whole_call(kernel, "momentum", shapes, *narrow, *wide, *moms)

def update(pieces, masters, keep, rates, group):
    def kernel(piece_ref, *refs):
        for m in range(4):
            master, new = refs[m], refs[4 + m]
            w = master.shape[1] // group
            for j in range(group):
                s = slice(j * w, (j + 1) * w)
                new[:, s] = master[:, s] * keep - rates[m] * piece_ref[m * group + j, :, :w].astype(F32)
    shapes = [jax.ShapeDtypeStruct(m.shape, F32) for m in masters]
    return whole_call(kernel, "update", shapes, pieces, *masters)

def gelu_and_slope(v):
    root = math.sqrt(2.0 / math.pi)
    square = v * v
    half = 0.5 * jnp.tanh(v * (root + (root * 0.044715) * square)) + 0.5
    value = v * half
    return value, half + value * (1.0 - half) * (2.0 * root + (6.0 * root * 0.044715) * square)

def pack(fc1, fc2, dense, vectors, qkv):
    rows = fc1.shape[0]
    widths = [x.shape[1] for x in (fc1, fc2, dense)]
    lanes = 2 * HD
    def kernel(fc1_ref, fc2_ref, dense_ref, vectors_ref, qkv_ref, ring_ref, pair_ref):
        start = 0
        for x in (fc1_ref, fc2_ref, dense_ref):
            ring_ref[:, start:start + x.shape[1]] = x[...].astype(BF)
            start += x.shape[1]
        spare = jnp.zeros((rows - vectors_ref.shape[0], lanes), F32)
        ring_ref[:, start:] = jnp.concatenate([vectors_ref[...], spare], axis=0).astype(BF)
        first = lax.broadcasted_iota(jnp.int32, (1, lanes), 1) < HD
        for c in range(0, qkv_ref.shape[1], 3 * lanes):
            a, b, d = (qkv_ref[:, c + i * lanes:c + (i + 1) * lanes] for i in range(3))
            k = jnp.where(first, pltpu.roll(a, HD, 1), pltpu.roll(d, HD, 1))
            for i, part in enumerate((jnp.where(first, a, b), k, jnp.where(first, b, d))):
                pair_ref[:, c + i * lanes:c + (i + 1) * lanes] = part.astype(BF)
    lines = -(-vectors.shape[0] // (8 * lanes)) * 8
    vectors = jnp.pad(vectors, (0, lines * lanes - vectors.shape[0])).reshape(lines, lanes)
    shapes = [(rows, sum(widths) + lanes), qkv.shape]
    args = (fc1, fc2, dense, vectors, qkv)
    block = lambda shape: pl.BlockSpec(shape, lambda i: (0, 0))
    return pl.pallas_call(
        kernel,
        grid=(1,),
        out_shape=[jax.ShapeDtypeStruct(s, BF) for s in shapes],
        in_specs=[block(a.shape) for a in args],
        out_specs=[block(s) for s in shapes],
        compiler_params=pltpu.CompilerParams(vmem_limit_bytes=56 * 2**20),
        name="pack",
    )(*args)


def other(x, axis, bit):
    n = lax.axis_size(axis)
    return lax.ppermute(x, axis, [(i, i ^ bit) for i in range(n)])


def in_order(mine, theirs, index, axis=0):
    low = jnp.where(index == 0, mine, theirs)
    high = jnp.where(index == 0, theirs, mine)
    return jnp.concatenate([low, high], axis=axis)


class Ring:
    def __init__(self):
        n = lax.axis_size("dp")
        self.count = n // 2
        rows = self.count // 2
        order = [2 * i for i in range(rows)] + [2 * i + 1 for i in reversed(range(rows))]
        index = lax.axis_index("dp")
        self.core = index % 2
        chip = index // 2
        self.position = jnp.where(chip % 2 == 0, chip // 2, self.count - 1 - chip // 2)
        self.up_pairs = [
            (2 * order[i] + c, 2 * order[(i + 1) % self.count] + c)
            for i in range(self.count)
            for c in range(2)
        ]
        self.down_pairs = [(b, a) for a, b in self.up_pairs]

    def chip(self, step):
        place = (self.position + step % self.count) % self.count
        return jnp.where(place < self.count // 2, 2 * place, 2 * (self.count - 1 - place) + 1)

    def up(self, x):
        return lax.ppermute(x, "dp", self.up_pairs)

    def down(self, x):
        return lax.ppermute(x, "dp", self.down_pairs)

    def gather(self, shard, rides, positions):
        rows = shard.shape[0]
        half, cut = self.count // 2, rows // 32 * 16 or rows // 2
        mine = {0: shard}
        rising = falling = shard
        ride = other(rides[0], "tensor", 1)
        for step in range(half):
            if step == half - 1:
                rising, falling = rising[:cut], falling[cut:]
            rising, falling = self.up(rising), self.down(falling)
            if step == 0:
                rising, positions = lax.optimization_barrier((rising, positions))
                tables = attention_tables(positions)
            elif step <= len(rides):
                if step == 1:
                    rising, falling, tables = lax.optimization_barrier((rising, falling, tables))
                else:
                    ride = other(rides[step - 1], "tensor", 1)
                rising, falling, rides[step - 1] = lax.optimization_barrier((rising, falling, ride))
            if step < half - 1:
                mine[self.count - 1 - step], mine[1 + step] = rising, falling
        mine[half] = jnp.concatenate([rising, falling], axis=0)
        mine = [(k, 0, mine[k]) for k in range(self.count)]
        return mine, [(k, row, other(block, "dp", 1)) for k, row, block in mine], tables

    def split(self, values, rows):
        parts = values.reshape(values.shape[0], self.count, 2, rows)
        return tuple(
            lax.dynamic_index_in_dim(parts, c, 2, False).reshape(values.shape[0], -1)
            for c in (self.core, 1 - self.core)
        )

    def pair_sum(self, lefts, right):
        keep, give = lefts
        theirs = other(dot_tn(give, right).astype(BF), "dp", 1)
        return (dot_tn(keep, right) + theirs.astype(F32)).astype(BF)

    def sweep(self, chain, work, state, last=False):
        (rising, falling), state = lax.optimization_barrier((chain.outgoing(), state))
        chain.received = self.up(rising), self.down(falling)
        state = work(state)
        if not last:
            chain.received, state = lax.optimization_barrier((chain.received, state))
        return state


class Chain:
    def __init__(self, ring, sums):
        self.ring, self.sums, self.received = ring, sums, None
        self.rows = sums[0].shape[0] // ring.count
        self.cut = self.rows // 32 * 16 or self.rows // 2
        self.left = ring.count // 2

    def block(self, step):
        start = self.ring.chip(step) * self.rows
        parts = [lax.dynamic_slice_in_dim(s, start, self.rows, 0) for s in self.sums]
        return jnp.concatenate(parts, axis=1)

    def outgoing(self):
        step, cut = self.left, self.cut
        self.left -= 1
        if self.received is None:
            far = self.block(step)
            return far[:cut], far[cut:]
        low, high = self.block(step).astype(F32), self.block(-step).astype(F32)
        rising, falling = (r.astype(F32) for r in self.received)
        if rising.shape[0] < self.rows:
            low = jnp.concatenate([low[:cut] + rising, low[cut:]], axis=0)
            high = jnp.concatenate([high[:cut], high[cut:] + falling], axis=0)
        else:
            low, high = low + rising, high + falling
        return low.astype(BF), high.astype(BF)

    def parts(self):
        return (self.block(0), *self.received)


def sum_over_group(core, columns, bits, tie):
    keep, give = gram(core, columns)
    rows = keep.shape[0]
    keep = keep + other(give, "dp", 1)
    pieces = [keep[: rows // 2], keep[rows // 2 :]]
    steps = [("dp", b) for b in bits] + [("tensor", 1)]
    for turn in range(len(steps)):
        if turn == len(steps) - 1:
            pieces, tie = lax.optimization_barrier((pieces, tie))
        axis, bit = steps[turn]
        first = other(pieces[0], axis, bit)
        axis, bit = steps[len(steps) - 1 - turn]
        second = other(pieces[1], axis, bit)
        pieces = [pieces[0] + first, pieces[1] + second]
    half = jnp.concatenate(pieces, axis=0)
    return half, other(half, "dp", 1), tie


def per_device(
    tokens,
    cotangent,
    positions,
    qkv_weight,
    dense_weight,
    fc1_weight,
    fc2_weight,
    vectors,
    mom_qkv,
    mom_dense,
    mom_fc1,
    mom_fc2,
    first_moment,
    second_moment,
):
    tensor_index = lax.axis_index("tensor")
    n = lax.axis_size("dp")
    ring = Ring()
    joined_width = 3 * D // 2
    unit_width = FF // 2
    shard_rows = qkv_weight.shape[0]
    half_rows = tokens.shape[0]
    seq = 2 * half_rows

    share = vectors.shape[0]
    first_pack, second_pack = pack(fc1_weight, fc2_weight, dense_weight, vectors, qkv_weight)
    lanes = 2 * HD
    quarter = half_rows // 2
    rides = [tokens, cotangent[:quarter], cotangent[quarter:]]
    mine, theirs, tables = ring.gather(first_pack, rides, positions)
    second_pack, rides[1] = lax.optimization_barrier((second_pack, rides[1]))
    tokens_theirs, cotangent_theirs = rides[0], jnp.concatenate(rides[1:], axis=0)
    full_qkv = lax.all_gather(second_pack, "dp", axis=0, tiled=True)
    widths = (unit_width, unit_width, D // 2, lanes)
    full_fc1, full_fc2, full_dense, lines_full = assemble(
        ring.core, ring.position, ring.count, shard_rows, mine, theirs, widths
    )
    lines_full = lines_full.reshape(n, shard_rows, lanes)[:, : -(-share // lanes)]
    vector_full = lines_full.reshape(n, -1)[:, :share].reshape(-1).astype(F32)

    ln_gain = vector_full[:D]
    ln_shift = vector_full[D : 2 * D]
    qkv_bias = lax.dynamic_slice_in_dim(
        vector_full, 2 * D + tensor_index * joined_width, joined_width
    )
    dense_bias = vector_full[5 * D : 6 * D]
    fc1_bias = lax.dynamic_slice_in_dim(vector_full, 6 * D + tensor_index * unit_width, unit_width)
    fc2_bias = vector_full[6 * D + FF :]

    tokens_all = in_order(tokens, tokens_theirs, tensor_index)
    cotangent_all = in_order(cotangent, cotangent_theirs, tensor_index)

    def normalized(rows):
        values = rows.astype(F32)
        centred = values - jnp.mean(values, axis=1, keepdims=True)
        inv_std = lax.rsqrt(jnp.mean(centred * centred, axis=1, keepdims=True) + 1e-05)
        return centred * inv_std, inv_std

    normed_all = (normalized(tokens_all)[0] * ln_gain + ln_shift).astype(BF)
    normed_parts = ring.split(normed_all, shard_rows)
    cotangent_parts = ring.split(cotangent_all, shard_rows)
    hidden = dot_nn(normed_all, full_fc1) + fc1_bias
    activation, slope = (v.astype(BF) for v in gelu_and_slope(hidden))
    grad_act = dot_nn(cotangent_all, full_fc2)
    grad_hidden = (grad_act * slope.astype(F32)).astype(BF)
    wide_sums = [
        ring.pair_sum(normed_parts, grad_hidden),
        ring.pair_sum(cotangent_parts, activation),
    ]

    def project(state):
        full_qkv, full_dense = state
        return dot_nn(normed_all, full_qkv), dot_nn(cotangent_all, full_dense).astype(BF)

    pairs = joined_width // (6 * HD)

    def attend_some(state):
        joined, grad_attended = state
        return joined, grad_attended, *attention(tables, joined, qkv_bias, grad_attended, 0, pairs // 2)

    def attend_rest(state):
        joined, grad_attended, *before = state
        return attention(
            tables, joined, qkv_bias, grad_attended, pairs // 2, pairs - pairs // 2, before
        )

    def sum_narrow(state):
        attended, grad_joined, qkv_bias_sum = state
        sums = [
            ring.pair_sum(normed_parts, grad_joined),
            ring.pair_sum(cotangent_parts, attended),
        ]
        return attended, grad_joined, qkv_bias_sum, sums

    def start_normed(state):
        attended, activation, grad_joined, grad_hidden = state
        return attended, activation, dot_nt(grad_joined, full_qkv), grad_hidden

    def sum_normed(state):
        attended, activation, partial, grad_hidden = state
        partial = (partial + dot_nt(grad_hidden, full_fc1)).astype(BF)
        return attended, activation, across(partial)

    def sum_branch(state):
        attended, activation, normed = state
        partial = (dot_nt(attended, full_dense) + dot_nt(activation, full_fc2)).astype(BF)
        return across(partial), normed

    def across(partial):
        mine = lax.dynamic_slice_in_dim(partial, tensor_index * half_rows, half_rows, 0)
        theirs = lax.dynamic_slice_in_dim(partial, (1 - tensor_index) * half_rows, half_rows, 0)
        return mine, theirs

    def run(chain, works, state):
        for step in range(ring.count // 2):
            work = works[step] if step < len(works) else lambda state: state
            state = ring.sweep(chain, work, state, step == ring.count // 2 - 1)
        return state

    wide = Chain(ring, wide_sums)
    works = (project, attend_some, attend_rest, sum_narrow)
    state = run(wide, works, (full_qkv, full_dense))
    attended, grad_joined, qkv_bias_sum, narrow_sums = state
    narrow = Chain(ring, narrow_sums)
    state = (attended, activation, grad_joined, grad_hidden)
    branch, normed = run(
        narrow, (lambda state: state, start_normed, sum_normed, sum_branch), state
    )
    branch_mine, branch_theirs = branch
    normed_mine, normed_theirs = normed[0], other(normed[1], "tensor", 1)
    moms = (mom_qkv, mom_dense, mom_fc1, mom_fc2)
    group = n // 4
    slot = unit_width // group
    *new_moms, blocks = momentum(momentum_decay, narrow.parts(), wide.parts(), moms, group)
    columns = lax.all_to_all(blocks, "dp", 0, 0, tiled=True)
    columns = columns.reshape(D, slot)
    grad_normed = normed_mine.astype(F32) + normed_theirs.astype(F32)
    unit_normed, inv_std = normalized(tokens)
    scaled_grad = grad_normed * ln_gain
    grad_tokens = cotangent.astype(F32) + inv_std * (
        scaled_grad
        - jnp.mean(scaled_grad, axis=1, keepdims=True)
        - unit_normed * jnp.mean(scaled_grad * unit_normed, axis=1, keepdims=True)
    )

    row_cotangent = jnp.sum(cotangent.astype(F32), axis=0)
    qkv_bias_grad = lax.dynamic_update_slice_in_dim(
        jnp.zeros((3 * D,), F32),
        qkv_bias_sum.reshape(-1),
        tensor_index * joined_width,
        0,
    )
    fc1_bias_grad = lax.dynamic_update_slice_in_dim(
        jnp.zeros((FF,), F32),
        jnp.sum(grad_hidden.astype(F32), axis=0),
        tensor_index * unit_width,
        0,
    )
    vector_grad = jnp.concatenate(
        [
            jnp.sum(grad_normed * unit_normed, axis=0),
            jnp.sum(grad_normed, axis=0),
            qkv_bias_grad,
            row_cotangent,
            fc1_bias_grad,
            row_cotangent,
        ]
    )
    bits = []
    bit = 2
    while bit < group:
        bits.append(bit)
        bit *= 2
    columns, vector_grad = lax.optimization_barrier((columns, vector_grad))
    vector_parts = lax.all_to_all(
        vector_grad.reshape(2 * n, share // 2), ("dp", "tensor"), 0, 0, tiled=True
    )
    mine, theirs, vector_parts = sum_over_group(ring.core, columns, bits, vector_parts)
    branch_theirs, mine = lax.optimization_barrier((branch_theirs, mine))
    ortho = chain(ring.core, mine, theirs, columns)
    ortho, branch_theirs = lax.optimization_barrier((ortho, other(branch_theirs, "tensor", 1)))
    branch = branch_mine.astype(F32) + branch_theirs.astype(F32)
    output = (tokens.astype(F32) + branch + dense_bias + fc2_bias).astype(BF)
    pieces = lax.all_to_all(ortho.reshape(n, shard_rows, slot), "dp", 0, 0, tiled=True)
    vector_share = jnp.sum(vector_parts, axis=0)

    masters = (qkv_weight, dense_weight, fc1_weight, fc2_weight)
    rates = [muon_rate * 0.2 * math.sqrt(max(D, 2 * m.shape[1])) for m in masters]
    new_weights = update(pieces, masters, 1.0 - muon_rate * weight_decay, rates, group)

    vector_slot = lax.dynamic_slice_in_dim(vectors, tensor_index * (share // 2), share // 2)
    new_first = beta_first * first_moment + (1.0 - beta_first) * vector_share
    new_second = beta_second * second_moment + (1.0 - beta_second) * vector_share * vector_share
    new_vectors = vector_slot - vector_rate * (new_first / (1.0 - beta_first**STEP)) / (
        jnp.sqrt(new_second / (1.0 - beta_second**STEP)) + 1e-08
    )
    return (
        output,
        grad_tokens,
        new_moms[0],
        new_weights[0],
        new_moms[1],
        new_weights[1],
        new_moms[2],
        new_weights[2],
        new_moms[3],
        new_weights[3],
        new_first,
        new_second,
        new_vectors,
    )


def solution(mesh):
    rows = P(("dp", "tensor"), None)
    weight = P("dp", "tensor")
    vector = P(("dp", "tensor"))
    return jax.shard_map(
        per_device,
        mesh=mesh,
        in_specs=(rows, rows, P("dp")) + (weight,) * 4 + (P("dp"),) + (weight,) * 4 + (vector,) * 2,
        out_specs=(rows, rows) + (weight,) * 8 + (vector,) * 3,
        check_vma=False,
    )
```

```python
import math

import jax
import jax.numpy as jnp
from jax import lax
from jax.experimental import pallas as pl
from jax.experimental.pallas import tpu as pltpu
from jax.sharding import PartitionSpec as P

D = 1024
HEADS = 16
FF = 4096
STEP = 10
momentum_decay = 0.95
muon_rate = 0.15
weight_decay = 0.1
vector_rate = 0.4
beta_first = 0.9
beta_second = 0.95
HD=64; ROT=32
F32=jnp.float32; BF=jnp.bfloat16
coef_linear = 3.4445
coef_square = -4.775
coef_cubic = 2.0315

def dot_nt(x, y):
    return lax.dot_general(x, y, (((1,), (1,)), ((), ())), preferred_element_type=F32)

def dot_tn(x, y):
    return lax.dot_general(x, y, (((0,), (0,)), ((), ())), preferred_element_type=F32)

def dot_nn(x, y):
    return jnp.dot(x, y, preferred_element_type=F32)

def tables_kernel(position_ref, frequency_ref, keep_ref, upper_ref, lower_ref):
    half = ROT // 2
    lane = lax.broadcasted_iota(jnp.int32, (1, 2 * HD), 1) % HD
    angles = position_ref[...].astype(F32) * frequency_ref[...]
    cosine, sine = jnp.cos(angles), jnp.sin(angles)
    keep_ref[...] = jnp.where(lane < ROT, cosine, 1.0)
    upper_ref[...] = jnp.where(lane < half, -sine, 0.0)
    lower_ref[...] = jnp.where((lane >= half) & (lane < ROT), sine, 0.0)

def rope_tables(positions):
    half = ROT // 2
    frequency = 10000.0 ** (-2.0 * jnp.arange(half, dtype=F32) / ROT)
    table = jax.ShapeDtypeStruct((positions.shape[0], 2 * HD), F32)
    return pl.pallas_call(
        tables_kernel,
        out_shape=[table] * 3,
        cost_estimate=pl.CostEstimate(flops=10**9, bytes_accessed=2 * 10**7, transcendentals=0),
        name="rope_tables",
    )(positions[:, None], jnp.tile(frequency, 2 * HD // half)[None])

ROWS = 256

def attention_kernel(lo_ref, x_ref, b_ref, g_ref, keep_ref, upper_ref, lower_ref, *refs):
    (att_ref, out_ref, sum_ref, bias_ref, s_ref, e_ref, top_ref, o_ref, ge_ref, q_ref, k_ref, v_ref,
     dk_ref, dv_ref, dq_ref) = refs[-15:]
    seq = x_ref.shape[0]
    width = 2 * HD
    lane = lax.broadcasted_iota(jnp.int32, (1, width), 1)
    first = lane < HD
    mine = (first, ~first)
    half = ROT // 2
    blocks = seq // ROWS
    @pl.when(pl.program_id(0) == 0)
    def _():
        for i in range(blocks):
            r0, n = i * ROWS, (i + 1) * ROWS
            col = lax.broadcasted_iota(jnp.int32, (ROWS, n), 1)
            row = lax.broadcasted_iota(jnp.int32, (ROWS, n), 0) + r0
            allowed = (col >= lo_ref[r0:n, :]) & (col <= row)
            bias_ref[r0:n, :n] = jnp.where(allowed, 0.0, -1e30)
    def rotated(values, sign):
        up = pltpu.roll(values, width - half, 1) * upper_ref[...]
        down = pltpu.roll(values, half, 1) * lower_ref[...]
        return values * keep_ref[...] + (up + down) * sign
    scale = HD ** -0.5
    def swapped(row):
        return pltpu.roll(jnp.broadcast_to(row, (8, width)), HD, 1)[:1]
    b0, b1, b2 = (b_ref[0, :, c * width:(c + 1) * width] for c in range(3))
    q = rotated(x_ref[:, :width] + jnp.where(first, b0, b1), 1.0) * scale
    bias_k = jnp.where(first, swapped(b0), swapped(b2))
    k_ref[...] = rotated(x_ref[:, width:2 * width] + bias_k, 1.0).astype(BF)
    v_ref[:, :width] = (x_ref[:, 2 * width:] + jnp.where(first, b1, b2)).astype(BF)
    v_ref[:, width:] = jnp.broadcast_to(jnp.where(lane < 2, 1.0, 0.0), (seq, width)).astype(BF)
    for i in range(blocks):
        for h in range(2):
            q_ref[i, h * ROWS:(h + 1) * ROWS, :] = jnp.where(
                mine[h], q[i * ROWS:(i + 1) * ROWS], 0.0
            ).astype(BF)
    for i in range(blocks):
        n = (i + 1) * ROWS
        both = dot_nt(q_ref[i], k_ref[:n, :])
        bias = bias_ref[i * ROWS:n, :n]
        for h in range(2):
            r = slice(h * ROWS, (h + 1) * ROWS)
            s = both[r] + bias
            s_ref[i, r, :n] = s
            m = s[:, :width]
            for c in range(width, n, width):
                m = jnp.maximum(m, s[:, c:c + width])
            top_ref[i, r, :] = m
    for i in range(blocks):
        top = jnp.max(top_ref[i], axis=1, keepdims=True)
        top_ref[i] = jnp.broadcast_to(top, (2 * ROWS, width))
    for i in range(blocks):
        n = (i + 1) * ROWS
        e = jnp.exp(s_ref[i, :, :n] - top_ref[i, :, :1]).astype(BF)
        e_ref[i, :, :n] = e
        o_ref[i] = dot_nn(e, v_ref[:n, :])
    for i in range(blocks):
        rows = slice(i * ROWS, (i + 1) * ROWS)
        g = g_ref[rows, :].astype(F32)
        atts = []
        for h in range(2):
            r = slice(h * ROWS, (h + 1) * ROWS)
            inv = 1.0 / o_ref[i, r, width:width + 1]
            att = jnp.where(mine[h], o_ref[i, r, :width] * inv, 0.0)
            atts.append(att)
            gs = jnp.where(mine[h], g * inv, 0.0).astype(BF)
            delta = jnp.sum(gs.astype(F32) * att, axis=1, keepdims=True)
            dh = delta.astype(BF).astype(F32)
            ge_ref[i, r, :width] = gs
            ge_ref[i, r, width:] = jnp.where(lane == 0, -dh, jnp.where(lane == 1, dh - delta, 0.0)).astype(BF)
        att_ref[rows, :] = jnp.where(first, atts[0], atts[1]).astype(BF)
    dk_ref[...] = jnp.zeros_like(dk_ref)
    dv_ref[...] = jnp.zeros_like(dv_ref)
    for i in range(blocks):
        n = (i + 1) * ROWS
        e = e_ref[i, :, :n]
        ds = (e.astype(F32) * dot_nt(ge_ref[i], v_ref[:n, :])).astype(BF)
        dq = dot_nn(ds, k_ref[:n, :]) * scale
        dq_ref[i * ROWS:n, :] = jnp.where(first, dq[:ROWS], dq[ROWS:])
        dk_ref[:, :n] += dot_nn(q_ref[i].T, ds)
        dv_ref[:, :n] += dot_nn(ge_ref[i, :, :width].T, e)
    sums = []
    values = (rotated(dq_ref[...], -1.0), rotated(dk_ref[...].T, -1.0), dv_ref[...].T)
    for c, value in enumerate(values):
        low = value.astype(BF)
        out_ref[:, c * width:(c + 1) * width] = low
        sums.append(jnp.sum(low.astype(F32), axis=0, keepdims=True))
    sq, sk, sv = sums
    sum_ref[0, :, :width] = jnp.where(first, sq, swapped(sk))
    sum_ref[0, :, width:2 * width] = jnp.where(first, sv, sq)
    sum_ref[0, :, 2 * width:] = jnp.where(first, swapped(sk), sv)

def attention_tables(positions):
    lo = (jnp.arange(positions.shape[0], dtype=jnp.int32) - positions)[:, None]
    return (lo, *rope_tables(positions))

def attention(tables, joined, bias, grad_att, start, count, before=()):
    lo, keep, upper, lower = tables
    seq, width = joined.shape
    pairs = width // (6 * HD)
    whole = lambda w: pl.BlockSpec((seq, w), lambda h: (0, 0))
    part = lambda w: pl.BlockSpec((seq, w), lambda h: (0, h + start))
    line = pl.BlockSpec((1, 1, 6 * HD), lambda h: (h + start, 0, 0))
    double = lambda w, dtype: pltpu.VMEM((seq // ROWS, 2 * ROWS, w), dtype)
    tables = [whole(2 * HD)] * 3
    return pl.pallas_call(
        attention_kernel,
        grid=(count,),
        in_specs=[whole(1), part(6 * HD), line, part(2 * HD)] + tables
        + [pl.BlockSpec(memory_space=pl.ANY)] * len(before),
        out_specs=[part(2 * HD), part(6 * HD), line],
        out_shape=[
            jax.ShapeDtypeStruct((seq, pairs * 2 * HD), BF),
            jax.ShapeDtypeStruct((seq, width), BF),
            jax.ShapeDtypeStruct((pairs, 1, 6 * HD), F32),
        ],
        input_output_aliases={7 + i: i for i in range(len(before))},
        scratch_shapes=[
            pltpu.VMEM((seq, seq), F32),
            double(seq, F32),
            double(seq, BF),
            double(2 * HD, F32),
            double(4 * HD, F32),
            double(4 * HD, BF),
            double(2 * HD, BF),
            pltpu.VMEM((seq, 2 * HD), BF),
            pltpu.VMEM((seq, 4 * HD), BF),
            pltpu.VMEM((2 * HD, seq), F32),
            pltpu.VMEM((2 * HD, seq), F32),
            pltpu.VMEM((seq, 2 * HD), F32),
        ],
        compiler_params=pltpu.CompilerParams(vmem_limit_bytes=37 * 2**20),
        cost_estimate=pl.CostEstimate(flops=10**10, bytes_accessed=4 * 10**7, transcendentals=0),
        name="attention_both",
    )(lo, joined, bias.reshape(pairs, 1, 6 * HD), grad_att, keep, upper, lower, *before)

BAND = 128

def extra_bands(start, bands):
    return [i for i in range(start, start + bands // 2) if i % 2 == (2 * i >= bands)]

def gram_kernel(core_ref, x_ref, keep_ref, give_ref, twice_ref):
    size, width = x_ref.shape
    bands = size // BAND
    span = size // 2
    twice_ref[:size, :] = x_ref[...]
    twice_ref[size:, :] = x_ref[:span, :]
    def half(out_ref, start):
        for i in range(start, start + bands // 2):
            r = (i - start) * BAND
            band = twice_ref[i * BAND:(i + 1) * BAND, :]
            out_ref[r:r + BAND, :] = dot_nt(band, twice_ref[i * BAND:i * BAND + span, :])
        for e, i in enumerate(extra_bands(start, bands)):
            block = dot_nt(twice_ref[i * BAND:(i + 1) * BAND, :], twice_ref[i * BAND + span:(i + 1) * BAND + span, :])
            cut = BAND // (bands // 2)
            for c in range(bands // 2):
                r = span + e * cut
                out_ref[r:r + cut, c * BAND:(c + 1) * BAND] = block[c * cut:(c + 1) * cut, :]
    @pl.when(core_ref[0] == 0)
    def _():
        half(give_ref, bands // 2)
        half(keep_ref, 0)
    @pl.when(core_ref[0] == 1)
    def _():
        half(give_ref, 0)
        half(keep_ref, bands // 2)

def gram(core, x):
    size, width = x.shape
    span = size // 2
    half = jax.ShapeDtypeStruct((span + BAND // 2, span), F32)
    spec = pl.BlockSpec(memory_space=pltpu.VMEM)
    return pl.pallas_call(
        gram_kernel,
        out_shape=[half, half],
        in_specs=[pl.BlockSpec(memory_space=pltpu.SMEM), spec],
        out_specs=[spec, spec],
        scratch_shapes=[pltpu.VMEM((size + span, width), BF)],
        compiler_params=pltpu.CompilerParams(vmem_limit_bytes=12 * 2**20),
        name="gram",
    )(core.reshape(1), x)

def chain_kernel(core_ref, mine_ref, theirs_ref, x0_ref, out_ref, a_ref, ah_ref, m_ref, u_ref, uh_ref, xa_ref):
    size = x0_ref.shape[0]
    bands = size // BAND
    row = lax.broadcasted_iota(jnp.int32, (size // 2, BAND), 0)
    col = lax.broadcasted_iota(jnp.int32, (size // 2, BAND), 1)
    diagonal = mine_ref[:size // 2, :BAND] + theirs_ref[:size // 2, :BAND]
    trace = jnp.sum(jnp.where(row % BAND == col, diagonal, 0.0))
    norm = jnp.sqrt(trace) + 1e-07
    scale = 1.0 / (norm * norm)
    def store(rs, cs, block):
        a_ref[rs, cs] = block
        ah_ref[rs, cs] = block.astype(BF)
    def place(i, j, block):
        store(slice(i * BAND, (i + 1) * BAND), slice(j * BAND, (j + 1) * BAND), block)
        if i != j:
            store(slice(j * BAND, (j + 1) * BAND), slice(i * BAND, (i + 1) * BAND), block.T)
    def unpack(half_ref, start):
        for i in range(start, start + bands // 2):
            r = (i - start) * BAND
            for o in range(bands // 2):
                block = half_ref[r:r + BAND, o * BAND:(o + 1) * BAND] * scale
                place(i, (i + o) % bands, block)
        cut = BAND // (bands // 2)
        for e, i in enumerate(extra_bands(start, bands)):
            rows = slice(size // 2 + e * cut, size // 2 + (e + 1) * cut)
            parts = [half_ref[rows, c * BAND:(c + 1) * BAND] for c in range(bands // 2)]
            place(i, (i + bands // 2) % bands, jnp.concatenate(parts, axis=0) * scale)
    @pl.when(core_ref[0] == 0)
    def _():
        unpack(mine_ref, 0)
        unpack(theirs_ref, bands // 2)
    @pl.when(core_ref[0] == 1)
    def _():
        unpack(theirs_ref, 0)
        unpack(mine_ref, bands // 2)
    xa_ref[...] = x0_ref[...]
    lin = coef_linear
    def turn(k, last):
        inv = jnp.where(k == 0, 1.0 / norm, 1.0)
        for r0 in range(0, size, ROWS):
            r, c = slice(r0, r0 + ROWS), slice(r0, size)
            s = dot_nn(ah_ref[r, :], ah_ref[:, c])
            m = (coef_square * ah_ref[r, c].astype(F32) + coef_cubic * s).astype(BF)
            m_ref[r, c] = m
            if r0 + ROWS < size:
                m_ref[r0 + ROWS:, r] = m[:, ROWS:].T
        for r0 in range(0, size, 2 * ROWS):
            r = slice(r0, r0 + (2 * ROWS))
            out_ref[r, :] = ((lin * xa_ref[r, :].astype(F32) + dot_nn(m_ref[r, :], xa_ref[...])) * inv).astype(BF)
        if last:
            return
        xa_ref[...] = out_ref[...]
        for r0 in range(0, size, 2 * ROWS):
            r = slice(r0, r0 + 2 * ROWS)
            u = lin * a_ref[r, :] + dot_nn(m_ref[r, :], ah_ref[...])
            u_ref[r, :] = u
            uh_ref[r, :] = u.astype(BF)
        for r0 in range(0, size, ROWS):
            r, c = slice(r0, r0 + ROWS), slice(r0, size)
            block = lin * u_ref[r, c] + dot_nn(uh_ref[r, :], m_ref[:, c])
            store(r, c, block)
            if r0 + ROWS < size:
                store(slice(r0 + ROWS, size), r, block[:, ROWS:].T)
    def body(k, _):
        turn(k, False)
        return 0
    lax.fori_loop(0, 4, body, 0)
    turn(4, True)
def chain(core, mine, theirs, x0):
    size, width = x0.shape
    V = lambda dt: pltpu.VMEM((size, size), dt)
    spec = pl.BlockSpec(memory_space=pltpu.VMEM)
    return pl.pallas_call(
        chain_kernel,
        out_shape=jax.ShapeDtypeStruct((size, width), BF),
        in_specs=[pl.BlockSpec(memory_space=pltpu.SMEM)] + [spec] * 3, out_specs=spec,
        scratch_shapes=[V(F32), V(BF), V(BF), V(F32), V(BF), pltpu.VMEM((size, width), BF)],
        compiler_params=pltpu.CompilerParams(vmem_limit_bytes=34 * 2**20),
        name="orthogonalize",
    )(core.reshape(1), mine, theirs, x0)

def assemble(core, position, count, rows, mine, theirs, widths):
    pieces = mine + theirs
    n = len(pieces)
    def kernel(core_ref, position_ref, *refs):
        values, outs = refs[:n], refs[n:]
        for k, (step, offset, piece) in enumerate(pieces):
            which = core_ref[0] if k < len(mine) else 1 - core_ref[0]
            place = position_ref[0] + step
            place = jnp.where(place < count, place, place - count)
            chip = jnp.where(place < count // 2, 2 * place, 2 * (count - 1 - place) + 1)
            size = piece.shape[0]
            tile = math.gcd(rows, size)
            span = pl.ds(pl.multiple_of((chip * 2 + which) * rows + offset, tile), size)
            start = 0
            for out, w in zip(outs, widths):
                out[span, :] = values[k][:, start:start + w]
                start += w
    vmem, smem = pl.BlockSpec(memory_space=pltpu.VMEM), pl.BlockSpec(memory_space=pltpu.SMEM)
    return pl.pallas_call(
        kernel,
        out_shape=[jax.ShapeDtypeStruct((2 * count * rows, w), BF) for w in widths],
        in_specs=[smem, smem] + [vmem] * n,
        out_specs=[vmem] * len(widths),
        compiler_params=pltpu.CompilerParams(vmem_limit_bytes=48 * 2**20),
        name="assemble",
    )(core.reshape(1), position.reshape(1), *(piece[2] for piece in pieces))

def whole_call(kernel, name, out_shape, *args, scalars=0, scratch=(), limit=12):
    vmem, smem = pl.BlockSpec(memory_space=pltpu.VMEM), pl.BlockSpec(memory_space=pltpu.SMEM)
    args = [a.reshape(1) if i < scalars else a for i, a in enumerate(args)]
    return pl.pallas_call(
        kernel,
        out_shape=out_shape,
        in_specs=[smem] * scalars + [vmem] * (len(args) - scalars),
        out_specs=[vmem] * len(out_shape),
        scratch_shapes=list(scratch),
        compiler_params=pltpu.CompilerParams(vmem_limit_bytes=limit * 2**20),
        name=name,
    )(*args)

def momentum(decay, narrow, wide, moms, group):
    rows = moms[0].shape[0]
    widths = [m.shape[1] for m in moms]
    slot = max(widths) // group
    def kernel(*refs):
        narrow_refs, wide_refs, mom_refs, new_refs, out_ref = refs[:3], refs[3:6], refs[6:10], refs[10:14], refs[14]
        def total(parts, c, w):
            return sum(p[:, c:c + w].astype(F32) for p in parts)
        first = lax.broadcasted_iota(jnp.int32, (1, 2 * HD), 1) < HD
        for c in range(0, widths[0], 6 * HD):
            q, k, v = (total(narrow_refs, c + i * 2 * HD, 2 * HD) for i in range(3))
            k = pltpu.roll(k, HD, 1)
            parts = (jnp.where(first, q, k), jnp.where(first, v, q), jnp.where(first, k, v))
            for i, part in enumerate(parts):
                s = slice(c + i * 2 * HD, c + (i + 1) * 2 * HD)
                new_refs[0][:, s] = decay * mom_refs[0][:, s] + part
        new_refs[1][...] = decay * mom_refs[1][...] + total(narrow_refs, widths[0], widths[1])
        new_refs[2][...] = decay * mom_refs[2][...] + total(wide_refs, 0, widths[2])
        new_refs[3][...] = decay * mom_refs[3][...] + total(wide_refs, widths[2], widths[3])
        for m, new in enumerate(new_refs):
            w = widths[m] // group
            for j in range(group):
                block = new[:, j * w:(j + 1) * w].astype(BF)
                if w < slot:
                    block = jnp.concatenate([block, jnp.zeros((rows, slot - w), BF)], axis=1)
                out_ref[m * group + j] = block
    shapes = [jax.ShapeDtypeStruct(m.shape, F32) for m in moms]
    shapes.append(jax.ShapeDtypeStruct((4 * group, rows, slot), BF))
    return whole_call(kernel, "momentum", shapes, *narrow, *wide, *moms)

def update(pieces, masters, keep, rates, group):
    def kernel(piece_ref, *refs):
        for m in range(4):
            master, new = refs[m], refs[4 + m]
            w = master.shape[1] // group
            for j in range(group):
                s = slice(j * w, (j + 1) * w)
                new[:, s] = master[:, s] * keep - rates[m] * piece_ref[m * group + j, :, :w].astype(F32)
    shapes = [jax.ShapeDtypeStruct(m.shape, F32) for m in masters]
    return whole_call(kernel, "update", shapes, pieces, *masters)

def gelu_and_slope(v):
    root = math.sqrt(2.0 / math.pi)
    square = v * v
    half = 0.5 * jnp.tanh(v * (root + (root * 0.044715) * square)) + 0.5
    value = v * half
    return value, half + value * (1.0 - half) * (2.0 * root + (6.0 * root * 0.044715) * square)

def pack(fc1, fc2, dense, vectors, qkv):
    rows = fc1.shape[0]
    widths = [x.shape[1] for x in (fc1, fc2, dense)]
    lanes = 2 * HD
    def kernel(fc1_ref, fc2_ref, dense_ref, vectors_ref, qkv_ref, ring_ref, pair_ref):
        start = 0
        for x in (fc1_ref, fc2_ref, dense_ref):
            ring_ref[:, start:start + x.shape[1]] = x[...].astype(BF)
            start += x.shape[1]
        spare = jnp.zeros((rows - vectors_ref.shape[0], lanes), F32)
        ring_ref[:, start:] = jnp.concatenate([vectors_ref[...], spare], axis=0).astype(BF)
        first = lax.broadcasted_iota(jnp.int32, (1, lanes), 1) < HD
        for c in range(0, qkv_ref.shape[1], 3 * lanes):
            a, b, d = (qkv_ref[:, c + i * lanes:c + (i + 1) * lanes] for i in range(3))
            k = jnp.where(first, pltpu.roll(a, HD, 1), pltpu.roll(d, HD, 1))
            for i, part in enumerate((jnp.where(first, a, b), k, jnp.where(first, b, d))):
                pair_ref[:, c + i * lanes:c + (i + 1) * lanes] = part.astype(BF)
    lines = -(-vectors.shape[0] // (8 * lanes)) * 8
    vectors = jnp.pad(vectors, (0, lines * lanes - vectors.shape[0])).reshape(lines, lanes)
    shapes = [(rows, sum(widths) + lanes), qkv.shape]
    args = (fc1, fc2, dense, vectors, qkv)
    block = lambda shape: pl.BlockSpec(shape, lambda i: (0, 0))
    return pl.pallas_call(
        kernel,
        grid=(1,),
        out_shape=[jax.ShapeDtypeStruct(s, BF) for s in shapes],
        in_specs=[block(a.shape) for a in args],
        out_specs=[block(s) for s in shapes],
        compiler_params=pltpu.CompilerParams(vmem_limit_bytes=56 * 2**20),
        name="pack",
    )(*args)


def other(x, axis, bit):
    n = lax.axis_size(axis)
    return lax.ppermute(x, axis, [(i, i ^ bit) for i in range(n)])


def in_order(mine, theirs, index, axis=0):
    low = jnp.where(index == 0, mine, theirs)
    high = jnp.where(index == 0, theirs, mine)
    return jnp.concatenate([low, high], axis=axis)


class Ring:
    def __init__(self):
        n = lax.axis_size("dp")
        self.count = n // 2
        rows = self.count // 2
        order = [2 * i for i in range(rows)] + [2 * i + 1 for i in reversed(range(rows))]
        index = lax.axis_index("dp")
        self.core = index % 2
        chip = index // 2
        self.position = jnp.where(chip % 2 == 0, chip // 2, self.count - 1 - chip // 2)
        self.up_pairs = [
            (2 * order[i] + c, 2 * order[(i + 1) % self.count] + c)
            for i in range(self.count)
            for c in range(2)
        ]
        self.down_pairs = [(b, a) for a, b in self.up_pairs]

    def chip(self, step):
        place = (self.position + step % self.count) % self.count
        return jnp.where(place < self.count // 2, 2 * place, 2 * (self.count - 1 - place) + 1)

    def up(self, x):
        return lax.ppermute(x, "dp", self.up_pairs)

    def down(self, x):
        return lax.ppermute(x, "dp", self.down_pairs)

    def gather(self, shard, rides, positions):
        rows = shard.shape[0]
        half, cut = self.count // 2, rows // 32 * 16 or rows // 2
        mine = {0: shard}
        rising = falling = shard
        ride = other(rides[0], "tensor", 1)
        for step in range(half):
            if step == half - 1:
                rising, falling = rising[:cut], falling[cut:]
            rising, falling = self.up(rising), self.down(falling)
            if step == 0:
                rising, positions = lax.optimization_barrier((rising, positions))
                tables = attention_tables(positions)
            elif step <= len(rides):
                if step == 1:
                    rising, falling, tables = lax.optimization_barrier((rising, falling, tables))
                else:
                    ride = other(rides[step - 1], "tensor", 1)
                rising, falling, rides[step - 1] = lax.optimization_barrier((rising, falling, ride))
            if step < half - 1:
                mine[self.count - 1 - step], mine[1 + step] = rising, falling
        mine[half] = jnp.concatenate([rising, falling], axis=0)
        mine = [(k, 0, mine[k]) for k in range(self.count)]
        return mine, [(k, row, other(block, "dp", 1)) for k, row, block in mine], tables

    def split(self, values, rows):
        parts = values.reshape(values.shape[0], self.count, 2, rows)
        return tuple(
            lax.dynamic_index_in_dim(parts, c, 2, False).reshape(values.shape[0], -1)
            for c in (self.core, 1 - self.core)
        )

    def pair_sum(self, lefts, right):
        keep, give = lefts
        theirs = other(dot_tn(give, right).astype(BF), "dp", 1)
        return (dot_tn(keep, right) + theirs.astype(F32)).astype(BF)

    def sweep(self, chain, work, state, last=False):
        (rising, falling), state = lax.optimization_barrier((chain.outgoing(), state))
        chain.received = self.up(rising), self.down(falling)
        state = work(state)
        if not last:
            chain.received, state = lax.optimization_barrier((chain.received, state))
        return state


class Chain:
    def __init__(self, ring, sums):
        self.ring, self.sums, self.received = ring, sums, None
        self.rows = sums[0].shape[0] // ring.count
        self.cut = self.rows // 32 * 16 or self.rows // 2
        self.left = ring.count // 2

    def block(self, step):
        start = self.ring.chip(step) * self.rows
        parts = [lax.dynamic_slice_in_dim(s, start, self.rows, 0) for s in self.sums]
        return jnp.concatenate(parts, axis=1)

    def outgoing(self):
        step, cut = self.left, self.cut
        self.left -= 1
        if self.received is None:
            far = self.block(step)
            return far[:cut], far[cut:]
        low, high = self.block(step).astype(F32), self.block(-step).astype(F32)
        rising, falling = (r.astype(F32) for r in self.received)
        if rising.shape[0] < self.rows:
            low = jnp.concatenate([low[:cut] + rising, low[cut:]], axis=0)
            high = jnp.concatenate([high[:cut], high[cut:] + falling], axis=0)
        else:
            low, high = low + rising, high + falling
        return low.astype(BF), high.astype(BF)

    def parts(self):
        return (self.block(0), *self.received)


def sum_over_group(core, columns, bits, tie):
    keep, give = gram(core, columns)
    rows = keep.shape[0]
    keep = keep + other(give, "dp", 1)
    pieces = [keep[: rows // 2], keep[rows // 2 :]]
    steps = [("dp", b) for b in bits] + [("tensor", 1)]
    for turn in range(len(steps)):
        if turn == len(steps) - 1:
            pieces, tie = lax.optimization_barrier((pieces, tie))
        axis, bit = steps[turn]
        first = other(pieces[0], axis, bit)
        axis, bit = steps[len(steps) - 1 - turn]
        second = other(pieces[1], axis, bit)
        pieces = [pieces[0] + first, pieces[1] + second]
    half = jnp.concatenate(pieces, axis=0)
    return half, other(half, "dp", 1), tie


def per_device(
    tokens,
    cotangent,
    positions,
    qkv_weight,
    dense_weight,
    fc1_weight,
    fc2_weight,
    vectors,
    mom_qkv,
    mom_dense,
    mom_fc1,
    mom_fc2,
    first_moment,
    second_moment,
):
    tensor_index = lax.axis_index("tensor")
    n = lax.axis_size("dp")
    ring = Ring()
    joined_width = 3 * D // 2
    unit_width = FF // 2
    shard_rows = qkv_weight.shape[0]
    half_rows = tokens.shape[0]
    seq = 2 * half_rows

    share = vectors.shape[0]
    first_pack, second_pack = pack(fc1_weight, fc2_weight, dense_weight, vectors, qkv_weight)
    lanes = 2 * HD
    quarter = half_rows // 2
    rides = [tokens, cotangent[:quarter], cotangent[quarter:]]
    mine, theirs, tables = ring.gather(first_pack, rides, positions)
    second_pack, rides[1] = lax.optimization_barrier((second_pack, rides[1]))
    tokens_theirs, cotangent_theirs = rides[0], jnp.concatenate(rides[1:], axis=0)
    full_qkv = lax.all_gather(second_pack, "dp", axis=0, tiled=True)
    widths = (unit_width, unit_width, D // 2, lanes)
    full_fc1, full_fc2, full_dense, lines_full = assemble(
        ring.core, ring.position, ring.count, shard_rows, mine, theirs, widths
    )
    lines_full = lines_full.reshape(n, shard_rows, lanes)[:, : -(-share // lanes)]
    vector_full = lines_full.reshape(n, -1)[:, :share].reshape(-1).astype(F32)

    ln_gain = vector_full[:D]
    ln_shift = vector_full[D : 2 * D]
    qkv_bias = lax.dynamic_slice_in_dim(
        vector_full, 2 * D + tensor_index * joined_width, joined_width
    )
    dense_bias = vector_full[5 * D : 6 * D]
    fc1_bias = lax.dynamic_slice_in_dim(vector_full, 6 * D + tensor_index * unit_width, unit_width)
    fc2_bias = vector_full[6 * D + FF :]

    tokens_all = in_order(tokens, tokens_theirs, tensor_index)
    cotangent_all = in_order(cotangent, cotangent_theirs, tensor_index)

    def normalized(rows):
        values = rows.astype(F32)
        centred = values - jnp.mean(values, axis=1, keepdims=True)
        inv_std = lax.rsqrt(jnp.mean(centred * centred, axis=1, keepdims=True) + 1e-05)
        return centred * inv_std, inv_std

    normed_all = (normalized(tokens_all)[0] * ln_gain + ln_shift).astype(BF)
    normed_parts = ring.split(normed_all, shard_rows)
    cotangent_parts = ring.split(cotangent_all, shard_rows)
    hidden = dot_nn(normed_all, full_fc1) + fc1_bias
    activation, slope = (v.astype(BF) for v in gelu_and_slope(hidden))
    grad_act = dot_nn(cotangent_all, full_fc2)
    grad_hidden = (grad_act * slope.astype(F32)).astype(BF)
    wide_sums = [
        ring.pair_sum(normed_parts, grad_hidden),
        ring.pair_sum(cotangent_parts, activation),
    ]

    def project(state):
        full_qkv, full_dense = state
        return dot_nn(normed_all, full_qkv), dot_nn(cotangent_all, full_dense).astype(BF)

    pairs = joined_width // (6 * HD)

    def attend_some(state):
        joined, grad_attended = state
        return joined, grad_attended, *attention(tables, joined, qkv_bias, grad_attended, 0, pairs // 2)

    def attend_rest(state):
        joined, grad_attended, *before = state
        return attention(
            tables, joined, qkv_bias, grad_attended, pairs // 2, pairs - pairs // 2, before
        )

    def sum_narrow(state):
        attended, grad_joined, qkv_bias_sum = state
        sums = [
            ring.pair_sum(normed_parts, grad_joined),
            ring.pair_sum(cotangent_parts, attended),
        ]
        return attended, grad_joined, qkv_bias_sum, sums

    def start_normed(state):
        attended, activation, grad_joined, grad_hidden = state
        return attended, activation, dot_nt(grad_joined, full_qkv), grad_hidden

    def sum_normed(state):
        attended, activation, partial, grad_hidden = state
        partial = (partial + dot_nt(grad_hidden, full_fc1)).astype(BF)
        return attended, activation, across(partial)

    def sum_branch(state):
        attended, activation, normed = state
        partial = (dot_nt(attended, full_dense) + dot_nt(activation, full_fc2)).astype(BF)
        return across(partial), normed

    def across(partial):
        mine = lax.dynamic_slice_in_dim(partial, tensor_index * half_rows, half_rows, 0)
        theirs = lax.dynamic_slice_in_dim(partial, (1 - tensor_index) * half_rows, half_rows, 0)
        return mine, theirs

    def run(chain, works, state):
        for step in range(ring.count // 2):
            work = works[step] if step < len(works) else lambda state: state
            state = ring.sweep(chain, work, state, step == ring.count // 2 - 1)
        return state

    wide = Chain(ring, wide_sums)
    works = (project, attend_some, attend_rest, sum_narrow)
    state = run(wide, works, (full_qkv, full_dense))
    attended, grad_joined, qkv_bias_sum, narrow_sums = state
    narrow = Chain(ring, narrow_sums)
    state = (attended, activation, grad_joined, grad_hidden)
    branch, normed = run(
        narrow, (start_normed, sum_normed, lambda state: state, sum_branch), state
    )
    branch_mine, branch_theirs = branch
    normed_mine, normed_theirs = normed[0], other(normed[1], "tensor", 1)
    moms = (mom_qkv, mom_dense, mom_fc1, mom_fc2)
    group = n // 4
    slot = unit_width // group
    *new_moms, blocks = momentum(momentum_decay, narrow.parts(), wide.parts(), moms, group)
    columns = lax.all_to_all(blocks, "dp", 0, 0, tiled=True)
    columns = columns.reshape(D, slot)
    grad_normed = normed_mine.astype(F32) + normed_theirs.astype(F32)
    unit_normed, inv_std = normalized(tokens)
    scaled_grad = grad_normed * ln_gain
    grad_tokens = cotangent.astype(F32) + inv_std * (
        scaled_grad
        - jnp.mean(scaled_grad, axis=1, keepdims=True)
        - unit_normed * jnp.mean(scaled_grad * unit_normed, axis=1, keepdims=True)
    )

    row_cotangent = jnp.sum(cotangent.astype(F32), axis=0)
    qkv_bias_grad = lax.dynamic_update_slice_in_dim(
        jnp.zeros((3 * D,), F32),
        qkv_bias_sum.reshape(-1),
        tensor_index * joined_width,
        0,
    )
    fc1_bias_grad = lax.dynamic_update_slice_in_dim(
        jnp.zeros((FF,), F32),
        jnp.sum(grad_hidden.astype(F32), axis=0),
        tensor_index * unit_width,
        0,
    )
    vector_grad = jnp.concatenate(
        [
            jnp.sum(grad_normed * unit_normed, axis=0),
            jnp.sum(grad_normed, axis=0),
            qkv_bias_grad,
            row_cotangent,
            fc1_bias_grad,
            row_cotangent,
        ]
    )
    bits = []
    bit = 2
    while bit < group:
        bits.append(bit)
        bit *= 2
    columns, vector_grad = lax.optimization_barrier((columns, vector_grad))
    vector_parts = lax.all_to_all(
        vector_grad.reshape(2 * n, share // 2), ("dp", "tensor"), 0, 0, tiled=True
    )
    mine, theirs, vector_parts = sum_over_group(ring.core, columns, bits, vector_parts)
    branch_theirs, mine = lax.optimization_barrier((branch_theirs, mine))
    ortho = chain(ring.core, mine, theirs, columns)
    ortho, branch_theirs = lax.optimization_barrier((ortho, other(branch_theirs, "tensor", 1)))
    branch = branch_mine.astype(F32) + branch_theirs.astype(F32)
    output = (tokens.astype(F32) + branch + dense_bias + fc2_bias).astype(BF)
    pieces = lax.all_to_all(ortho.reshape(n, shard_rows, slot), "dp", 0, 0, tiled=True)
    vector_share = jnp.sum(vector_parts, axis=0)

    masters = (qkv_weight, dense_weight, fc1_weight, fc2_weight)
    rates = [muon_rate * 0.2 * math.sqrt(max(D, 2 * m.shape[1])) for m in masters]
    new_weights = update(pieces, masters, 1.0 - muon_rate * weight_decay, rates, group)

    vector_slot = lax.dynamic_slice_in_dim(vectors, tensor_index * (share // 2), share // 2)
    new_first = beta_first * first_moment + (1.0 - beta_first) * vector_share
    new_second = beta_second * second_moment + (1.0 - beta_second) * vector_share * vector_share
    new_vectors = vector_slot - vector_rate * (new_first / (1.0 - beta_first**STEP)) / (
        jnp.sqrt(new_second / (1.0 - beta_second**STEP)) + 1e-08
    )
    return (
        output,
        grad_tokens,
        new_moms[0],
        new_weights[0],
        new_moms[1],
        new_weights[1],
        new_moms[2],
        new_weights[2],
        new_moms[3],
        new_weights[3],
        new_first,
        new_second,
        new_vectors,
    )


def solution(mesh):
    rows = P(("dp", "tensor"), None)
    weight = P("dp", "tensor")
    vector = P(("dp", "tensor"))
    return jax.shard_map(
        per_device,
        mesh=mesh,
        in_specs=(rows, rows, P("dp")) + (weight,) * 4 + (P("dp"),) + (weight,) * 4 + (vector,) * 2,
        out_specs=(rows, rows) + (weight,) * 8 + (vector,) * 3,
        check_vma=False,
    )
```
